32 devices in a mesh: fsdp: 8 (over z, x), seq: 4 (over y, core).
Axes of the slice: x: 2, y: 2, z: 4, core: 2. Of those that a mesh axis runs over, the one named last changes fastest.
Arguments:
- block_input: bfloat16 [16, 1024, 1024], P('fsdp', 'seq'), may hold values from -6 to 6
- out_cotangent: bfloat16 [16, 1024, 1024], P('fsdp', 'seq'), may hold values from -6 to 6
- positions: int32 [3, 16, 1024], P(None, 'fsdp', 'seq'), may hold values from 0 to 15, as said below
- w_qkv: bfloat16 [1024, 3072], P('fsdp'), may hold values from -0.3125 to 0.3125
- w_out: bfloat16 [1024, 1024], P('fsdp'), may hold values from -0.75 to 0.75
- w_up: bfloat16 [1024, 4096], P('fsdp'), may hold values from -0.1875 to 0.1875
- w_down: bfloat16 [4096, 1024], P('fsdp'), may hold values from -0.09375 to 0.09375
- norm_gains: float32 [2, 1024], replicated, may hold values from 0.25 to 1.75
- norm_shifts: float32 [2, 1024], replicated, may hold values from -4 to 4
- qkv_bias: float32 [3072], replicated, may hold values from -6 to 6
- proj_bias: float32 [2, 1024], replicated, may hold values from -6 to 6
- up_bias: float32 [4096], replicated, may hold values from -6 to 6
- clip_threshold: float32 [1], replicated, may hold values from 10 to 13
Outputs:
- block_out: bfloat16 [16, 1024, 1024], P('fsdp', 'seq')
- grad_input: float32 [16, 1024, 1024], P('fsdp', 'seq')
- grad_qkv: float32 [1024, 3072], P(('fsdp', 'seq'))
- grad_out: float32 [1024, 1024], P(('fsdp', 'seq'))
- grad_up: float32 [1024, 4096], P(('fsdp', 'seq'))
- grad_down: float32 [4096, 1024], P(('fsdp', 'seq'))
- grad_gains: float32 [2, 1024], P(None, ('fsdp', 'seq'))
- grad_shifts: float32 [2, 1024], P(None, ('fsdp', 'seq'))
- grad_qkv_bias: float32 [3072], P(('fsdp', 'seq'))
- grad_proj_bias: float32 [2, 1024], P(None, ('fsdp', 'seq'))
- grad_up_bias: float32 [4096], P(('fsdp', 'seq'))
- logit_max: float32 [16], replicated
- clipped_qk: float32 [1024, 2048], P('fsdp')
- clipped_qk_bias: float32 [2048], replicated
The draws below stay inside these ranges and needn't reach their ends.
Inputs may be any that keep to these rules, and one draw needn't show every extreme that they name: `positions`: in each clip the (frame, row, column) triples are distinct: they are the first 1024 patches of frames of 16 by 16 patches, counted frame by frame, in some order.
All inputs are finite; a program needn't handle non-finite values.
Results may differ from the reference program's by a relative error of at most 0.014.
The reference program's roundings to bfloat16 on the way count: a program that leaves them out, or rounds other values in their place, can miss the bound.
Values may be sent and summed in bfloat16 or wider, within the bound.
No kernel may reach another device: no remote copies, remote signals or barrier semaphores. Data moves between devices by JAX's collectives and lax.ppermute only.
A program may use at most 256 MiB of HBM per device.

```python
import jax
import jax.numpy as jnp
from jax import lax

D = 1024
HEADS = 16
FF = 4096
HEAD_DIM = 64
CLIP_LEN = 1024
CLIPS = 16


def draw_w_qkv(key, part):
    key = jax.random.fold_in(key, 11)
    first_key, second_key, third_key = jax.random.split(key, 3)
    base = jnp.clip(jax.random.normal(first_key, (D, 3 * D), jnp.float32), -4.0, 4.0)
    order = jax.random.permutation(second_key, HEADS).astype(jnp.float32)
    jitter = jax.random.uniform(third_key, (HEADS,), jnp.float32)
    factor = 0.8 * jnp.power(3.0, (order + jitter) / HEADS)
    column_scale = jnp.concatenate([jnp.repeat(factor, HEAD_DIM), jnp.full((D,), 1.4, jnp.float32), jnp.ones((D,), jnp.float32)])
    return (base * column_scale[None, :] / jnp.sqrt(jnp.float32(D))).astype(jnp.bfloat16)


def draw_positions(key, part):
    key = jax.random.fold_in(key, 23)
    clip_keys = jax.random.split(key, CLIPS)
    cells = jax.vmap(lambda clip_key: jax.random.permutation(clip_key, CLIP_LEN))(clip_keys)
    frame = cells // 256
    row_index = cells // 16 % 16
    column = cells % 16
    return jnp.stack([frame, row_index, column]).astype(jnp.int32)


def shard_levels(own_key, extent, cuts, smallest, largest):
    def one(dim, shards_of):
        heights = jax.random.uniform(jax.random.fold_in(jax.random.fold_in(own_key, 6), dim), (shards_of,), jnp.float32, smallest / len(cuts), largest / len(cuts))
        return jnp.repeat(jnp.exp(heights), extent[dim] // shards_of).reshape((-1,) + (1,) * (len(extent) - dim - 1))

    level = one(*cuts[0])
    for cut in cuts[1:]:
        level = level * one(*cut)
    return level


def noise(stream_key, shape, width, most, shards=(), kind=jnp.bfloat16):
    array = jax.random.normal(stream_key, shape, jnp.float32) * width
    if len(shards) > 0:
        array = shard_levels(stream_key, shape, shards, -0.22, 0.18) * array
    return jnp.clip(array, min=-most, max=most).astype(kind)


def setup_inputs(seed: int = 0) -> dict:
    key_list = jax.random.split(jax.random.key(seed), 14)
    return {
        "block_input": noise(key_list[0], (CLIPS, CLIP_LEN, D), 1.0, 6.0, ((0, 8), (1, 4))),
        "out_cotangent": noise(key_list[1], (CLIPS, CLIP_LEN, D), 1.0, 6.0, ((0, 8), (1, 4))),
        "positions": draw_positions(jax.random.fold_in(key_list[13], 71), 0),
        "w_qkv": draw_w_qkv(jax.random.fold_in(key_list[13], 71), 0),
        "w_out": noise(key_list[4], (D, D), (D // 16) ** -0.5, 0.75, ((0, 8),)),
        "w_up": noise(key_list[5], (D, FF), D ** -0.5, 0.1875, ((0, 8),)),
        "w_down": noise(key_list[6], (FF, D), FF ** -0.5, 0.09375, ((0, 8),)),
        "norm_gains": jnp.clip(1.0 + 0.15 * jax.random.normal(key_list[7], (2, D), jnp.float32), 0.25, 1.75),
        "norm_shifts": noise(key_list[8], (2, D), 0.3, 4.0, (), jnp.float32),
        "qkv_bias": noise(key_list[9], (3 * D,), 0.5, 6.0, (), jnp.float32),
        "proj_bias": noise(key_list[10], (2, D), 0.5, 6.0, (), jnp.float32),
        "up_bias": noise(key_list[11], (FF,), 0.5, 6.0, (), jnp.float32),
        "clip_threshold": jnp.clip(jax.random.uniform(key_list[12], (1,), jnp.float32, 10.0, 13.0), 10.0, 13.0),
    }


EPSILON = 1e-06
ROPE_BASE = 100.0

@jax.custom_vjp
def low(v):
    return lax.optimization_barrier(v.astype(jnp.bfloat16)).astype(jnp.float32)

@jax.custom_vjp
def low_back(v):
    return v

def low_keep(v):
    return (low(v), None)

def low_pass(kept, grad):
    return (grad,)

def back_keep(v):
    return (v, None)

def back_low(kept, grad):
    return (low(grad),)
low.defvjp(low_keep, low_pass)
low_back.defvjp(back_keep, back_low)

def layer_norm(values_in, gain_row, shift_row):
    row_mean = lax.optimization_barrier(jnp.mean(values_in, axis=-1, keepdims=True))
    centred = values_in - row_mean
    row_var = lax.optimization_barrier(jnp.mean(centred * centred, axis=-1, keepdims=True))
    return centred * lax.rsqrt(row_var + EPSILON) * gain_row + shift_row

def rotary_tables(coords, head_size):
    pair_count = head_size // 2
    band_count = (pair_count + 2) // 3
    pair_index = jnp.arange(pair_count)
    band_level = (pair_index // 3).astype(jnp.float32)
    frequency = jnp.power(ROPE_BASE, -band_level / band_count)
    coords_float = coords.astype(jnp.float32)
    axis_pick = (pair_index % 3)[:, None]
    chosen = jnp.where(axis_pick == 0, coords_float[0][None, :], jnp.where(axis_pick == 1, coords_float[1][None, :], coords_float[2][None, :]))
    angles = chosen.T * frequency[None, :]
    return (jnp.cos(angles)[:, None, :], jnp.sin(angles)[:, None, :])

def rotate(values_in, cosine_table, sine_table):
    half_width = values_in.shape[-1] // 2
    first_half = values_in[..., :half_width]
    second = values_in[..., half_width:]
    return jnp.concatenate([first_half * cosine_table - second * sine_table, first_half * sine_table + second * cosine_table], axis=-1)

def clip_forward(clip_rows, w_qkv, w_out, w_up, w_down, norm_gains, norm_shifts, qkv_bias, proj_bias, up_bias, cosine_table, sine_table):
    highest = lax.Precision.HIGHEST
    length = clip_rows.shape[0]
    normed = low(layer_norm(clip_rows, norm_gains[0], norm_shifts[0]))
    mixed = low_back(jnp.dot(normed, w_qkv, precision=highest) + qkv_bias)
    shaped = mixed.reshape(length, 3, HEADS, HEAD_DIM)
    query = low(rotate(shaped[:, 0], cosine_table, sine_table))
    keys = low(rotate(shaped[:, 1], cosine_table, sine_table))
    values = low(shaped[:, 2])
    scale = HEAD_DIM ** (-0.5)
    block_rows = min(512, length)

    def attend(query_block):
        scores = low_back(jnp.einsum('qhd,khd->hqk', query_block, keys, precision=highest) * scale)
        row_top = lax.optimization_barrier(jnp.max(scores, axis=2, keepdims=True))
        exponent = jnp.exp(scores - row_top)
        prob_full = exponent / lax.optimization_barrier(jnp.sum(exponent, axis=2, keepdims=True))
        attended_block = jnp.einsum('hqk,khd->qhd', low(prob_full), values, precision=highest)
        return (attended_block, lax.optimization_barrier(jnp.max(row_top[:, :, 0], axis=1)))
    attended, block_tops = lax.map(jax.checkpoint(attend), query.reshape(length // block_rows, block_rows, HEADS, HEAD_DIM))
    attended = low(low_back(attended.reshape(length, D)))
    resid1 = clip_rows + low_back(jnp.dot(attended, w_out, precision=highest) + proj_bias[0])
    normed2 = low(layer_norm(resid1, norm_gains[1], norm_shifts[1]))
    hidden = low_back(jnp.dot(normed2, w_up, precision=highest) + up_bias)
    activated = low(jax.nn.gelu(hidden, approximate=False))
    result = resid1 + low_back(jnp.dot(activated, w_down, precision=highest) + proj_bias[1])
    return (result, lax.optimization_barrier(jnp.max(block_tops, axis=0)))

def reference(block_input, out_cotangent, positions, w_qkv, w_out, w_up, w_down, norm_gains, norm_shifts, qkv_bias, proj_bias, up_bias, clip_threshold):
    params = tuple((item.astype(jnp.float32) for item in (w_qkv, w_out, w_up, w_down, norm_gains, norm_shifts, qkv_bias, proj_bias, up_bias)))

    def per_clip(totals, inputs):
        clip_rows, clip_grad, clip_coords = inputs
        cosine_table, sine_table = rotary_tables(clip_coords, HEAD_DIM)

        def forward(rows_in, *weights):
            return clip_forward(rows_in, *weights, cosine_table, sine_table)
        result, pull, tops = jax.vjp(forward, clip_rows.astype(jnp.float32), *params, has_aux=True)
        grads = pull(clip_grad.astype(jnp.float32))
        totals = tuple((total + grad for total, grad in zip(totals, grads[1:])))
        return (totals, (result.astype(jnp.bfloat16), grads[0], tops))
    zeros = tuple((jnp.zeros_like(item) for item in params))
    clip_coords = jnp.transpose(positions, (1, 0, 2))
    totals, (outputs, input_grads, tops) = lax.scan(per_clip, zeros, (block_input, out_cotangent, clip_coords))
    maxima = lax.optimization_barrier(jnp.max(tops, axis=0))
    threshold = clip_threshold[0]
    gamma = jnp.sqrt(threshold / jnp.maximum(maxima, threshold))
    columns = jnp.repeat(gamma, HEAD_DIM)
    weight_full = params[0]
    bias_full = params[6]
    clipped = jnp.concatenate([weight_full[:, :D] * columns, weight_full[:, D:2 * D] * columns], axis=1)
    clipped_bias = jnp.concatenate([bias_full[:D] * columns, bias_full[D:2 * D] * columns])
    return (outputs, input_grads, totals[0], totals[1], totals[2], totals[3], totals[4], totals[5], totals[6], totals[7], totals[8], maxima, clipped, clipped_bias)
```

```python
import functools

import jax
import jax.numpy as jnp
import numpy as np
from jax import lax
from jax.experimental import pallas as pl
from jax.experimental.pallas import tpu as pltpu
from jax.sharding import PartitionSpec as P

HEADS = 16
EPSILON = 1e-06
ROPE_BASE = 100.0
GRID_SIDE = 16

BF = jnp.bfloat16
F32 = jnp.float32
NN = (((1,), (0,)), ((), ()))
NT = (((1,), (1,)), ((), ()))
TN = (((0,), (0,)), ((), ()))


def dot(left, right, dims):
    return lax.dot_general(left, right, dims, preferred_element_type=F32)


def params(megabytes=48):
    return pltpu.CompilerParams(vmem_limit_bytes=megabytes << 20)


def flip(value, axis, mask):
    size = lax.axis_size(axis)
    return lax.ppermute(value, axis, [(i, i ^ mask) for i in range(size)])


def dim_of(name):
    inner = 2
    if name == "x":
        return "fsdp", 1, inner
    if name == "z":
        return "fsdp", inner, lax.axis_size("fsdp") // inner
    if name == "core":
        return "seq", 1, inner
    return "seq", inner, lax.axis_size("seq") // inner


def gather_dim(value, name, axis):
    mesh_axis, stride, size = dim_of(name)
    parts = [value] + [flip(value, mesh_axis, k * stride) for k in range(1, size)]
    return jnp.stack(parts, axis)


def scatter_dim(value, name, axis, last):
    mesh_axis, stride, size = dim_of(name)
    total = lax.index_in_dim(value, 0, axis, keepdims=False).astype(F32)
    for k in range(1, size):
        part = lax.index_in_dim(value, k, axis, keepdims=False)
        total = total + flip(part, mesh_axis, k * stride).astype(F32)
    return total if last else total.astype(BF)


def copy_kernel(source, target):
    target[...] = source[...].reshape(target.shape)


def gather_order_kernel(pieces, shift, *refs):
    sources, target = refs[:-1], refs[-1]
    width = target.shape[1] // (len(sources) * pieces)
    for o, source in enumerate(sources):
        for y in range(pieces):
            first = (o * pieces + y) * width
            target[:, first : first + width] = source[0, y ^ shift[1]]


def weights_in_order(parts, fsdp_index, y_index):
    count, pieces, rows, width = parts[0].shape
    total = len(parts) * pieces * width
    where = jnp.stack([fsdp_index, y_index]).astype(jnp.int32)

    def body(shift, *refs):
        gather_order_kernel(pieces, shift, *refs)

    return pl.pallas_call(
        body,
        grid_spec=pltpu.PrefetchScalarGridSpec(
            num_scalar_prefetch=1,
            grid=(count,),
            in_specs=[
                pl.BlockSpec((1, pieces, rows, width), lambda j, s: (j ^ s[0], 0, 0, 0))
                for _ in parts
            ],
            out_specs=pl.BlockSpec((rows, total), lambda j, s: (j, 0)),
        ),
        out_shape=jax.ShapeDtypeStruct((count * rows, total), parts[0].dtype),
        compiler_params=params(),
    )(where, *parts)


def rows_by_distance(value, orders, pieces, fsdp_index, y_index):
    count = lax.axis_size("fsdp")
    rows, width = value.shape[0] // (count * pieces), value.shape[1]
    share = width // orders
    if rows % 16:
        view = value.reshape(count, pieces, rows, orders, share)
        view = jnp.take(view, jnp.arange(count) ^ fsdp_index, axis=0)
        view = jnp.take(view, jnp.arange(pieces) ^ y_index, axis=1)
        return [view[:, :, :, o] for o in range(orders)]
    where = jnp.stack([fsdp_index, y_index]).astype(jnp.int32)

    def body(shift, source, *targets):
        for o, target in enumerate(targets):
            target[0, 0] = source[:, o * share : (o + 1) * share]

    return pl.pallas_call(
        body,
        grid_spec=pltpu.PrefetchScalarGridSpec(
            num_scalar_prefetch=1,
            grid=(count, pieces),
            in_specs=[
                pl.BlockSpec(
                    (rows, width),
                    lambda j, y, s: ((j ^ s[0]) * pieces + (y ^ s[1]), 0),
                )
            ],
            out_specs=[
                pl.BlockSpec((1, 1, rows, share), lambda j, y, s: (j, y, 0, 0))
            ]
            * orders,
        ),
        out_shape=[
            jax.ShapeDtypeStruct((count, pieces, rows, share), value.dtype)
        ]
        * orders,
        compiler_params=params(),
    )(where, value)


def columns_in_order(value, shift):
    count, rows, width = value.shape
    if width % 128:
        ordered = jnp.take(value, jnp.arange(count) ^ shift, axis=0)
        return jnp.moveaxis(ordered, 0, 1).reshape(rows, count * width)
    return pl.pallas_call(
        lambda s, source, target: copy_kernel(source, target),
        grid_spec=pltpu.PrefetchScalarGridSpec(
            num_scalar_prefetch=1,
            grid=(count,),
            in_specs=[pl.BlockSpec((1, rows, width), lambda j, s: (j ^ s[0], 0, 0))],
            out_specs=pl.BlockSpec((rows, width), lambda j, s: (0, j)),
        ),
        out_shape=jax.ShapeDtypeStruct((rows, count * width), value.dtype),
        compiler_params=params(),
    )(shift.reshape(1).astype(jnp.int32), value)


def columns_by_distance(value, count, shift):
    rows, width = value.shape[0], value.shape[1] // count
    if width % 128:
        blocks = jnp.moveaxis(value.reshape(rows, count, width), 1, 0)
        return jnp.take(blocks, jnp.arange(count) ^ shift, axis=0)
    return pl.pallas_call(
        lambda s, source, target: copy_kernel(source, target),
        grid_spec=pltpu.PrefetchScalarGridSpec(
            num_scalar_prefetch=1,
            grid=(count,),
            in_specs=[pl.BlockSpec((rows, width), lambda j, s: (0, j ^ s[0]))],
            out_specs=pl.BlockSpec((1, rows, width), lambda j, s: (j, 0, 0)),
        ),
        out_shape=jax.ShapeDtypeStruct((count, rows, width), value.dtype),
        compiler_params=params(),
    )(shift.reshape(1).astype(jnp.int32), value)


def keep_head(value, head, head_size):
    lane = lax.broadcasted_iota(jnp.int32, (1, value.shape[1]), 1)
    return jnp.where(lane // head_size == head, value, jnp.zeros_like(value))


def attend_kernel(head_size, chunk, query, keys, values, out, tops, inverses):
    length, width = keys.shape
    scale = jnp.asarray(head_size**-0.5, BF)
    for h in range(width // head_size):
        own_keys = keep_head(keys[...], h, head_size) * scale
        own_values = keep_head(values[...], h, head_size)
        for i in range(length // chunk):
            rows = pl.ds(i * chunk, chunk)
            scores = dot(own_keys, query[rows, :], NT)
            top = jnp.max(scores, axis=0, keepdims=True)
            exponent = jnp.exp(scores - top)
            inverse = 1.0 / jnp.sum(exponent, axis=0, keepdims=True)
            part = dot((exponent * inverse).astype(BF), own_values, TN)
            if h == 0:
                out[rows, :] = part.astype(BF)
            else:
                out[rows, :] = (out[rows, :].astype(F32) + part).astype(BF)
            tops[0, h : h + 1, rows] = top
            inverses[0, h : h + 1, rows] = inverse


def attend(query, keys, values, head_size):
    length, width = query.shape
    block = min(128, width)
    wide = pl.BlockSpec((length, block), lambda h: (0, h))
    flat = pl.BlockSpec((1, block // head_size, length), lambda h: (h, 0, 0))
    stats = jax.ShapeDtypeStruct((width // block, block // head_size, length), F32)
    return pl.pallas_call(
        functools.partial(attend_kernel, head_size, min(512, length)),
        grid=(width // block,),
        in_specs=[wide] * 3,
        out_specs=[wide, flat, flat],
        out_shape=[jax.ShapeDtypeStruct((length, width), BF), stats, stats],
        compiler_params=params(),
    )(query, keys, values)


def attend_back_kernel(
    head_size, chunk, query, keys, values, grad, tops, inverses, d_query, d_keys, d_values
):
    length, width = keys.shape
    scale = jnp.asarray(head_size**-0.5, BF)
    for h in range(width // head_size):
        own_keys = keep_head(keys[...], h, head_size) * scale
        own_values = keep_head(values[...], h, head_size)
        for i in range(length // chunk):
            rows = pl.ds(i * chunk, chunk)
            query_rows, grad_rows = query[rows, :], grad[rows, :]
            scores = dot(own_keys, query_rows, NT)
            probs = jnp.exp(scores - tops[0, h : h + 1, rows]) * inverses[0, h : h + 1, rows]
            d_probs = dot(own_values, grad_rows, NT)
            delta = jnp.sum(probs * d_probs, axis=0, keepdims=True)
            d_scores = (probs * (d_probs - delta)).astype(BF)
            value_part = dot(probs.astype(BF), keep_head(grad_rows, h, head_size), NN)
            key_part = dot(d_scores, keep_head(query_rows, h, head_size) * scale, NN)
            query_part = dot(d_scores, own_keys, TN)
            if h == 0 and i == 0:
                d_values[...] = value_part
                d_keys[...] = key_part
            else:
                d_values[...] += value_part
                d_keys[...] += key_part
            if h == 0:
                d_query[rows, :] = query_part
            else:
                d_query[rows, :] += query_part


def attend_back(query, keys, values, grad, tops, inverses, head_size):
    length, width = query.shape
    block = min(128, width)
    wide = pl.BlockSpec((length, block), lambda h: (0, h))
    flat = pl.BlockSpec((1, block // head_size, length), lambda h: (h, 0, 0))
    return pl.pallas_call(
        functools.partial(attend_back_kernel, head_size, min(512, length)),
        grid=(width // block,),
        in_specs=[wide] * 4 + [flat] * 2,
        out_specs=[wide] * 3,
        out_shape=[jax.ShapeDtypeStruct((length, width), F32)] * 3,
        compiler_params=params(),
    )(query, keys, values, grad, tops, inverses)


def rotary_table(head_size):
    half = head_size // 2
    pair = np.arange(half)
    bands = (half + 2) // 3
    frequency = np.power(np.float32(ROPE_BASE), -(pair // 3).astype(np.float32) / bands)
    angles = np.arange(GRID_SIDE, dtype=np.float32)[:, None] * frequency[None, :]
    chosen = (pair % 3)[None, None, :] == np.arange(3)[:, None, None]

    def table(of):
        return np.where(chosen, of[None], 0.0).reshape(3 * GRID_SIDE, half)

    cosine, sine = table(np.cos(angles)), table(np.sin(angles))
    return np.concatenate([cosine, cosine, -sine, sine], axis=1).astype(np.float32)


def rotary_rows(coords, head_size):
    cells = jnp.arange(GRID_SIDE)
    hot = (coords[:, :, None] == cells).astype(F32)
    hot = jnp.transpose(hot, (1, 0, 2)).reshape(coords.shape[1], 3 * GRID_SIDE)
    both = jnp.dot(hot, rotary_table(head_size), precision=lax.Precision.HIGHEST)
    return both[:, :head_size], both[:, head_size:]


def half_swap(values, head_size):
    length, width = values.shape
    halves = values.reshape(length, width // head_size, 2, head_size // 2)
    return halves[:, :, ::-1, :].reshape(length, width)


def turn(values, cosine, sine, head_size):
    repeats = values.shape[1] // head_size
    return values * jnp.tile(cosine, (1, repeats)) + half_swap(values, head_size) * jnp.tile(
        sine, (1, repeats)
    )


def normalise(values):
    row_mean = jnp.mean(values, axis=-1, keepdims=True)
    centred = values - row_mean
    row_var = jnp.mean(centred * centred, axis=-1, keepdims=True)
    inverse = lax.rsqrt(row_var + EPSILON)
    return centred * inverse, inverse


def norm_back(unit, inverse, d_unit):
    return inverse * (
        d_unit
        - jnp.mean(d_unit, axis=-1, keepdims=True)
        - unit * jnp.mean(d_unit * unit, axis=-1, keepdims=True)
    )


def gelu_exact(values_in):
    return jax.nn.gelu(values_in, approximate=False)


def on_device(
    block_input,
    out_cotangent,
    positions,
    w_qkv,
    w_out,
    w_up,
    w_down,
    norm_gains,
    norm_shifts,
    qkv_bias,
    proj_bias,
    up_bias,
    clip_threshold,
):
    clips, tokens, width = block_input.shape
    fsdp, seq = lax.axis_size("fsdp"), lax.axis_size("seq")
    outer = seq // 2
    head_size = width // HEADS
    group = width // seq
    hidden = up_bias.shape[0]
    share = hidden // (fsdp * seq)
    length = tokens * seq
    f = lax.axis_index("fsdp")
    s = lax.axis_index("seq")
    y, c = s // 2, s % 2

    def along_seq(value):
        rows = gather_dim(value, "y", 0)
        return gather_dim(rows, "core", 1).reshape((seq,) + value.shape)

    x_all = [along_seq(block_input[i]).reshape(length, width) for i in range(clips)]
    coords_all = jnp.moveaxis(along_seq(positions), 0, 2).reshape(3, clips, length)

    own_heads = lax.dynamic_index_in_dim(
        w_qkv.reshape(-1, 3, seq, group), s, 2, keepdims=False
    ).reshape(-1, 3 * group)
    halves = []
    for o, order in enumerate(("zx", "xz")):
        piece = own_heads[:, o * (3 * group // 2) : (o + 1) * (3 * group // 2)]
        shape = (fsdp, 1) + piece.shape
        if order == "zx":
            piece = gather_dim(gather_dim(piece, "z", 0), "x", 1)
        else:
            piece = gather_dim(gather_dim(piece, "x", 0), "z", 0)
        halves.append(piece.reshape(shape))
    full_qkv = weights_in_order(halves, f, jnp.zeros_like(f))

    def gathered(local):
        rows, columns = local.shape
        part = columns // (2 * outer)
        views = local.reshape(rows, 2, outer, part)
        parts = []
        for o, order in enumerate(("zxy", "zyx")):
            piece = lax.dynamic_index_in_dim(views[:, o], y, 1, keepdims=False)
            piece = gather_dim(piece, "z", 0)
            if order == "zxy":
                piece = gather_dim(gather_dim(piece, "x", 1), "y", 2)
            else:
                piece = gather_dim(gather_dim(piece, "y", 1), "x", 1)
            parts.append(piece.reshape(fsdp, outer, rows, part))
        return weights_in_order(parts, f, y)

    def summed(partial):
        parts = rows_by_distance(partial, 2, outer, f, y)
        sums = []
        for order, part in zip(("yxz", "xyz"), parts, strict=True):
            value = part.reshape((fsdp // 2, 2) + part.shape[1:])
            if order == "yxz":
                value = scatter_dim(scatter_dim(value, "y", 2, False), "x", 1, False)
            else:
                value = scatter_dim(scatter_dim(value, "x", 1, False), "y", 1, False)
            sums.append(scatter_dim(value, "z", 0, True))
        return jnp.concatenate(sums, axis=1)

    def core_part(value, axis):
        shape = value.shape
        view = value.reshape(shape[:axis] + (-1, 2, share) + shape[axis + 1 :])
        view = lax.dynamic_index_in_dim(view, c, axis + 1, keepdims=False)
        return view.reshape(shape[:axis] + (shape[axis] // 2,) + shape[axis + 1 :])

    full_out = gathered(w_out)
    full_up = gathered(core_part(w_up, 1))
    full_down = gathered(core_part(w_down, 0))
    own_up_bias = core_part(up_bias, 0)

    own_bias = lax.dynamic_index_in_dim(qkv_bias.reshape(3, seq, group), s, 1, keepdims=False)
    kept = []
    attended_parts = []
    for i in range(clips):
        unit, inverse = normalise(x_all[i].astype(F32))
        normed = (unit * norm_gains[0] + norm_shifts[0]).astype(BF)
        mixed = dot(normed, full_qkv, NN) + own_bias.reshape(-1)
        cosine, sine = rotary_rows(coords_all[:, i], head_size)
        query = turn(mixed[:, :group], cosine, sine, head_size).astype(BF)
        keys = turn(mixed[:, group : 2 * group], cosine, sine, head_size).astype(BF)
        values = mixed[:, 2 * group :].astype(BF)
        attended, tops, inverses = attend(query, keys, values, head_size)
        kept.append((normed, query, keys, values, tops, inverses, cosine, sine))
        blocks = attended.reshape(seq, tokens, group)
        attended_parts.append(
            jnp.stack([blocks[0]] + [flip(blocks[m], "seq", m) for m in range(1, seq)])
        )
    attended_own = columns_in_order(
        jnp.concatenate(attended_parts, axis=1), s
    )
    tops_own = functools.reduce(
        jnp.maximum, [jnp.max(k[4], axis=2).reshape(-1) for k in kept]
    )

    x_own = block_input.reshape(clips * tokens, width).astype(F32)
    g_own = out_cotangent.reshape(clips * tokens, width)
    resid1 = x_own + dot(attended_own, full_out, NN) + proj_bias[0]
    unit2, inverse2 = normalise(resid1)
    normed2 = (unit2 * norm_gains[1] + norm_shifts[1]).astype(BF)

    def pair(value):
        return jnp.concatenate([value, flip(value, "seq", 1)], axis=0)

    def pair_sum(value):
        half = value.shape[0] // 2
        return value[:half] + flip(value[half:], "seq", 1)

    normed2_chip = pair(normed2)
    g_chip = pair(g_own)
    hidden_pre = dot(normed2_chip, full_up, NN) + own_up_bias
    activated, gelu_pull = jax.vjp(gelu_exact, hidden_pre)
    activated = activated.astype(BF)
    block_out = (resid1 + pair_sum(dot(activated, full_down, NN)) + proj_bias[1]).astype(BF)

    grad_down = summed(dot(activated, g_chip, TN).astype(BF))
    d_hidden = gelu_pull(dot(g_chip, full_down, NT))[0].astype(BF)
    grad_up_half = summed(dot(normed2_chip, d_hidden, TN).astype(BF))
    up_bias_part = jnp.sum(d_hidden.astype(F32), axis=0)
    d_normed2 = pair_sum(dot(d_hidden, full_up, NT))
    gain2_part = jnp.sum(d_normed2 * unit2, axis=0)
    shift2_part = jnp.sum(d_normed2, axis=0)
    g_wide = g_own.astype(F32)
    down_bias_part = jnp.sum(g_wide, axis=0)
    d_resid1 = g_wide + norm_back(unit2, inverse2, d_normed2 * norm_gains[1])
    d_resid1_low = d_resid1.astype(BF)
    out_bias_part = jnp.sum(d_resid1_low.astype(F32), axis=0)

    d_attended = dot(d_resid1_low, full_out, NT).astype(BF)
    pieces = columns_by_distance(d_attended, seq, s).reshape(seq, clips, tokens, group)

    out_rows = dot(attended_own, d_resid1_low, TN).astype(BF)
    out_rows = out_rows.reshape(-1, 2, width // (fsdp * seq), width)
    mine = lax.dynamic_index_in_dim(out_rows, c, 1, keepdims=False)
    theirs = lax.dynamic_index_in_dim(out_rows, 1 - c, 1, keepdims=False)
    out_rows = (mine.astype(F32) + flip(theirs, "seq", 1).astype(F32)).astype(BF)
    grad_out = summed(out_rows.reshape(-1, width))

    d_normed1_parts = []
    qkv_part = 0.0
    qkv_bias_part = 0.0
    gain1_part = 0.0
    shift1_part = 0.0
    for i in range(clips):
        normed, query, keys, values, tops, inverses, cosine, sine = kept[i]
        grad = jnp.concatenate(
            [pieces[0, i]] + [flip(pieces[m, i], "seq", m) for m in range(1, seq)], axis=0
        )
        d_query, d_keys, d_values = attend_back(
            query, keys, values, grad, tops, inverses, head_size
        )
        d_mixed = jnp.concatenate(
            [
                turn(d_query, cosine, -sine, head_size),
                turn(d_keys, cosine, -sine, head_size),
                d_values,
            ],
            axis=1,
        ).astype(BF)
        qkv_part = qkv_part + dot(normed, d_mixed, TN)
        qkv_bias_part = qkv_bias_part + jnp.sum(d_mixed.astype(F32), axis=0)
        d_normed1 = dot(d_mixed, full_qkv, NT)
        unit, _ = normalise(x_all[i].astype(F32))
        gain1_part = gain1_part + jnp.sum(d_normed1 * unit, axis=0)
        shift1_part = shift1_part + jnp.sum(d_normed1, axis=0)
        d_normed1_parts.append(d_normed1.astype(BF))

    blocks = rows_by_distance(qkv_part.astype(BF), 2, 1, f, jnp.zeros_like(f))
    sums = []
    for order, part in zip(("xz", "zx"), blocks, strict=True):
        value = part.reshape((fsdp // 2, 2) + part.shape[2:])
        if order == "xz":
            value = scatter_dim(scatter_dim(value, "x", 1, False), "z", 0, True)
        else:
            value = scatter_dim(scatter_dim(value, "z", 0, False), "x", 0, True)
        sums.append(value)
    own_rows = jnp.concatenate(sums, axis=1).reshape(seq, -1, 3 * group)

    def rows_of(m):
        return lax.dynamic_index_in_dim(own_rows, s ^ m, 0, keepdims=False)

    arrived = jnp.stack([rows_of(0)] + [flip(rows_of(m), "seq", m) for m in range(1, seq)])
    ordered = [
        lax.dynamic_index_in_dim(arrived, s ^ t, 0, keepdims=False).reshape(-1, 3, 1, group)
        for t in range(seq)
    ]
    grad_qkv = jnp.concatenate(ordered, axis=2).reshape(-1, 3 * width)

    halves = grad_up_half.reshape(2, -1, fsdp * outer, share)
    mine = lax.dynamic_index_in_dim(halves, c, 0, keepdims=False)
    other = flip(lax.dynamic_index_in_dim(halves, 1 - c, 0, keepdims=False), "seq", 1)
    first = jnp.where(c == 0, mine, other)
    second = jnp.where(c == 0, other, mine)
    grad_up = jnp.stack([first, second], axis=2).reshape(-1, hidden)

    d_normed1 = jnp.stack([p.reshape(seq, tokens, width) for p in d_normed1_parts], axis=1)
    value = d_normed1.reshape((outer, 2) + d_normed1.shape[1:])
    value = scatter_dim(scatter_dim(value, "core", 1, False), "y", 0, True)
    unit1, inverse1 = normalise(x_own)
    d_unit1 = value.reshape(clips * tokens, width) * norm_gains[0]
    grad_input = (d_resid1 + norm_back(unit1, inverse1, d_unit1)).reshape(block_input.shape)

    qkv_slots = lax.dynamic_update_index_in_dim(
        jnp.zeros((3, seq, group), F32), qkv_bias_part.reshape(3, group), s, 1
    )
    up_slots = lax.dynamic_update_index_in_dim(
        jnp.zeros((fsdp * outer, 2, share), F32),
        up_bias_part.reshape(fsdp * outer, share),
        c,
        1,
    )
    devices = fsdp * seq
    rows = [
        gain1_part, gain2_part, shift1_part, shift2_part, out_bias_part, down_bias_part,
        qkv_slots.reshape(-1), up_slots.reshape(-1),
    ]
    rows = jnp.concatenate([r.reshape(devices, -1) for r in rows], axis=1)
    sums = lax.psum_scatter(rows, ("fsdp", "seq"), scatter_dimension=0, tiled=True)[0]
    one = width // devices
    grad_gains = sums[: 2 * one].reshape(2, one)
    grad_shifts = sums[2 * one : 4 * one].reshape(2, one)
    grad_proj_bias = sums[4 * one : 6 * one].reshape(2, one)
    grad_qkv_bias = sums[6 * one : 9 * one]
    grad_up_bias = sums[9 * one :]

    slots = jnp.full((seq, HEADS // seq), -jnp.inf, F32)
    slots = lax.dynamic_update_index_in_dim(slots, tops_own, s, 0)
    maxima = lax.pmax(slots.reshape(-1), ("fsdp", "seq"))
    threshold = clip_threshold[0]
    gamma = jnp.sqrt(threshold / jnp.maximum(maxima, threshold))
    columns = jnp.tile(jnp.repeat(gamma, head_size), 2)
    clipped = w_qkv[:, : 2 * width].astype(F32) * columns
    clipped_bias = qkv_bias[: 2 * width] * columns
    return (
        block_out.reshape(block_input.shape),
        grad_input,
        grad_qkv,
        grad_out,
        grad_up,
        grad_down,
        grad_gains,
        grad_shifts,
        grad_qkv_bias,
        grad_proj_bias,
        grad_up_bias,
        maxima,
        clipped,
        clipped_bias,
    )


def solution(mesh):
    in_specs = (
        P("fsdp", "seq", None),
        P("fsdp", "seq", None),
        P(None, "fsdp", "seq"),
        P("fsdp", None),
        P("fsdp", None),
        P("fsdp", None),
        P("fsdp", None),
        P(),
        P(),
        P(),
        P(),
        P(),
        P(),
    )
    out_specs = (
        P("fsdp", "seq", None),
        P("fsdp", "seq", None),
        P(("fsdp", "seq"), None),
        P(("fsdp", "seq"), None),
        P(("fsdp", "seq"), None),
        P(("fsdp", "seq"), None),
        P(None, ("fsdp", "seq")),
        P(None, ("fsdp", "seq")),
        P(("fsdp", "seq")),
        P(None, ("fsdp", "seq")),
        P(("fsdp", "seq")),
        P(),
        P("fsdp", None),
        P(),
    )
    return jax.shard_map(
        on_device, mesh=mesh, in_specs=in_specs, out_specs=out_specs, check_vma=False
    )
```

```python
import functools

import jax
import jax.numpy as jnp
import numpy as np
from jax import lax
from jax.experimental import pallas as pl
from jax.experimental.pallas import tpu as pltpu
from jax.sharding import Mesh
from jax.sharding import PartitionSpec as P

HEADS = 16
EPSILON = 1e-06
ROPE_BASE = 100.0
GRID_SIDE = 16

FSDP = ("z", "x")
SEQ = ("y", "core")

BF = jnp.bfloat16
F32 = jnp.float32
NN = (((1,), (0,)), ((), ()))
NT = (((1,), (1,)), ((), ()))
TN = (((0,), (0,)), ((), ()))


def dot(left, right, dims):
    return lax.dot_general(left, right, dims, preferred_element_type=F32)


def params(megabytes=62):
    return pltpu.CompilerParams(vmem_limit_bytes=megabytes << 20)


def axis_size(names):
    size = 1
    for name in names:
        size *= lax.axis_size(name)
    return size


def flip(value, axis, mask):
    size = axis_size(axis)
    return lax.ppermute(value, axis, [(i, i ^ mask) for i in range(size)])


def dim_of(name):
    inner = 2
    if name == "x":
        return FSDP, 1, inner
    if name == "z":
        return FSDP, inner, axis_size(FSDP) // inner
    if name == "core":
        return SEQ, 1, inner
    return SEQ, inner, axis_size(SEQ) // inner


def gather_dim(value, name, axis):
    mesh_axis, stride, size = dim_of(name)
    parts = [value] + [flip(value, mesh_axis, k * stride) for k in range(1, size)]
    return jnp.stack(parts, axis)


def scatter_dim(value, name, axis, last):
    mesh_axis, stride, size = dim_of(name)
    total = lax.index_in_dim(value, 0, axis, keepdims=False).astype(F32)
    for k in range(1, size):
        part = lax.index_in_dim(value, k, axis, keepdims=False)
        total = total + flip(part, mesh_axis, k * stride).astype(F32)
    return total if last else total.astype(BF)


def copy_kernel(source, target):
    target[...] = source[...].reshape(target.shape)


def gather_order_kernel(pieces, shift, *refs):
    sources, target = refs[:-1], refs[-1]
    width = target.shape[1] // (len(sources) * pieces)
    for o, source in enumerate(sources):
        for y in range(pieces):
            first = (o * pieces + y) * width
            target[:, first : first + width] = source[0, y ^ shift[1]]


def weights_in_order(parts, fsdp_index, y_index):
    count, pieces, rows, width = parts[0].shape
    total = len(parts) * pieces * width
    where = jnp.stack([fsdp_index, y_index]).astype(jnp.int32)

    def body(shift, *refs):
        gather_order_kernel(pieces, shift, *refs)

    return pl.pallas_call(
        body,
        grid_spec=pltpu.PrefetchScalarGridSpec(
            num_scalar_prefetch=1,
            grid=(count,),
            in_specs=[
                pl.BlockSpec((1, pieces, rows, width), lambda j, s: (j ^ s[0], 0, 0, 0))
                for _ in parts
            ],
            out_specs=pl.BlockSpec((rows, total), lambda j, s: (j, 0)),
        ),
        out_shape=jax.ShapeDtypeStruct((count * rows, total), parts[0].dtype),
        compiler_params=params(),
    )(where, *parts)


def rows_by_distance(value, orders, pieces, fsdp_index, y_index):
    count = axis_size(FSDP)
    rows, width = value.shape[0] // (count * pieces), value.shape[1]
    share = width // orders
    if rows % 16:
        view = value.reshape(count, pieces, rows, orders, share)
        view = jnp.take(view, jnp.arange(count) ^ fsdp_index, axis=0)
        view = jnp.take(view, jnp.arange(pieces) ^ y_index, axis=1)
        return [view[:, :, :, o] for o in range(orders)]
    where = jnp.stack([fsdp_index, y_index]).astype(jnp.int32)

    def body(shift, source, *targets):
        for o, target in enumerate(targets):
            target[0, 0] = source[:, o * share : (o + 1) * share]

    return pl.pallas_call(
        body,
        grid_spec=pltpu.PrefetchScalarGridSpec(
            num_scalar_prefetch=1,
            grid=(count, pieces),
            in_specs=[
                pl.BlockSpec(
                    (rows, width),
                    lambda j, y, s: ((j ^ s[0]) * pieces + (y ^ s[1]), 0),
                )
            ],
            out_specs=[
                pl.BlockSpec((1, 1, rows, share), lambda j, y, s: (j, y, 0, 0))
            ]
            * orders,
        ),
        out_shape=[
            jax.ShapeDtypeStruct((count, pieces, rows, share), value.dtype)
        ]
        * orders,
        compiler_params=params(),
    )(where, value)


def columns_in_order(value, shift):
    count, rows, width = value.shape
    if width % 128:
        ordered = jnp.take(value, jnp.arange(count) ^ shift, axis=0)
        return jnp.moveaxis(ordered, 0, 1).reshape(rows, count * width)
    return pl.pallas_call(
        lambda s, source, target: copy_kernel(source, target),
        grid_spec=pltpu.PrefetchScalarGridSpec(
            num_scalar_prefetch=1,
            grid=(count,),
            in_specs=[pl.BlockSpec((1, rows, width), lambda j, s: (j ^ s[0], 0, 0))],
            out_specs=pl.BlockSpec((rows, width), lambda j, s: (0, j)),
        ),
        out_shape=jax.ShapeDtypeStruct((rows, count * width), value.dtype),
        compiler_params=params(),
    )(shift.reshape(1).astype(jnp.int32), value)


def columns_by_distance(value, count, shift):
    rows, width = value.shape[0], value.shape[1] // count
    if width % 128:
        blocks = jnp.moveaxis(value.reshape(rows, count, width), 1, 0)
        return jnp.take(blocks, jnp.arange(count) ^ shift, axis=0)
    return pl.pallas_call(
        lambda s, source, target: copy_kernel(source, target),
        grid_spec=pltpu.PrefetchScalarGridSpec(
            num_scalar_prefetch=1,
            grid=(count,),
            in_specs=[pl.BlockSpec((rows, width), lambda j, s: (0, j ^ s[0]))],
            out_specs=pl.BlockSpec((1, rows, width), lambda j, s: (j, 0, 0)),
        ),
        out_shape=jax.ShapeDtypeStruct((count, rows, width), value.dtype),
        compiler_params=params(),
    )(shift.reshape(1).astype(jnp.int32), value)


def keep_head(value, head, head_size):
    lane = lax.broadcasted_iota(jnp.int32, (1, value.shape[1]), 1)
    return jnp.where(lane // head_size == head, value, jnp.zeros_like(value))


def attend_kernel(head_size, chunk, query, keys, values, out, tops, inverses):
    length, width = keys.shape
    scale = jnp.asarray(head_size**-0.5, BF)
    for h in range(width // head_size):
        own_keys = keep_head(keys[...], h, head_size) * scale
        own_values = keep_head(values[...], h, head_size)
        for i in range(length // chunk):
            rows = pl.ds(i * chunk, chunk)
            scores = dot(own_keys, query[rows, :], NT)
            top = jnp.max(scores, axis=0, keepdims=True)
            exponent = jnp.exp(scores - top)
            inverse = 1.0 / jnp.sum(exponent, axis=0, keepdims=True)
            part = dot((exponent * inverse).astype(BF), own_values, TN)
            if h == 0:
                out[rows, :] = part.astype(BF)
            else:
                out[rows, :] = (out[rows, :].astype(F32) + part).astype(BF)
            tops[0, h : h + 1, rows] = top
            inverses[0, h : h + 1, rows] = inverse


def attend(query, keys, values, head_size):
    length, width = query.shape
    block = min(128, width)
    wide = pl.BlockSpec((length, block), lambda h: (0, h))
    flat = pl.BlockSpec((1, block // head_size, length), lambda h: (h, 0, 0))
    stats = jax.ShapeDtypeStruct((width // block, block // head_size, length), F32)
    return pl.pallas_call(
        functools.partial(attend_kernel, head_size, min(512, length)),
        grid=(width // block,),
        in_specs=[wide] * 3,
        out_specs=[wide, flat, flat],
        out_shape=[jax.ShapeDtypeStruct((length, width), BF), stats, stats],
        compiler_params=params(),
    )(query, keys, values)


def attend_back_kernel(
    head_size, chunk, query, keys, values, grad, tops, inverses, d_query, d_keys, d_values
):
    length, width = keys.shape
    scale = jnp.asarray(head_size**-0.5, BF)
    for h in range(width // head_size):
        own_keys = keep_head(keys[...], h, head_size) * scale
        own_values = keep_head(values[...], h, head_size)
        for i in range(length // chunk):
            rows = pl.ds(i * chunk, chunk)
            query_rows, grad_rows = query[rows, :], grad[rows, :]
            scores = dot(own_keys, query_rows, NT)
            probs = jnp.exp(scores - tops[0, h : h + 1, rows]) * inverses[0, h : h + 1, rows]
            d_probs = dot(own_values, grad_rows, NT)
            delta = jnp.sum(probs * d_probs, axis=0, keepdims=True)
            d_scores = (probs * (d_probs - delta)).astype(BF)
            value_part = dot(probs.astype(BF), keep_head(grad_rows, h, head_size), NN)
            key_part = dot(d_scores, keep_head(query_rows, h, head_size) * scale, NN)
            query_part = dot(d_scores, own_keys, TN)
            if h == 0 and i == 0:
                d_values[...] = value_part
                d_keys[...] = key_part
            else:
                d_values[...] += value_part
                d_keys[...] += key_part
            if h == 0:
                d_query[rows, :] = query_part
            else:
                d_query[rows, :] += query_part


def attend_back(query, keys, values, grad, tops, inverses, head_size):
    length, width = query.shape
    block = min(128, width)
    wide = pl.BlockSpec((length, block), lambda h: (0, h))
    flat = pl.BlockSpec((1, block // head_size, length), lambda h: (h, 0, 0))
    return pl.pallas_call(
        functools.partial(attend_back_kernel, head_size, min(512, length)),
        grid=(width // block,),
        in_specs=[wide] * 4 + [flat] * 2,
        out_specs=[wide] * 3,
        out_shape=[jax.ShapeDtypeStruct((length, width), F32)] * 3,
        compiler_params=params(),
    )(query, keys, values, grad, tops, inverses)


def rotary_table(head_size):
    half = head_size // 2
    pair = np.arange(half)
    bands = (half + 2) // 3
    frequency = np.power(np.float32(ROPE_BASE), -(pair // 3).astype(np.float32) / bands)
    angles = np.arange(GRID_SIDE, dtype=np.float32)[:, None] * frequency[None, :]
    chosen = (pair % 3)[None, None, :] == np.arange(3)[:, None, None]

    def table(of):
        return np.where(chosen, of[None], 0.0).reshape(3 * GRID_SIDE, half)

    cosine, sine = table(np.cos(angles)), table(np.sin(angles))
    return np.concatenate([cosine, cosine, -sine, sine], axis=1).astype(np.float32)


def rotary_rows(coords, head_size):
    cells = jnp.arange(GRID_SIDE)
    hot = (coords[:, :, None] == cells).astype(F32)
    hot = jnp.transpose(hot, (1, 0, 2)).reshape(coords.shape[1], 3 * GRID_SIDE)
    both = jnp.dot(hot, rotary_table(head_size), precision=lax.Precision.HIGHEST)
    return both[:, :head_size], both[:, head_size:]


def half_swap(values, head_size):
    length, width = values.shape
    halves = values.reshape(length, width // head_size, 2, head_size // 2)
    return halves[:, :, ::-1, :].reshape(length, width)


def turn(values, cosine, sine, head_size):
    repeats = values.shape[1] // head_size
    return values * jnp.tile(cosine, (1, repeats)) + half_swap(values, head_size) * jnp.tile(
        sine, (1, repeats)
    )


def normalise(values):
    row_mean = jnp.mean(values, axis=-1, keepdims=True)
    centred = values - row_mean
    row_var = jnp.mean(centred * centred, axis=-1, keepdims=True)
    inverse = lax.rsqrt(row_var + EPSILON)
    return centred * inverse, inverse


def norm_back(unit, inverse, d_unit):
    return inverse * (
        d_unit
        - jnp.mean(d_unit, axis=-1, keepdims=True)
        - unit * jnp.mean(d_unit * unit, axis=-1, keepdims=True)
    )


def gelu_exact(values_in):
    return jax.nn.gelu(values_in, approximate=False)


def general_device(
    block_input,
    out_cotangent,
    positions,
    w_qkv,
    w_out,
    w_up,
    w_down,
    norm_gains,
    norm_shifts,
    qkv_bias,
    proj_bias,
    up_bias,
    clip_threshold,
):
    clips, tokens, width = block_input.shape
    fsdp, seq = axis_size(FSDP), axis_size(SEQ)
    outer = seq // 2
    head_size = width // HEADS
    group = width // seq
    hidden = up_bias.shape[0]
    share = hidden // (fsdp * seq)
    length = tokens * seq
    f = lax.axis_index(FSDP)
    s = lax.axis_index(SEQ)
    y, c = s // 2, s % 2

    def along_seq(value):
        rows = gather_dim(value, "y", 0)
        return gather_dim(rows, "core", 1).reshape((seq,) + value.shape)

    x_all = [along_seq(block_input[i]).reshape(length, width) for i in range(clips)]
    coords_all = jnp.moveaxis(along_seq(positions), 0, 2).reshape(3, clips, length)

    own_heads = lax.dynamic_index_in_dim(
        w_qkv.reshape(-1, 3, seq, group), s, 2, keepdims=False
    ).reshape(-1, 3 * group)
    halves = []
    for o, order in enumerate(("zx", "xz")):
        piece = own_heads[:, o * (3 * group // 2) : (o + 1) * (3 * group // 2)]
        shape = (fsdp, 1) + piece.shape
        if order == "zx":
            piece = gather_dim(gather_dim(piece, "z", 0), "x", 1)
        else:
            piece = gather_dim(gather_dim(piece, "x", 0), "z", 0)
        halves.append(piece.reshape(shape))
    full_qkv = weights_in_order(halves, f, jnp.zeros_like(f))

    def gathered(local):
        rows, columns = local.shape
        part = columns // (2 * outer)
        views = local.reshape(rows, 2, outer, part)
        parts = []
        for o, order in enumerate(("zxy", "zyx")):
            piece = lax.dynamic_index_in_dim(views[:, o], y, 1, keepdims=False)
            piece = gather_dim(piece, "z", 0)
            if order == "zxy":
                piece = gather_dim(gather_dim(piece, "x", 1), "y", 2)
            else:
                piece = gather_dim(gather_dim(piece, "y", 1), "x", 1)
            parts.append(piece.reshape(fsdp, outer, rows, part))
        return weights_in_order(parts, f, y)

    def summed(partial):
        parts = rows_by_distance(partial, 2, outer, f, y)
        sums = []
        for order, part in zip(("yxz", "xyz"), parts, strict=True):
            value = part.reshape((fsdp // 2, 2) + part.shape[1:])
            if order == "yxz":
                value = scatter_dim(scatter_dim(value, "y", 2, False), "x", 1, False)
            else:
                value = scatter_dim(scatter_dim(value, "x", 1, False), "y", 1, False)
            sums.append(scatter_dim(value, "z", 0, True))
        return jnp.concatenate(sums, axis=1)

    def core_part(value, axis):
        shape = value.shape
        view = value.reshape(shape[:axis] + (-1, 2, share) + shape[axis + 1 :])
        view = lax.dynamic_index_in_dim(view, c, axis + 1, keepdims=False)
        return view.reshape(shape[:axis] + (shape[axis] // 2,) + shape[axis + 1 :])

    full_out = gathered(w_out)
    full_up = gathered(core_part(w_up, 1))
    full_down = gathered(core_part(w_down, 0))
    own_up_bias = core_part(up_bias, 0)

    own_bias = lax.dynamic_index_in_dim(qkv_bias.reshape(3, seq, group), s, 1, keepdims=False)
    kept = []
    attended_parts = []
    for i in range(clips):
        unit, inverse = normalise(x_all[i].astype(F32))
        normed = (unit * norm_gains[0] + norm_shifts[0]).astype(BF)
        mixed = dot(normed, full_qkv, NN) + own_bias.reshape(-1)
        cosine, sine = rotary_rows(coords_all[:, i], head_size)
        query = turn(mixed[:, :group], cosine, sine, head_size).astype(BF)
        keys = turn(mixed[:, group : 2 * group], cosine, sine, head_size).astype(BF)
        values = mixed[:, 2 * group :].astype(BF)
        attended, tops, inverses = attend(query, keys, values, head_size)
        kept.append((normed, query, keys, values, tops, inverses, cosine, sine))
        blocks = attended.reshape(seq, tokens, group)
        attended_parts.append(
            jnp.stack([blocks[0]] + [flip(blocks[m], SEQ, m) for m in range(1, seq)])
        )
    attended_own = columns_in_order(
        jnp.concatenate(attended_parts, axis=1), s
    )
    tops_own = functools.reduce(
        jnp.maximum, [jnp.max(k[4], axis=2).reshape(-1) for k in kept]
    )

    x_own = block_input.reshape(clips * tokens, width).astype(F32)
    g_own = out_cotangent.reshape(clips * tokens, width)
    resid1 = x_own + dot(attended_own, full_out, NN) + proj_bias[0]
    unit2, inverse2 = normalise(resid1)
    normed2 = (unit2 * norm_gains[1] + norm_shifts[1]).astype(BF)

    def pair(value):
        return jnp.concatenate([value, flip(value, SEQ, 1)], axis=0)

    def pair_sum(value):
        half = value.shape[0] // 2
        return value[:half] + flip(value[half:], SEQ, 1)

    normed2_chip = pair(normed2)
    g_chip = pair(g_own)
    hidden_pre = dot(normed2_chip, full_up, NN) + own_up_bias
    activated, gelu_pull = jax.vjp(gelu_exact, hidden_pre)
    activated = activated.astype(BF)
    block_out = (resid1 + pair_sum(dot(activated, full_down, NN)) + proj_bias[1]).astype(BF)

    grad_down = summed(dot(activated, g_chip, TN).astype(BF))
    d_hidden = gelu_pull(dot(g_chip, full_down, NT))[0].astype(BF)
    grad_up_half = summed(dot(normed2_chip, d_hidden, TN).astype(BF))
    up_bias_part = jnp.sum(d_hidden.astype(F32), axis=0)
    d_normed2 = pair_sum(dot(d_hidden, full_up, NT))
    gain2_part = jnp.sum(d_normed2 * unit2, axis=0)
    shift2_part = jnp.sum(d_normed2, axis=0)
    g_wide = g_own.astype(F32)
    down_bias_part = jnp.sum(g_wide, axis=0)
    d_resid1 = g_wide + norm_back(unit2, inverse2, d_normed2 * norm_gains[1])
    d_resid1_low = d_resid1.astype(BF)
    out_bias_part = jnp.sum(d_resid1_low.astype(F32), axis=0)

    d_attended = dot(d_resid1_low, full_out, NT).astype(BF)
    pieces = columns_by_distance(d_attended, seq, s).reshape(seq, clips, tokens, group)

    out_rows = dot(attended_own, d_resid1_low, TN).astype(BF)
    out_rows = out_rows.reshape(-1, 2, width // (fsdp * seq), width)
    mine = lax.dynamic_index_in_dim(out_rows, c, 1, keepdims=False)
    theirs = lax.dynamic_index_in_dim(out_rows, 1 - c, 1, keepdims=False)
    out_rows = (mine.astype(F32) + flip(theirs, SEQ, 1).astype(F32)).astype(BF)
    grad_out = summed(out_rows.reshape(-1, width))

    d_normed1_parts = []
    qkv_part = 0.0
    qkv_bias_part = 0.0
    gain1_part = 0.0
    shift1_part = 0.0
    for i in range(clips):
        normed, query, keys, values, tops, inverses, cosine, sine = kept[i]
        grad = jnp.concatenate(
            [pieces[0, i]] + [flip(pieces[m, i], SEQ, m) for m in range(1, seq)], axis=0
        )
        d_query, d_keys, d_values = attend_back(
            query, keys, values, grad, tops, inverses, head_size
        )
        d_mixed = jnp.concatenate(
            [
                turn(d_query, cosine, -sine, head_size),
                turn(d_keys, cosine, -sine, head_size),
                d_values,
            ],
            axis=1,
        ).astype(BF)
        qkv_part = qkv_part + dot(normed, d_mixed, TN)
        qkv_bias_part = qkv_bias_part + jnp.sum(d_mixed.astype(F32), axis=0)
        d_normed1 = dot(d_mixed, full_qkv, NT)
        unit, _ = normalise(x_all[i].astype(F32))
        gain1_part = gain1_part + jnp.sum(d_normed1 * unit, axis=0)
        shift1_part = shift1_part + jnp.sum(d_normed1, axis=0)
        d_normed1_parts.append(d_normed1.astype(BF))

    blocks = rows_by_distance(qkv_part.astype(BF), 2, 1, f, jnp.zeros_like(f))
    sums = []
    for order, part in zip(("xz", "zx"), blocks, strict=True):
        value = part.reshape((fsdp // 2, 2) + part.shape[2:])
        if order == "xz":
            value = scatter_dim(scatter_dim(value, "x", 1, False), "z", 0, True)
        else:
            value = scatter_dim(scatter_dim(value, "z", 0, False), "x", 0, True)
        sums.append(value)
    own_rows = jnp.concatenate(sums, axis=1).reshape(seq, -1, 3 * group)

    def rows_of(m):
        return lax.dynamic_index_in_dim(own_rows, s ^ m, 0, keepdims=False)

    arrived = jnp.stack([rows_of(0)] + [flip(rows_of(m), SEQ, m) for m in range(1, seq)])
    ordered = [
        lax.dynamic_index_in_dim(arrived, s ^ t, 0, keepdims=False).reshape(-1, 3, 1, group)
        for t in range(seq)
    ]
    grad_qkv = jnp.concatenate(ordered, axis=2).reshape(-1, 3 * width)

    halves = grad_up_half.reshape(2, -1, fsdp * outer, share)
    mine = lax.dynamic_index_in_dim(halves, c, 0, keepdims=False)
    other = flip(lax.dynamic_index_in_dim(halves, 1 - c, 0, keepdims=False), SEQ, 1)
    first = jnp.where(c == 0, mine, other)
    second = jnp.where(c == 0, other, mine)
    grad_up = jnp.stack([first, second], axis=2).reshape(-1, hidden)

    d_normed1 = jnp.stack([p.reshape(seq, tokens, width) for p in d_normed1_parts], axis=1)
    value = d_normed1.reshape((outer, 2) + d_normed1.shape[1:])
    value = scatter_dim(scatter_dim(value, "core", 1, False), "y", 0, True)
    unit1, inverse1 = normalise(x_own)
    d_unit1 = value.reshape(clips * tokens, width) * norm_gains[0]
    grad_input = (d_resid1 + norm_back(unit1, inverse1, d_unit1)).reshape(block_input.shape)

    qkv_slots = lax.dynamic_update_index_in_dim(
        jnp.zeros((3, seq, group), F32), qkv_bias_part.reshape(3, group), s, 1
    )
    up_slots = lax.dynamic_update_index_in_dim(
        jnp.zeros((fsdp * outer, 2, share), F32),
        up_bias_part.reshape(fsdp * outer, share),
        c,
        1,
    )
    devices = fsdp * seq
    rows = [
        gain1_part, gain2_part, shift1_part, shift2_part, out_bias_part, down_bias_part,
        qkv_slots.reshape(-1), up_slots.reshape(-1),
    ]
    rows = jnp.concatenate([r.reshape(devices, -1) for r in rows], axis=1)
    sums = lax.psum_scatter(rows, FSDP + SEQ, scatter_dimension=0, tiled=True)[0]
    one = width // devices
    grad_gains = sums[: 2 * one].reshape(2, one)
    grad_shifts = sums[2 * one : 4 * one].reshape(2, one)
    grad_proj_bias = sums[4 * one : 6 * one].reshape(2, one)
    grad_qkv_bias = sums[6 * one : 9 * one]
    grad_up_bias = sums[9 * one :]

    slots = jnp.full((seq, HEADS // seq), -jnp.inf, F32)
    slots = lax.dynamic_update_index_in_dim(slots, tops_own, s, 0)
    maxima = lax.pmax(slots.reshape(-1), FSDP + SEQ)
    threshold = clip_threshold[0]
    gamma = jnp.sqrt(threshold / jnp.maximum(maxima, threshold))
    columns = jnp.tile(jnp.repeat(gamma, head_size), 2)
    clipped = w_qkv[:, : 2 * width].astype(F32) * columns
    clipped_bias = qkv_bias[: 2 * width] * columns
    return (
        block_out.reshape(block_input.shape),
        grad_input,
        grad_qkv,
        grad_out,
        grad_up,
        grad_down,
        grad_gains,
        grad_shifts,
        grad_qkv_bias,
        grad_proj_bias,
        grad_up_bias,
        maxima,
        clipped,
        clipped_bias,
    )


def flip_one(value, name):
    return lax.ppermute(value, name, [(0, 1), (1, 0)])


def after(value, *others):
    return lax.optimization_barrier((value, *others))[0]


def after_all(values, *others):
    return lax.optimization_barrier((tuple(values), *others))[0]


def add_low(*terms):
    return functools.reduce(jnp.add, [t.astype(F32) for t in terms]).astype(BF)


def cost(microseconds):
    return pl.CostEstimate(
        flops=int(microseconds * 0.05e9), bytes_accessed=1 << 20, transcendentals=0
    )


def whole(shape):
    return pl.BlockSpec(shape, lambda *_: (0,) * len(shape))


def in_order(index, bit, axis):
    return jnp.where(bit == 0, index, jnp.flip(index, axis))


def swap_halves(values, head_size):
    half = head_size // 2
    lane = lax.broadcasted_iota(jnp.int32, (1, values.shape[1]), 1)
    width = values.shape[1]
    return jnp.where(
        lane % head_size < half,
        pltpu.roll(values, width - half, 1),
        pltpu.roll(values, half, 1),
    )


def first_norm_kernel(first, second, gain, shift, normed, unit):
    tokens = first.shape[0]
    for i, part in enumerate((first, second)):
        value, _ = normalise(part[...].astype(F32))
        here = slice(i * tokens, (i + 1) * tokens)
        unit[0, here, :] = value.astype(BF)
        normed[0, here, :] = (value * gain[...] + shift[...]).astype(BF)


def first_norm(first, second, gain, shift, clips):
    rows, width = first.shape
    tokens = rows // clips
    block = pl.BlockSpec((tokens, width), lambda i: (i, 0))
    out = pl.BlockSpec((1, 2 * tokens, width), lambda i: (i, 0, 0))
    return pl.pallas_call(
        first_norm_kernel,
        grid=(clips,),
        in_specs=[block, block, whole((1, width)), whole((1, width))],
        out_specs=[out, out],
        out_shape=[jax.ShapeDtypeStruct((clips, 2 * tokens, width), BF)] * 2,
        compiler_params=params(),
        cost_estimate=cost(4),
        name="first_norm",
    )(first, second, gain, shift)


def own_columns(where, value, count, share):
    rows = value.shape[0]
    return pl.pallas_call(
        lambda w, source, target: copy_kernel(source, target),
        grid_spec=pltpu.PrefetchScalarGridSpec(
            num_scalar_prefetch=1,
            grid=(count,),
            in_specs=[
                pl.BlockSpec((rows, share), lambda k, w: (0, (k * 2 + w[1]) * 2 + w[2]))
            ],
            out_specs=pl.BlockSpec((rows, share), lambda k, w: (0, k)),
        ),
        out_shape=jax.ShapeDtypeStruct((rows, count * share), value.dtype),
        compiler_params=params(),
        cost_estimate=cost(3),
        name="own_columns",
    )(where, value)


def heads_forward_kernel(
    head_size, blocks, where, first_rows, last_rows, near, beside, bias, cosine, sine,
    query, keys, values, out, tops, inverses, weights,
):
    levels, rows, width = near.shape
    length, lanes = query.shape[1:]

    @pl.when(pl.program_id(0) == 0)
    def _():
        for z in range(levels):
            for part, bit in ((near, 0), (beside, 1)):
                first = (z * 2 + (where[0] ^ bit)) * rows
                weights[pl.ds(pl.multiple_of(first, rows), rows), :] = part[z]

    mixed = [dot(part[0], weights[...], NN) + bias[...] for part in (first_rows, last_rows)]
    mixed = jnp.concatenate(mixed, axis=0)
    turned = [
        part * cosine[0] + swap_halves(part, head_size) * sine[0]
        for part in (mixed[:, :lanes], mixed[:, lanes : 2 * lanes])
    ]
    query[0], keys[0] = turned[0].astype(BF), turned[1].astype(BF)
    values[0] = mixed[:, 2 * lanes :].astype(BF)
    scale = jnp.asarray(head_size**-0.5, BF)
    chunk = length // 2
    tokens = length // blocks
    for i in range(2):
        rows_here = pl.ds(i * chunk, chunk)
        query_rows = query[0, rows_here, :]
        total = None
        for h in range(lanes // head_size):
            own_keys = keep_head(keys[0], h, head_size) * scale
            own_values = keep_head(values[0], h, head_size)
            scores = dot(own_keys, query_rows, NT)
            top = jnp.max(scores, axis=0, keepdims=True)
            exponent = jnp.exp(scores - top)
            inverse = 1.0 / jnp.sum(exponent, axis=0, keepdims=True)
            part = dot((exponent * inverse).astype(BF), own_values, TN)
            total = part if total is None else total + part
            tops[0, h : h + 1, rows_here] = top
            inverses[0, h : h + 1, rows_here] = inverse
        low = total.astype(BF)
        for b in range(blocks // 2):
            out[i * (blocks // 2) + b, 0] = low[b * tokens : (b + 1) * tokens]


def heads_forward(where, normed, near, beside, bias, cosine, sine, blocks, head_size):
    clips, half, width = normed[0].shape
    length = 2 * half
    lanes = bias.shape[1] // 3
    pieces = whole(near.shape[:2] + bias.shape[1:])
    clip = lambda *rest: pl.BlockSpec((1,) + rest, lambda i, w: (i,) + (0,) * len(rest))
    head = jax.ShapeDtypeStruct((clips, length, lanes), BF)
    stats = jax.ShapeDtypeStruct((clips, lanes // head_size, length), F32)
    return pl.pallas_call(
        functools.partial(heads_forward_kernel, head_size, blocks),
        grid_spec=pltpu.PrefetchScalarGridSpec(
            num_scalar_prefetch=1,
            grid=(clips,),
            in_specs=[
                clip(half, width),
                clip(half, width),
                pieces,
                pieces,
                whole(bias.shape),
                clip(length, lanes),
                clip(length, lanes),
            ],
            out_specs=[clip(length, lanes)] * 3
            + [
                pl.BlockSpec(
                    (blocks, 1, length // blocks, lanes), lambda i, w: (0, i, 0, 0)
                )
            ]
            + [clip(lanes // head_size, length)] * 2,
            scratch_shapes=[pltpu.VMEM((width, 3 * lanes), BF)],
        ),
        out_shape=[
            head,
            head,
            head,
            jax.ShapeDtypeStruct((blocks, clips, length // blocks, lanes), BF),
            stats,
            stats,
        ],
        compiler_params=params(),
        cost_estimate=cost(15),
        name="heads_forward",
    )(where, *normed, near, beside, bias, cosine, sine)


def out_row(z, x, where, rows):
    index = z * 2 + x
    return ((((index // 2) ^ where[3]) * 2) + index % 2) * rows


def project_kernel(where, *refs, groups):
    pieces, refs = refs[: 4 * groups], refs[4 * groups :]
    x_blocks, refs = refs[:4], refs[4:]
    own, other, bias, gain, shift = refs[:5]
    resid, attended, normed, weights, joined = refs[5:]
    levels, rows, share = own.shape[2:]
    step = pl.program_id(0)

    @pl.when(step == 0)
    def _():
        for core, part in ((0, own), (1, other)):
            for far_y in range(2):
                column = ((where[1] ^ far_y) * 2 + (where[2] ^ core)) * share
                column = pl.ds(pl.multiple_of(column, share), share)
                for far_x in range(2):
                    for z in range(levels):
                        place = out_row(z, where[0] ^ far_x, where, rows)
                        place = pl.ds(pl.multiple_of(place, rows), rows)
                        weights[place, column] = part[far_y, far_x, z]

    lanes = pieces[0].shape[3]
    for h in range(groups):
        for m in range(4):
            first = (m * groups + h) * lanes
            joined[:, first : first + lanes] = pieces[h * 4 + m][0, 0]
    for b in range(4):

        @pl.when(step // 2 == b)
        def _(b=b):
            out = x_blocks[b][...].astype(F32)
            out = out + dot(joined[...], weights[...], NN) + bias[...]
            unit, _ = normalise(out)
            normed[...] = (unit * gain[...] + shift[...]).astype(BF)
            if b == 0:
                resid[...] = out
                attended[...] = joined[...]


def project(where, pieces, x_blocks, own, other, bias, gain, shift):
    clips, tokens, lanes = pieces[0][0].shape[1:]
    rows, width = x_blocks[0].shape
    piece_specs = [
        pl.BlockSpec((1, 1, tokens, lanes), lambda t, w, m=m: ((t // 2) ^ m, t % 2, 0, 0))
        for _ in pieces
        for m in range(4)
    ]
    x_specs = [
        pl.BlockSpec((tokens, width), lambda t, w, b=b: (jnp.clip(t - 2 * b, 0, 1), 0))
        for b in range(4)
    ]
    first = pl.BlockSpec((tokens, width), lambda t, w: (jnp.minimum(t, 1), 0))
    return pl.pallas_call(
        functools.partial(project_kernel, groups=len(pieces)),
        grid_spec=pltpu.PrefetchScalarGridSpec(
            num_scalar_prefetch=1,
            grid=(4 * clips,),
            in_specs=piece_specs
            + x_specs
            + [whole(own.shape), whole(other.shape)]
            + [whole((1, width))] * 3,
            out_specs=[
                first,
                first,
                pl.BlockSpec((tokens, width), lambda t, w: (t, 0)),
                whole((width, width)),
            ],
            scratch_shapes=[pltpu.VMEM((tokens, width), BF)],
        ),
        out_shape=[
            jax.ShapeDtypeStruct((rows, width), F32),
            jax.ShapeDtypeStruct((rows, width), BF),
            jax.ShapeDtypeStruct((4 * rows, width), BF),
            jax.ShapeDtypeStruct((width, width), BF),
        ],
        compiler_params=params(),
        cost_estimate=cost(13),
        name="project_out",
    )(where, *(p for group in pieces for p in group), *x_blocks, own, other, bias, gain, shift)


def gelu_pair(values):
    cumulative = 0.5 * (1.0 + lax.erf(values * np.float32(0.5**0.5)))
    density = jnp.exp(-0.5 * values * values) * np.float32((2.0 * np.pi) ** -0.5)
    return values * cumulative, cumulative + values * density


def up_kernel(
    where, normed, near, beside, bias, *refs
):
    grads, refs = refs[:4], refs[4:]
    activated, slope, columns, near_out, beside_out, held, low, sems = refs
    levels, rows, block = near.shape
    share = block // 2
    step = pl.program_id(0)
    tokens = normed.shape[0] // 4
    copies = [
        pltpu.make_async_copy(g, held.at[pl.ds(i * tokens, tokens)], sems.at[i])
        for i, g in enumerate(grads)
    ]

    @pl.when(step == 0)
    def _():
        for one in copies:
            one.start()

    for z in range(levels):
        for far_x, part in enumerate((near, beside)):
            first = (z * 2 + (where[0] ^ far_x)) * rows
            columns[pl.ds(pl.multiple_of(first, rows), rows), :] = part[z]
    for i in range(4):
        here = slice(i * tokens, (i + 1) * tokens)
        hidden = dot(normed[here, :], columns[...], NN) + bias[0]
        act, d_act = gelu_pair(hidden)
        activated[here, :] = act.astype(BF)
        slope[here, :] = d_act.astype(BF)

    @pl.when(step == 0)
    def _():
        for one in copies:
            one.wait()

    low[...] = dot(activated[...], held[...], TN).astype(BF)
    for far_x, out in enumerate((near_out, beside_out)):
        first = (where[0] ^ far_x) * share
        out[0] = low[pl.ds(pl.multiple_of(first, share), share), :]


def feed_up(where, normed, grads, pieces, bias):
    levels, rows, hidden = pieces[0].shape
    tokens, width = normed.shape
    block = hidden // levels
    by_column = pl.BlockSpec((levels, rows, block), lambda t, w: (0, 0, t))
    line = pl.BlockSpec((tokens, block), lambda t, w: (0, t))
    out = pl.BlockSpec((1, block // 2, width), lambda t, w: (t, 0, 0))
    return pl.pallas_call(
        up_kernel,
        grid_spec=pltpu.PrefetchScalarGridSpec(
            num_scalar_prefetch=1,
            grid=(levels,),
            in_specs=[whole((tokens, width)), by_column, by_column]
            + [pl.BlockSpec((1, 1, block), lambda t, w: (t, 0, 0))]
            + [pl.BlockSpec(memory_space=pl.ANY)] * 4,
            out_specs=[line, line, pl.BlockSpec((width, block), lambda t, w: (0, t)), out, out],
            scratch_shapes=[
                pltpu.VMEM((tokens, width), BF),
                pltpu.VMEM((block, width), BF),
                pltpu.SemaphoreType.DMA((4,)),
            ],
        ),
        out_shape=[jax.ShapeDtypeStruct((tokens, hidden), BF)] * 2
        + [jax.ShapeDtypeStruct((width, hidden), BF)]
        + [jax.ShapeDtypeStruct((levels, block // 2, width), BF)] * 2,
        compiler_params=params(),
        cost_estimate=cost(17),
        name="feed_up",
    )(where, normed, *pieces, bias, *grads)


def far_kernel(
    where, first_grad, last_grad, near, beside, slope, columns,
    first_back, last_back, weights, d_hidden, hidden, up,
):
    step = pl.program_id(0)
    steps = pl.num_programs(0) - 2
    share = near.shape[1]
    block = 2 * share
    tokens = first_grad.shape[0]

    @pl.when(step < steps)
    def _():
        for far_x, part in enumerate((near, beside)):
            first = (where[0] ^ far_x) * share
            weights[pl.ds(pl.multiple_of(first, share), share), :] = part[0]
        place = pl.ds(pl.multiple_of(step * block, block), block)
        up[:, place] = columns[...]
        for i, grad in enumerate((first_grad, last_grad)):
            here = slice(i * tokens, (i + 1) * tokens)
            d_act = dot(grad[...], weights[...], NT)
            low = (d_act * slope[here, :].astype(F32)).astype(BF)
            hidden[here, place] = low
            d_hidden[here, :] = low

    @pl.when(step == steps)
    def _():
        first_back[...] = dot(hidden[:tokens, :], up[...], NT)

    @pl.when(step == steps + 1)
    def _():
        last_back[...] = dot(hidden[tokens:, :], up[...], NT).astype(BF)


def feed_down_far(where, grads, pieces, slope, columns):
    levels, share, width = pieces[0].shape
    tokens = grads[0].shape[0]
    block = 2 * share
    hidden = levels * block
    at = lambda t: jnp.minimum(t, levels - 1)
    piece = pl.BlockSpec((1, share, width), lambda t, w: (at(t), 0, 0))
    return pl.pallas_call(
        far_kernel,
        grid_spec=pltpu.PrefetchScalarGridSpec(
            num_scalar_prefetch=1,
            grid=(levels + 2,),
            in_specs=[whole((tokens, width))] * 2
            + [piece, piece]
            + [
                pl.BlockSpec((2 * tokens, block), lambda t, w: (1, at(t))),
                pl.BlockSpec((width, block), lambda t, w: (0, at(t))),
            ],
            out_specs=[whole((tokens, width))] * 2
            + [
                pl.BlockSpec((block, width), lambda t, w: (at(t), 0)),
                pl.BlockSpec((2 * tokens, block), lambda t, w: (0, at(t))),
            ],
            scratch_shapes=[
                pltpu.VMEM((2 * tokens, hidden), BF),
                pltpu.VMEM((width, hidden), BF),
            ],
        ),
        out_shape=[
            jax.ShapeDtypeStruct((tokens, width), F32),
            jax.ShapeDtypeStruct((tokens, width), BF),
            jax.ShapeDtypeStruct((hidden, width), BF),
            jax.ShapeDtypeStruct((2 * tokens, hidden), BF),
        ],
        compiler_params=params(),
        cost_estimate=cost(8),
        name="feed_down_far",
    )(where, *grads, *pieces, slope, columns)


def near_kernel(
    where, normed, first_grad, last_grad, weights, slope, columns, far_hidden,
    first_back, last_back, sums, near_out, beside_out, flipped, hidden, up, product,
):
    step = pl.program_id(0)
    steps = pl.num_programs(0) - 2
    block = weights.shape[0]
    levels, rows = near_out.shape[:2]
    tokens = first_grad.shape[0]

    @pl.when(step == 0)
    def _():
        for i in range(4):
            here = slice(i * tokens, (i + 1) * tokens)
            flipped[:, here] = normed[here, :].T

    @pl.when(step < steps)
    def _():
        place = pl.ds(pl.multiple_of(step * block, block), block)
        up[:, place] = columns[...]
        parts = []
        for i, grad in enumerate((first_grad, last_grad)):
            here = slice(i * tokens, (i + 1) * tokens)
            d_act = dot(grad[...], weights[...], NT)
            low = (d_act * slope[here, :].astype(F32)).astype(BF)
            hidden[here, place] = low
            parts.append(low)
        parts.append(far_hidden[...])
        every = jnp.concatenate(parts, axis=0)
        sums[0] = jnp.sum(every.astype(F32), axis=0, keepdims=True)
        product[...] = dot(flipped[...], every, NN).astype(BF)
        for far_x, out in enumerate((near_out, beside_out)):
            for z in range(levels):
                first = (z * 2 + (where[0] ^ far_x)) * rows
                out[z] = product[pl.ds(pl.multiple_of(first, rows), rows), :]

    @pl.when(step == steps)
    def _():
        first_back[...] = dot(hidden[:tokens, :], up[...], NT)

    @pl.when(step == steps + 1)
    def _():
        last_back[...] = dot(hidden[tokens:, :], up[...], NT).astype(BF)


def feed_down_near(where, normed, grads, weights, slope, columns, far_hidden, levels):
    tokens, width = grads[0].shape
    hidden = weights.shape[0]
    block = hidden // levels
    rows = width // (2 * levels)
    at = lambda t: jnp.minimum(t, levels - 1)
    line = pl.BlockSpec((2 * tokens, block), lambda t, w: (0, at(t)))
    out = pl.BlockSpec((levels, rows, block), lambda t, w: (0, 0, at(t)))
    return pl.pallas_call(
        near_kernel,
        grid_spec=pltpu.PrefetchScalarGridSpec(
            num_scalar_prefetch=1,
            grid=(levels + 2,),
            in_specs=[whole((4 * tokens, width))]
            + [whole((tokens, width))] * 2
            + [
                pl.BlockSpec((block, width), lambda t, w: (at(t), 0)),
                line,
                pl.BlockSpec((width, block), lambda t, w: (0, at(t))),
                line,
            ],
            out_specs=[whole((tokens, width))] * 2
            + [pl.BlockSpec((1, 1, block), lambda t, w: (at(t), 0, 0)), out, out],
            scratch_shapes=[
                pltpu.VMEM((width, 4 * tokens), BF),
                pltpu.VMEM((2 * tokens, hidden), BF),
                pltpu.VMEM((width, hidden), BF),
                pltpu.VMEM((width, block), BF),
            ],
        ),
        out_shape=[
            jax.ShapeDtypeStruct((tokens, width), F32),
            jax.ShapeDtypeStruct((tokens, width), BF),
            jax.ShapeDtypeStruct((levels, 1, block), F32),
        ]
        + [jax.ShapeDtypeStruct((levels, rows, hidden), BF)] * 2,
        compiler_params=params(),
        cost_estimate=cost(12),
        name="feed_down_near",
    )(where, normed, *grads, weights, slope, columns, far_hidden)


def part_kernel(activated, weights, near, beside):
    out = dot(activated[...], weights[...], NN)

    @pl.when(pl.program_id(0) % 2 == 0)
    def _():
        near[0] = out

    @pl.when(pl.program_id(0) % 2 == 1)
    def _():
        beside[0] = out.astype(BF)


def feed_out(activated, weights):
    rows, (hidden, width) = activated.shape[0] // 4, weights.shape
    out = pl.BlockSpec((1, rows, width), lambda b: (b // 2, 0, 0))
    return pl.pallas_call(
        part_kernel,
        grid=(4,),
        in_specs=[pl.BlockSpec((rows, hidden), lambda b: (b, 0)), whole(weights.shape)],
        out_specs=[out, out],
        out_shape=[
            jax.ShapeDtypeStruct((2, rows, width), F32),
            jax.ShapeDtypeStruct((2, rows, width), BF),
        ],
        compiler_params=params(),
        cost_estimate=cost(7),
        name="feed_out",
    )(activated, weights)


def norm_back_kernel(
    where, own, arrived, far, resid, grad, gain, weights, d_resid, d_low, *rest
):
    outs, sums = rest[:-1], rest[-1]
    d_normed = own[...] + arrived[...].astype(F32) + far[...].astype(F32)
    unit, inverse = normalise(resid[...])
    wide = grad[...].astype(F32)
    out = wide + norm_back(unit, inverse, d_normed * gain[...])
    low = out.astype(BF)
    d_resid[...] = out
    d_low[...] = low
    parts = [d_normed * unit, d_normed, low.astype(F32), wide]
    parts = [jnp.sum(p, axis=0, keepdims=True) for p in parts]
    parts = jnp.concatenate(parts + [jnp.zeros_like(parts[0])] * 4, axis=0)

    @pl.when(pl.program_id(0) == 0)
    def _():
        sums[...] = parts

    @pl.when(pl.program_id(0) > 0)
    def _():
        sums[...] += parts

    d_attended = dot(low, weights[...], NT).astype(BF)
    for h, out in enumerate(outs):
        for s in range(out.shape[0]):
            lanes = out.shape[2]
            first = (s * len(outs) + h) * lanes
            out[s ^ where[3]] = d_attended[:, first : first + lanes]


def second_norm_back(where, own, arrived, far, resid, grad, gain, weights, seq, groups):
    rows, width = resid.shape
    step = rows // 2
    lanes = width // (seq * groups)
    line = pl.BlockSpec((step, width), lambda i, w: (i, 0))
    return pl.pallas_call(
        norm_back_kernel,
        grid_spec=pltpu.PrefetchScalarGridSpec(
            num_scalar_prefetch=1,
            grid=(rows // step,),
            in_specs=[line] * 5 + [whole((1, width)), whole((width, width))],
            out_specs=[line, line]
            + [pl.BlockSpec((seq, step, lanes), lambda i, w: (0, i, 0))] * groups
            + [whole((8, width))],
        ),
        out_shape=[
            jax.ShapeDtypeStruct((rows, width), F32),
            jax.ShapeDtypeStruct((rows, width), BF),
        ]
        + [jax.ShapeDtypeStruct((seq, rows, lanes), BF)] * groups
        + [jax.ShapeDtypeStruct((8, width), F32)],
        compiler_params=params(),
        cost_estimate=cost(8),
        name="second_norm_back",
    )(where, own, arrived, far, resid, grad, gain, weights)


def out_grad_kernel(where, attended, grad, near, beside, product):
    product[...] = dot(attended[...], grad[...], TN).astype(BF)
    levels, rows = near.shape[2:4]
    for m in range(4):
        out = (near, beside)[m % 2]
        for far_x in range(2):
            for z in range(levels):
                first = out_row(z, where[0] ^ far_x, where, 4 * rows) + (where[3] ^ m) * rows
                out[m // 2, far_x, z] = product[pl.ds(pl.multiple_of(first, rows), rows), :]


def out_grad(where, attended, grad, levels):
    width = grad.shape[1]
    shape = (2, 2, levels, width // (8 * levels), width)
    return pl.pallas_call(
        out_grad_kernel,
        grid_spec=pltpu.PrefetchScalarGridSpec(
            num_scalar_prefetch=1,
            grid=(1,),
            in_specs=[whole(attended.shape), whole(grad.shape)],
            out_specs=[whole(shape)] * 2,
            scratch_shapes=[pltpu.VMEM((width, width), BF)],
        ),
        out_shape=[jax.ShapeDtypeStruct(shape, BF)] * 2,
        compiler_params=params(),
        cost_estimate=cost(4),
        name="out_grad",
    )(where, attended, grad)


def heads_back_kernel(
    head_size, blocks, last, where, grad, query, keys, values, tops, inverses,
    cosine, sine, first_rows, last_rows, *rest,
):
    if last:
        near, beside, near0, beside0, earlier, first_unit, last_unit, *rest = rest
        norm_sums2, up_sums, tops_row, earlier_sum, *rest = rest
        sent_back, sent_beside, near_grad, beside_grad, *rest = rest
        weights, joined, vectors, norm_sums, bias_sum, total, d_keys, d_values, grads = rest
    else:
        sent_back, near_grad, beside_grad, bias_sum, *rest = rest
        total, d_keys, d_values, grads = rest
    levels, rows = near_grad.shape[0], near_grad.shape[2]
    length, lanes = query.shape[1:]
    three = 3 * lanes
    tokens = length // blocks
    clip = pl.program_id(0)

    if last:

        @pl.when(clip == 0)
        def _():
            for z in range(levels):
                for bit, parts in enumerate(((near0, near), (beside0, beside))):
                    first = (z * 2 + (where[0] ^ bit)) * rows
                    here = pl.ds(pl.multiple_of(first, rows), rows)
                    for h, part in enumerate(parts):
                        weights[here, h * three : (h + 1) * three] = part[z]

    for b in range(blocks):
        grads[b * tokens : (b + 1) * tokens, :] = grad[b ^ where[1], 0]
    scale = jnp.asarray(head_size**-0.5, BF)
    chunk = length // 2
    parts = []
    for i in range(2):
        here = pl.ds(i * chunk, chunk)
        query_rows, grad_rows = query[0, here, :], grads[here, :]
        query_total = None
        for h in range(lanes // head_size):
            own_keys = keep_head(keys[0], h, head_size) * scale
            own_values = keep_head(values[0], h, head_size)
            scores = dot(own_keys, query_rows, NT)
            probs = jnp.exp(scores - tops[0, h : h + 1, here]) * inverses[0, h : h + 1, here]
            d_probs = dot(own_values, grad_rows, NT)
            delta = jnp.sum(probs * d_probs, axis=0, keepdims=True)
            d_scores = (probs * (d_probs - delta)).astype(BF)
            value_part = dot(probs.astype(BF), keep_head(grad_rows, h, head_size), NN)
            key_part = dot(d_scores, keep_head(query_rows, h, head_size) * scale, NN)
            query_part = dot(d_scores, own_keys, TN)
            if h == 0 and i == 0:
                d_values[...] = value_part
                d_keys[...] = key_part
            else:
                d_values[...] += value_part
                d_keys[...] += key_part
            query_total = query_part if query_total is None else query_total + query_part
        parts.append(query_total)
    d_query = jnp.concatenate(parts, axis=0)

    def back(part):
        return (part * cosine[0] - swap_halves(part, head_size) * sine[0]).astype(BF)

    d_mixed = jnp.concatenate(
        [back(d_query), back(d_keys[...]), d_values[...].astype(BF)], axis=1
    )
    sums = jnp.sum(d_mixed.astype(F32), axis=0, keepdims=True)
    half = length // 2
    part = dot(d_mixed[:half], first_rows[0], TN) + dot(d_mixed[half:], last_rows[0], TN)

    @pl.when(clip == 0)
    def _():
        bias_sum[...] = sums
        total[...] = part

    @pl.when(clip > 0)
    def _():
        bias_sum[...] += sums
        total[...] += part

    def put_grads(bit, out):
        for z in range(levels):
            first = (z * 2 + (where[0] ^ bit)) * rows
            out[z, :three, :] = total[:, pl.ds(pl.multiple_of(first, rows), rows)].astype(BF)

    if not last:
        sent_back[0] = d_mixed

        @pl.when(clip == pl.num_programs(0) - 1)
        def _():
            put_grads(0, near_grad)
            put_grads(1, beside_grad)

        return
    joined[:, :three] = earlier[0]
    joined[:, three:] = d_mixed
    both = 0.0
    for i, unit in enumerate((first_unit, last_unit)):
        d_normed = dot(joined[i * half : (i + 1) * half, :], weights[...], NT)
        two = [
            jnp.sum(d_normed * unit[0].astype(F32), axis=0, keepdims=True),
            jnp.sum(d_normed, axis=0, keepdims=True),
        ]
        both = both + jnp.concatenate(two + [jnp.zeros_like(two[0])] * 6, axis=0)
        low = d_normed.astype(BF)
        for b in range(blocks // 2):
            out = (sent_back, sent_beside)[b % 2]
            out[i * (blocks // 4) + b // 2, 0] = low[b * tokens : (b + 1) * tokens]

    @pl.when(clip == 0)
    def _():
        norm_sums[...] = both

    @pl.when(clip > 0)
    def _():
        norm_sums[...] += both

    @pl.when(clip == pl.num_programs(0) - 1)
    def _():
        vectors[...] = jnp.zeros_like(vectors)
        for f in range(2 * levels):
            here = slice(f * rows, (f + 1) * rows)
            for row, (source, at) in enumerate(
                ((norm_sums, 0), (norm_sums2, 0), (norm_sums, 1), (norm_sums2, 1),
                 (norm_sums2, 2), (norm_sums2, 3))
            ):
                vectors[f, row : row + 1, :] = source[at : at + 1, here]
            vectors[f, pl.ds(9 + where[1], 1), :] = up_sums[f // 2, :, (f % 2) * rows : (f % 2 + 1) * rows]
            vectors[f, VECTOR_ROWS - 1 : VECTOR_ROWS, :] = tops_row[...]
        for h, source in enumerate((earlier_sum, bias_sum)):
            for part in range(3):
                place = (part * blocks + where[1]) * 2 + h
                at = 6 + lax.rem(place, 3)
                vectors[place // 3, pl.ds(at, 1), :] = source[:, part * lanes : (part + 1) * lanes]
        put_grads(0, near_grad)
        put_grads(1, beside_grad)
        for z in range(levels):
            for bit, out in ((0, near_grad), (1, beside_grad)):
                out[z, three:, :] = vectors[z * 2 + (where[0] ^ bit)].astype(BF)


def heads_back(
    where, grad, saved, cosine, sine, normed, levels, blocks, head_size, weights=(), earlier=None, unit=None, vectors=()
):
    clips, half, width = normed[0].shape
    length, lanes = 2 * half, grad.shape[3]
    three, rows = 3 * lanes, width // (2 * levels)
    last = earlier is not None
    clip = lambda *rest: pl.BlockSpec((1,) + rest, lambda i, w: (i,) + (0,) * len(rest))
    by_block = lambda m, n: pl.BlockSpec(
        (m, 1, length // blocks, n), lambda i, w: (0, i, 0, 0)
    )
    stats = clip(lanes // head_size, length)
    query, keys, values, tops, inverses = saved
    grads = (levels, three + (VECTOR_ROWS + 2 if last else 0), rows)
    outs = [jax.ShapeDtypeStruct(grads, BF)] * 2
    out_specs = [whole(grads)] * 2
    in_specs = [by_block(blocks, lanes)] + [clip(length, lanes)] * 3 + [stats] * 2
    in_specs += [clip(length, lanes)] * 2 + [clip(half, width)] * 2
    scratch = [
        pltpu.VMEM((three, width), F32),
        pltpu.VMEM((length, lanes), F32),
        pltpu.VMEM((length, lanes), F32),
        pltpu.VMEM((length, lanes), BF),
    ]
    if last:
        outs = [jax.ShapeDtypeStruct((blocks // 2, clips, length // blocks, width), BF)] * 2 + outs
        out_specs = [by_block(blocks // 2, width)] * 2 + out_specs
        in_specs += [whole(w.shape[:2] + (three,)) for w in weights]
        in_specs += [clip(length, three)] + [clip(half, width)] * 2
        in_specs += [whole(v.shape) for v in vectors]
        scratch = [
            pltpu.VMEM((width, 2 * three), BF),
            pltpu.VMEM((length, 2 * three), BF),
            pltpu.VMEM((2 * levels, VECTOR_ROWS + 2, lanes), F32),
            pltpu.VMEM((8, width), F32),
            pltpu.VMEM((1, three), F32),
        ] + scratch
    else:
        outs = [jax.ShapeDtypeStruct((clips, length, three), BF)] + outs
        outs += [jax.ShapeDtypeStruct((1, three), F32)]
        out_specs = [clip(length, three)] + out_specs + [whole((1, three))]
    return pl.pallas_call(
        functools.partial(heads_back_kernel, head_size, blocks, last),
        grid_spec=pltpu.PrefetchScalarGridSpec(
            num_scalar_prefetch=1,
            grid=(clips,),
            in_specs=in_specs,
            out_specs=out_specs,
            scratch_shapes=scratch,
        ),
        out_shape=outs,
        compiler_params=params(),
        cost_estimate=cost(22),
        name="heads_back",
    )(
        where, grad, query, keys, values, tops, inverses, cosine, sine, *normed,
        *weights, *([earlier, *unit, *vectors] if last else []),
    )


VECTOR_ROWS = 14


def square_device(
    block_input,
    out_cotangent,
    positions,
    w_qkv,
    w_out,
    w_up,
    w_down,
    norm_gains,
    norm_shifts,
    qkv_bias,
    proj_bias,
    up_bias,
    clip_threshold,
):
    clips, tokens, width = block_input.shape
    fsdp, seq = axis_size(FSDP), axis_size(SEQ)
    levels, outer = fsdp // 2, seq // 2
    head_size = width // HEADS
    group = width // seq
    lanes = 128
    groups = group // lanes
    hidden = up_bias.shape[0]
    share = hidden // (fsdp * seq)
    length = tokens * seq
    rows = width // fsdp
    levels_index = lax.axis_index("z")
    x, y, c = lax.axis_index("x"), lax.axis_index("y"), lax.axis_index("core")
    s = y * 2 + c
    heads_where = jnp.stack([x, s]).astype(jnp.int32)
    where = jnp.stack([x, y, c, s]).astype(jnp.int32)
    x_own = block_input.reshape(clips * tokens, width)
    g_own = out_cotangent.reshape(clips * tokens, width)

    def copies(piece):
        return jnp.broadcast_to(piece[None], (levels,) + piece.shape)

    def over_z(piece):
        return lax.all_to_all(piece, "z", 0, 0, tiled=True)

    def heads_piece(h):
        firsts = [(part * seq + s) * group + h * lanes for part in range(3)]
        return copies(
            jnp.concatenate(
                [lax.dynamic_slice_in_dim(w_qkv, first, lanes, 1) for first in firsts], axis=1
            )
        )

    x_beside = flip_one(x_own, "y")
    near0 = over_z(heads_piece(0))
    x_core = flip_one(x_own, "core")

    out_part = lax.dynamic_slice_in_dim(w_out, s * group, group, 1)
    piece1 = jnp.concatenate([heads_piece(1), copies(out_part)], axis=2)
    near1 = over_z(after(piece1, near0))
    beside0 = flip_one(near0, "x")

    up = own_columns(where, w_up, fsdp, share)
    up = lax.all_gather(after(up, near0), "z", axis=0)
    down = lax.dynamic_slice_in_dim(w_down, s * share, share, 0)
    down = lax.all_gather(after(down, near1), "z", axis=0)

    halves = [first_norm(x_own, x_core, norm_gains[:1], norm_shifts[:1], clips)]
    x_far = flip_one(x_beside, "core")
    halves.append(first_norm(x_beside, x_far, norm_gains[:1], norm_shifts[:1], clips))
    normed1, unit1 = zip(*halves, strict=True)
    x_blocks = (x_own, x_core, x_beside, x_far)
    g_beside = flip_one(after(g_own, x_beside), "y")
    g_core = flip_one(after(g_own, near1), "core")
    g_far = flip_one(g_beside, "core")
    coords = jnp.moveaxis(positions, 0, 2)
    coords = jnp.stack([coords, flip_one(coords, "y")])
    coords = jnp.stack([coords, flip_one(coords, "core")], axis=1)
    coords = jnp.moveaxis(coords.reshape(seq, clips, tokens, 3), 3, 0)
    coords = jnp.swapaxes(coords, 1, 2).reshape(3, clips * length)
    cosine, sine = rotary_rows(coords, head_size)
    repeats = lanes // head_size
    cosine = jnp.tile(cosine, (1, repeats)).reshape(clips, length, lanes)
    sine = jnp.tile(sine, (1, repeats)).reshape(clips, length, lanes)

    own_bias = lax.dynamic_index_in_dim(
        qkv_bias.reshape(3, seq, groups, lanes), s, 1, keepdims=False
    )

    def forward(h, near, beside):
        return heads_forward(
            heads_where, normed1, near, beside, own_bias[:, h].reshape(1, -1),
            cosine, sine, seq, head_size,
        )

    def from_heads(own):
        beside = flip_one(own, "y")
        return own, flip_one(own, "core"), beside, flip_one(beside, "core")

    beside1 = flip_one(near1, "x")
    *saved0, out0, tops0, inverses0 = forward(0, near0, beside0)
    saved0 += [tops0, inverses0]
    own_out = jnp.stack([near1[..., 3 * lanes :], beside1[..., 3 * lanes :]])
    own_out = jnp.stack([own_out, flip_one(own_out, "y")])
    other_out = flip_one(own_out, "core")
    pieces0 = from_heads(out0)
    up = (up, flip_one(after(up, tops0), "x"))

    *saved1, out1, tops1, inverses1 = forward(1, after(near1, up[0]), beside1)
    saved1 += [tops1, inverses1]
    pieces1 = from_heads(out1)
    down = (down, flip_one(after(down, tops1), "x"))
    tops_own = jnp.concatenate([jnp.max(t, axis=(0, 2)) for t in (tops0, tops1)])

    resid1, attended_own, normed2, full_out = project(
        where, (pieces0, pieces1), x_blocks, own_out, other_out,
        proj_bias[:1], norm_gains[1:], norm_shifts[1:],
    )

    bias = up_bias.reshape(levels, 2, seq, share)
    bias = lax.dynamic_index_in_dim(bias, s, 2, keepdims=False).reshape(levels, 1, 2 * share)
    grads = (g_own, g_core, g_beside, g_far)
    activated, slope, columns, down_near, down_beside = feed_up(where, normed2, grads, up, bias)
    down_beside = flip_one(down_beside, "x")
    far_back, far_other, full_down, far_hidden = feed_down_far(
        where, grads[2:], down, slope, columns
    )
    far_back = flip_one(add_low(far_back, flip_one(far_other, "core")), "y")
    own_back, other_back, up_sums, up_near, up_beside = feed_down_near(
        where, normed2, grads[:2], full_down, slope, columns, far_hidden, levels
    )
    other_back = flip_one(other_back, "core")
    up_beside = flip_one(up_beside, "x")
    part_near, part_beside = feed_out(after(activated, up_sums), full_down)
    part_beside = flip_one(part_beside, "core")
    down_sum = add_low(down_near, after(down_beside, up_sums))
    d_resid1, d_resid1_low, *rest = second_norm_back(
        where, own_back, other_back, far_back, resid1, g_own, norm_gains[1:], full_out,
        seq, groups,
    )
    d_attended, sums2 = rest[:-1], rest[-1]

    def to_heads(d):
        return lax.all_to_all(d.reshape(seq, clips, tokens, lanes), SEQ, 0, 0, tiled=True)

    d_heads0 = to_heads(d_attended[0])
    d_heads1 = to_heads(d_attended[1])
    grad_down = lax.psum_scatter(down_sum, "z", scatter_dimension=0, tiled=True)
    grad_down = grad_down.reshape(share, width).astype(F32)
    out_near, out_beside = out_grad(where, attended_own, d_resid1_low, levels)
    out_beside = flip_one(out_beside, "core")
    part_far = add_low(part_near[1], part_beside[1])
    part_far = flip_one(after(part_far, d_heads1), "y")
    up_sum = add_low(up_near, after(up_beside, d_resid1_low))

    tops_row, rest = [], tops_own
    for _ in range(3):
        tops_row.append(lax.reduce_precision(rest, 8, 7))
        rest = rest - tops_row[-1]
    tops_row = lax.dynamic_update_slice_in_dim(
        jnp.zeros((lanes,), F32), jnp.concatenate(tops_row), (levels_index * 2 + x) * 12, 0
    )[None]

    d_heads0, d_heads1 = after_all((d_heads0, d_heads1), down_sum, up_sum)
    mixed0, near_grad0, beside_grad0, bias_sum0 = heads_back(
        heads_where, d_heads0, saved0, cosine, sine, normed1, levels, seq, head_size
    )
    beside_grad0 = flip_one(beside_grad0, "x")
    out_sum = add_low(out_near, out_beside)
    out_sum = add_low(out_sum[0], flip_one(out_sum[1], "y"))

    last, last_beside, near_grad1, beside_grad1 = heads_back(
        heads_where, after(d_heads1, grad_down, out_sum), saved1, cosine, sine, normed1, levels,
        seq, head_size, (near1, beside1, near0, beside0), mixed0, unit1,
        (sums2, up_sums, tops_row, bias_sum0),
    )
    last_beside = flip_one(last_beside, "core")
    beside_grad1 = flip_one(beside_grad1, "x")
    qkv_sum0 = over_z(add_low(near_grad0, beside_grad0))
    up_sum = lax.psum_scatter(up_sum, "z", scatter_dimension=0, tiled=True)
    up_sum = up_sum.reshape(rows, fsdp * share)
    out_sum = add_low(out_sum[0], flip_one(out_sum[1], "x"))
    grad_out = lax.psum_scatter(out_sum, "z", scatter_dimension=0, tiled=True)
    grad_out = grad_out.reshape(-1, width).astype(F32)

    near_blocks = add_low(last, last_beside)
    d_normed1 = near_blocks[0].astype(F32) + flip_one(near_blocks[1], "y").astype(F32)
    qkv_sum1 = over_z(add_low(near_grad1, beside_grad1))
    block_out = resid1 + part_near[0] + part_beside[0].astype(F32) + part_far.astype(F32)
    block_out = (block_out + proj_bias[1]).astype(BF)
    unit, inverse = normalise(x_own.astype(F32))
    d_unit1 = d_normed1.reshape(clips * tokens, width) * norm_gains[0]
    grad_input = (d_resid1 + norm_back(unit, inverse, d_unit1)).reshape(block_input.shape)
    qkv_sum0 = jnp.sum(qkv_sum0.astype(F32), axis=0)
    qkv_sum1 = jnp.sum(qkv_sum1.astype(F32), axis=0)
    vectors = qkv_sum1[3 * lanes :]
    qkv_sums = [q[: 3 * lanes].T for q in (qkv_sum0, qkv_sum1)]

    one = rows // seq
    best = vectors[VECTOR_ROWS - 1, : fsdp * 12].reshape(fsdp, 3, 4)
    best = jnp.max(best[:, 0] + best[:, 1] + best[:, 2], axis=0)
    short = [
        jnp.swapaxes(vectors[:6].reshape(6, seq, one), 0, 1).reshape(seq, 6 * one),
        vectors[6:9].reshape(seq, 3 * one),
        vectors[9 : 9 + seq],
        jnp.tile(best[None], (seq, 1)),
    ]
    short = jnp.concatenate(short, axis=1)
    size = short.shape[1]
    short = jnp.pad(short, ((0, 0), (0, 3 * group - size)))

    own_rows = jnp.stack([q.reshape(seq, one, 3, lanes) for q in qkv_sums], axis=3)
    own_rows = jnp.concatenate([own_rows.reshape(seq, one, 3 * group), short[:, None]], axis=1)
    up_sum = up_sum.reshape(seq, one, fsdp * share)
    up_rows = lax.all_to_all(up_sum, SEQ, 0, 0, tiled=True)
    own_rows = lax.all_to_all(own_rows, SEQ, 0, 0, tiled=True)
    grad_qkv = own_rows[:, :one].reshape(seq, one, 3, group)
    grad_qkv = jnp.transpose(grad_qkv, (1, 2, 0, 3)).reshape(one, 3 * width)
    short = own_rows[:, one, :size]
    maxima = short[:, size - HEADS // seq :].reshape(HEADS)
    sums = jnp.sum(short, axis=0)
    grad_gains = sums[: 2 * one].reshape(2, one)
    grad_shifts = sums[2 * one : 4 * one].reshape(2, one)
    grad_proj_bias = sums[4 * one : 6 * one].reshape(2, one)
    grad_qkv_bias = sums[6 * one : 9 * one]
    grad_up_bias = sums[9 * one : 9 * one + share]

    up_rows = up_rows.reshape(seq, one, fsdp, share)
    grad_up = jnp.transpose(up_rows, (1, 2, 0, 3)).reshape(one, hidden).astype(F32)

    threshold = clip_threshold[0]
    gamma = jnp.sqrt(threshold / jnp.maximum(maxima, threshold))
    scales = jnp.tile(jnp.repeat(gamma, head_size), 2)
    clipped = w_qkv[:, : 2 * width].astype(F32) * scales
    clipped_bias = qkv_bias[: 2 * width] * scales
    return (
        block_out.reshape(block_input.shape),
        grad_input,
        grad_qkv,
        grad_out,
        grad_up,
        grad_down,
        grad_gains,
        grad_shifts,
        grad_qkv_bias,
        grad_proj_bias,
        grad_up_bias,
        maxima,
        clipped,
        clipped_bias,
    )


def on_device(block_input, *rest):
    fsdp, seq = axis_size(FSDP), axis_size(SEQ)
    width, hidden = block_input.shape[2], rest[-2].shape[0]
    square = seq == 4 and fsdp % 4 == 0 and fsdp <= 8 and width == 256 * seq and hidden % (128 * fsdp * seq) == 0
    square = square and width % (128 * fsdp) == 0
    return (square_device if square else general_device)(block_input, *rest)


def solution(mesh):
    fsdp, seq = mesh.shape["fsdp"], mesh.shape["seq"]
    fine = Mesh(mesh.devices.reshape(fsdp // 2, 2, seq // 2, 2), FSDP + SEQ)
    in_specs = (
        P(FSDP, SEQ, None),
        P(FSDP, SEQ, None),
        P(None, FSDP, SEQ),
        P(FSDP, None),
        P(FSDP, None),
        P(FSDP, None),
        P(FSDP, None),
        P(),
        P(),
        P(),
        P(),
        P(),
        P(),
    )
    out_specs = (
        P(FSDP, SEQ, None),
        P(FSDP, SEQ, None),
        P(FSDP + SEQ, None),
        P(FSDP + SEQ, None),
        P(FSDP + SEQ, None),
        P(FSDP + SEQ, None),
        P(None, FSDP + SEQ),
        P(None, FSDP + SEQ),
        P(FSDP + SEQ),
        P(None, FSDP + SEQ),
        P(FSDP + SEQ),
        P(),
        P(FSDP, None),
        P(),
    )
    return jax.shard_map(
        on_device, mesh=fine, in_specs=in_specs, out_specs=out_specs, check_vma=False
    )
```

```python
import functools

import jax
import jax.numpy as jnp
import numpy as np
from jax import lax
from jax.experimental import pallas as pl
from jax.experimental.pallas import tpu as pltpu
from jax.sharding import Mesh
from jax.sharding import PartitionSpec as P

HEADS = 16
EPSILON = 1e-06
ROPE_BASE = 100.0
GRID_SIDE = 16

FSDP = ("z", "x")
SEQ = ("y", "core")

BF = jnp.bfloat16
F32 = jnp.float32
NN = (((1,), (0,)), ((), ()))
NT = (((1,), (1,)), ((), ()))
TN = (((0,), (0,)), ((), ()))


def dot(left, right, dims):
    return lax.dot_general(left, right, dims, preferred_element_type=F32)


def params(megabytes=62):
    return pltpu.CompilerParams(vmem_limit_bytes=megabytes << 20)


def axis_size(names):
    size = 1
    for name in names:
        size *= lax.axis_size(name)
    return size


def flip(value, axis, mask):
    size = axis_size(axis)
    return lax.ppermute(value, axis, [(i, i ^ mask) for i in range(size)])


def dim_of(name):
    inner = 2
    if name == "x":
        return FSDP, 1, inner
    if name == "z":
        return FSDP, inner, axis_size(FSDP) // inner
    if name == "core":
        return SEQ, 1, inner
    return SEQ, inner, axis_size(SEQ) // inner


def gather_dim(value, name, axis):
    mesh_axis, stride, size = dim_of(name)
    parts = [value] + [flip(value, mesh_axis, k * stride) for k in range(1, size)]
    return jnp.stack(parts, axis)


def scatter_dim(value, name, axis, last):
    mesh_axis, stride, size = dim_of(name)
    total = lax.index_in_dim(value, 0, axis, keepdims=False).astype(F32)
    for k in range(1, size):
        part = lax.index_in_dim(value, k, axis, keepdims=False)
        total = total + flip(part, mesh_axis, k * stride).astype(F32)
    return total if last else total.astype(BF)


def copy_kernel(source, target):
    target[...] = source[...].reshape(target.shape)


def gather_order_kernel(pieces, shift, *refs):
    sources, target = refs[:-1], refs[-1]
    width = target.shape[1] // (len(sources) * pieces)
    for o, source in enumerate(sources):
        for y in range(pieces):
            first = (o * pieces + y) * width
            target[:, first : first + width] = source[0, y ^ shift[1]]


def weights_in_order(parts, fsdp_index, y_index):
    count, pieces, rows, width = parts[0].shape
    total = len(parts) * pieces * width
    where = jnp.stack([fsdp_index, y_index]).astype(jnp.int32)

    def body(shift, *refs):
        gather_order_kernel(pieces, shift, *refs)

    return pl.pallas_call(
        body,
        grid_spec=pltpu.PrefetchScalarGridSpec(
            num_scalar_prefetch=1,
            grid=(count,),
            in_specs=[
                pl.BlockSpec((1, pieces, rows, width), lambda j, s: (j ^ s[0], 0, 0, 0))
                for _ in parts
            ],
            out_specs=pl.BlockSpec((rows, total), lambda j, s: (j, 0)),
        ),
        out_shape=jax.ShapeDtypeStruct((count * rows, total), parts[0].dtype),
        compiler_params=params(),
    )(where, *parts)


def rows_by_distance(value, orders, pieces, fsdp_index, y_index):
    count = axis_size(FSDP)
    rows, width = value.shape[0] // (count * pieces), value.shape[1]
    share = width // orders
    if rows % 16:
        view = value.reshape(count, pieces, rows, orders, share)
        view = jnp.take(view, jnp.arange(count) ^ fsdp_index, axis=0)
        view = jnp.take(view, jnp.arange(pieces) ^ y_index, axis=1)
        return [view[:, :, :, o] for o in range(orders)]
    where = jnp.stack([fsdp_index, y_index]).astype(jnp.int32)

    def body(shift, source, *targets):
        for o, target in enumerate(targets):
            target[0, 0] = source[:, o * share : (o + 1) * share]

    return pl.pallas_call(
        body,
        grid_spec=pltpu.PrefetchScalarGridSpec(
            num_scalar_prefetch=1,
            grid=(count, pieces),
            in_specs=[
                pl.BlockSpec(
                    (rows, width),
                    lambda j, y, s: ((j ^ s[0]) * pieces + (y ^ s[1]), 0),
                )
            ],
            out_specs=[
                pl.BlockSpec((1, 1, rows, share), lambda j, y, s: (j, y, 0, 0))
            ]
            * orders,
        ),
        out_shape=[
            jax.ShapeDtypeStruct((count, pieces, rows, share), value.dtype)
        ]
        * orders,
        compiler_params=params(),
    )(where, value)


def columns_in_order(value, shift):
    count, rows, width = value.shape
    if width % 128:
        ordered = jnp.take(value, jnp.arange(count) ^ shift, axis=0)
        return jnp.moveaxis(ordered, 0, 1).reshape(rows, count * width)
    return pl.pallas_call(
        lambda s, source, target: copy_kernel(source, target),
        grid_spec=pltpu.PrefetchScalarGridSpec(
            num_scalar_prefetch=1,
            grid=(count,),
            in_specs=[pl.BlockSpec((1, rows, width), lambda j, s: (j ^ s[0], 0, 0))],
            out_specs=pl.BlockSpec((rows, width), lambda j, s: (0, j)),
        ),
        out_shape=jax.ShapeDtypeStruct((rows, count * width), value.dtype),
        compiler_params=params(),
    )(shift.reshape(1).astype(jnp.int32), value)


def columns_by_distance(value, count, shift):
    rows, width = value.shape[0], value.shape[1] // count
    if width % 128:
        blocks = jnp.moveaxis(value.reshape(rows, count, width), 1, 0)
        return jnp.take(blocks, jnp.arange(count) ^ shift, axis=0)
    return pl.pallas_call(
        lambda s, source, target: copy_kernel(source, target),
        grid_spec=pltpu.PrefetchScalarGridSpec(
            num_scalar_prefetch=1,
            grid=(count,),
            in_specs=[pl.BlockSpec((rows, width), lambda j, s: (0, j ^ s[0]))],
            out_specs=pl.BlockSpec((1, rows, width), lambda j, s: (j, 0, 0)),
        ),
        out_shape=jax.ShapeDtypeStruct((count, rows, width), value.dtype),
        compiler_params=params(),
    )(shift.reshape(1).astype(jnp.int32), value)


def keep_head(value, head, head_size):
    lane = lax.broadcasted_iota(jnp.int32, (1, value.shape[1]), 1)
    return jnp.where(lane // head_size == head, value, jnp.zeros_like(value))


def attend_kernel(head_size, chunk, query, keys, values, out, tops, inverses):
    length, width = keys.shape
    scale = jnp.asarray(head_size**-0.5, BF)
    for h in range(width // head_size):
        own_keys = keep_head(keys[...], h, head_size) * scale
        own_values = keep_head(values[...], h, head_size)
        for i in range(length // chunk):
            rows = pl.ds(i * chunk, chunk)
            scores = dot(own_keys, query[rows, :], NT)
            top = jnp.max(scores, axis=0, keepdims=True)
            exponent = jnp.exp(scores - top)
            inverse = 1.0 / jnp.sum(exponent, axis=0, keepdims=True)
            part = dot((exponent * inverse).astype(BF), own_values, TN)
            if h == 0:
                out[rows, :] = part.astype(BF)
            else:
                out[rows, :] = (out[rows, :].astype(F32) + part).astype(BF)
            tops[0, h : h + 1, rows] = top
            inverses[0, h : h + 1, rows] = inverse


def attend(query, keys, values, head_size):
    length, width = query.shape
    block = min(128, width)
    wide = pl.BlockSpec((length, block), lambda h: (0, h))
    flat = pl.BlockSpec((1, block // head_size, length), lambda h: (h, 0, 0))
    stats = jax.ShapeDtypeStruct((width // block, block // head_size, length), F32)
    return pl.pallas_call(
        functools.partial(attend_kernel, head_size, min(512, length)),
        grid=(width // block,),
        in_specs=[wide] * 3,
        out_specs=[wide, flat, flat],
        out_shape=[jax.ShapeDtypeStruct((length, width), BF), stats, stats],
        compiler_params=params(),
    )(query, keys, values)


def attend_back_kernel(
    head_size, chunk, query, keys, values, grad, tops, inverses, d_query, d_keys, d_values
):
    length, width = keys.shape
    scale = jnp.asarray(head_size**-0.5, BF)
    for h in range(width // head_size):
        own_keys = keep_head(keys[...], h, head_size) * scale
        own_values = keep_head(values[...], h, head_size)
        for i in range(length // chunk):
            rows = pl.ds(i * chunk, chunk)
            query_rows, grad_rows = query[rows, :], grad[rows, :]
            scores = dot(own_keys, query_rows, NT)
            probs = jnp.exp(scores - tops[0, h : h + 1, rows]) * inverses[0, h : h + 1, rows]
            d_probs = dot(own_values, grad_rows, NT)
            delta = jnp.sum(probs * d_probs, axis=0, keepdims=True)
            d_scores = (probs * (d_probs - delta)).astype(BF)
            value_part = dot(probs.astype(BF), keep_head(grad_rows, h, head_size), NN)
            key_part = dot(d_scores, keep_head(query_rows, h, head_size) * scale, NN)
            query_part = dot(d_scores, own_keys, TN)
            if h == 0 and i == 0:
                d_values[...] = value_part
                d_keys[...] = key_part
            else:
                d_values[...] += value_part
                d_keys[...] += key_part
            if h == 0:
                d_query[rows, :] = query_part
            else:
                d_query[rows, :] += query_part


def attend_back(query, keys, values, grad, tops, inverses, head_size):
    length, width = query.shape
    block = min(128, width)
    wide = pl.BlockSpec((length, block), lambda h: (0, h))
    flat = pl.BlockSpec((1, block // head_size, length), lambda h: (h, 0, 0))
    return pl.pallas_call(
        functools.partial(attend_back_kernel, head_size, min(512, length)),
        grid=(width // block,),
        in_specs=[wide] * 4 + [flat] * 2,
        out_specs=[wide] * 3,
        out_shape=[jax.ShapeDtypeStruct((length, width), F32)] * 3,
        compiler_params=params(),
    )(query, keys, values, grad, tops, inverses)


def rotary_table(head_size):
    half = head_size // 2
    pair = np.arange(half)
    bands = (half + 2) // 3
    frequency = np.power(np.float32(ROPE_BASE), -(pair // 3).astype(np.float32) / bands)
    angles = np.arange(GRID_SIDE, dtype=np.float32)[:, None] * frequency[None, :]
    chosen = (pair % 3)[None, None, :] == np.arange(3)[:, None, None]

    def table(of):
        return np.where(chosen, of[None], 0.0).reshape(3 * GRID_SIDE, half)

    cosine, sine = table(np.cos(angles)), table(np.sin(angles))
    return np.concatenate([cosine, cosine, -sine, sine], axis=1).astype(np.float32)


def rotary_rows(coords, head_size):
    cells = jnp.arange(GRID_SIDE)
    hot = (coords[:, :, None] == cells).astype(F32)
    hot = jnp.transpose(hot, (1, 0, 2)).reshape(coords.shape[1], 3 * GRID_SIDE)
    both = jnp.dot(hot, rotary_table(head_size), precision=lax.Precision.HIGHEST)
    return both[:, :head_size], both[:, head_size:]


def half_swap(values, head_size):
    length, width = values.shape
    halves = values.reshape(length, width // head_size, 2, head_size // 2)
    return halves[:, :, ::-1, :].reshape(length, width)


def turn(values, cosine, sine, head_size):
    repeats = values.shape[1] // head_size
    return values * jnp.tile(cosine, (1, repeats)) + half_swap(values, head_size) * jnp.tile(
        sine, (1, repeats)
    )


def normalise(values):
    row_mean = jnp.mean(values, axis=-1, keepdims=True)
    centred = values - row_mean
    row_var = jnp.mean(centred * centred, axis=-1, keepdims=True)
    inverse = lax.rsqrt(row_var + EPSILON)
    return centred * inverse, inverse


def norm_back(unit, inverse, d_unit):
    return inverse * (
        d_unit
        - jnp.mean(d_unit, axis=-1, keepdims=True)
        - unit * jnp.mean(d_unit * unit, axis=-1, keepdims=True)
    )


def gelu_exact(values_in):
    return jax.nn.gelu(values_in, approximate=False)


def general_device(
    block_input,
    out_cotangent,
    positions,
    w_qkv,
    w_out,
    w_up,
    w_down,
    norm_gains,
    norm_shifts,
    qkv_bias,
    proj_bias,
    up_bias,
    clip_threshold,
):
    clips, tokens, width = block_input.shape
    fsdp, seq = axis_size(FSDP), axis_size(SEQ)
    outer = seq // 2
    head_size = width // HEADS
    group = width // seq
    hidden = up_bias.shape[0]
    share = hidden // (fsdp * seq)
    length = tokens * seq
    f = lax.axis_index(FSDP)
    s = lax.axis_index(SEQ)
    y, c = s // 2, s % 2

    def along_seq(value):
        rows = gather_dim(value, "y", 0)
        return gather_dim(rows, "core", 1).reshape((seq,) + value.shape)

    x_all = [along_seq(block_input[i]).reshape(length, width) for i in range(clips)]
    coords_all = jnp.moveaxis(along_seq(positions), 0, 2).reshape(3, clips, length)

    own_heads = lax.dynamic_index_in_dim(
        w_qkv.reshape(-1, 3, seq, group), s, 2, keepdims=False
    ).reshape(-1, 3 * group)
    halves = []
    for o, order in enumerate(("zx", "xz")):
        piece = own_heads[:, o * (3 * group // 2) : (o + 1) * (3 * group // 2)]
        shape = (fsdp, 1) + piece.shape
        if order == "zx":
            piece = gather_dim(gather_dim(piece, "z", 0), "x", 1)
        else:
            piece = gather_dim(gather_dim(piece, "x", 0), "z", 0)
        halves.append(piece.reshape(shape))
    full_qkv = weights_in_order(halves, f, jnp.zeros_like(f))

    def gathered(local):
        rows, columns = local.shape
        part = columns // (2 * outer)
        views = local.reshape(rows, 2, outer, part)
        parts = []
        for o, order in enumerate(("zxy", "zyx")):
            piece = lax.dynamic_index_in_dim(views[:, o], y, 1, keepdims=False)
            piece = gather_dim(piece, "z", 0)
            if order == "zxy":
                piece = gather_dim(gather_dim(piece, "x", 1), "y", 2)
            else:
                piece = gather_dim(gather_dim(piece, "y", 1), "x", 1)
            parts.append(piece.reshape(fsdp, outer, rows, part))
        return weights_in_order(parts, f, y)

    def summed(partial):
        parts = rows_by_distance(partial, 2, outer, f, y)
        sums = []
        for order, part in zip(("yxz", "xyz"), parts, strict=True):
            value = part.reshape((fsdp // 2, 2) + part.shape[1:])
            if order == "yxz":
                value = scatter_dim(scatter_dim(value, "y", 2, False), "x", 1, False)
            else:
                value = scatter_dim(scatter_dim(value, "x", 1, False), "y", 1, False)
            sums.append(scatter_dim(value, "z", 0, True))
        return jnp.concatenate(sums, axis=1)

    def core_part(value, axis):
        shape = value.shape
        view = value.reshape(shape[:axis] + (-1, 2, share) + shape[axis + 1 :])
        view = lax.dynamic_index_in_dim(view, c, axis + 1, keepdims=False)
        return view.reshape(shape[:axis] + (shape[axis] // 2,) + shape[axis + 1 :])

    full_out = gathered(w_out)
    full_up = gathered(core_part(w_up, 1))
    full_down = gathered(core_part(w_down, 0))
    own_up_bias = core_part(up_bias, 0)

    own_bias = lax.dynamic_index_in_dim(qkv_bias.reshape(3, seq, group), s, 1, keepdims=False)
    kept = []
    attended_parts = []
    for i in range(clips):
        unit, inverse = normalise(x_all[i].astype(F32))
        normed = (unit * norm_gains[0] + norm_shifts[0]).astype(BF)
        mixed = dot(normed, full_qkv, NN) + own_bias.reshape(-1)
        cosine, sine = rotary_rows(coords_all[:, i], head_size)
        query = turn(mixed[:, :group], cosine, sine, head_size).astype(BF)
        keys = turn(mixed[:, group : 2 * group], cosine, sine, head_size).astype(BF)
        values = mixed[:, 2 * group :].astype(BF)
        attended, tops, inverses = attend(query, keys, values, head_size)
        kept.append((normed, query, keys, values, tops, inverses, cosine, sine))
        blocks = attended.reshape(seq, tokens, group)
        attended_parts.append(
            jnp.stack([blocks[0]] + [flip(blocks[m], SEQ, m) for m in range(1, seq)])
        )
    attended_own = columns_in_order(
        jnp.concatenate(attended_parts, axis=1), s
    )
    tops_own = functools.reduce(
        jnp.maximum, [jnp.max(k[4], axis=2).reshape(-1) for k in kept]
    )

    x_own = block_input.reshape(clips * tokens, width).astype(F32)
    g_own = out_cotangent.reshape(clips * tokens, width)
    resid1 = x_own + dot(attended_own, full_out, NN) + proj_bias[0]
    unit2, inverse2 = normalise(resid1)
    normed2 = (unit2 * norm_gains[1] + norm_shifts[1]).astype(BF)

    def pair(value):
        return jnp.concatenate([value, flip(value, SEQ, 1)], axis=0)

    def pair_sum(value):
        half = value.shape[0] // 2
        return value[:half] + flip(value[half:], SEQ, 1)

    normed2_chip = pair(normed2)
    g_chip = pair(g_own)
    hidden_pre = dot(normed2_chip, full_up, NN) + own_up_bias
    activated, gelu_pull = jax.vjp(gelu_exact, hidden_pre)
    activated = activated.astype(BF)
    block_out = (resid1 + pair_sum(dot(activated, full_down, NN)) + proj_bias[1]).astype(BF)

    grad_down = summed(dot(activated, g_chip, TN).astype(BF))
    d_hidden = gelu_pull(dot(g_chip, full_down, NT))[0].astype(BF)
    grad_up_half = summed(dot(normed2_chip, d_hidden, TN).astype(BF))
    up_bias_part = jnp.sum(d_hidden.astype(F32), axis=0)
    d_normed2 = pair_sum(dot(d_hidden, full_up, NT))
    gain2_part = jnp.sum(d_normed2 * unit2, axis=0)
    shift2_part = jnp.sum(d_normed2, axis=0)
    g_wide = g_own.astype(F32)
    down_bias_part = jnp.sum(g_wide, axis=0)
    d_resid1 = g_wide + norm_back(unit2, inverse2, d_normed2 * norm_gains[1])
    d_resid1_low = d_resid1.astype(BF)
    out_bias_part = jnp.sum(d_resid1_low.astype(F32), axis=0)

    d_attended = dot(d_resid1_low, full_out, NT).astype(BF)
    pieces = columns_by_distance(d_attended, seq, s).reshape(seq, clips, tokens, group)

    out_rows = dot(attended_own, d_resid1_low, TN).astype(BF)
    out_rows = out_rows.reshape(-1, 2, width // (fsdp * seq), width)
    mine = lax.dynamic_index_in_dim(out_rows, c, 1, keepdims=False)
    theirs = lax.dynamic_index_in_dim(out_rows, 1 - c, 1, keepdims=False)
    out_rows = (mine.astype(F32) + flip(theirs, SEQ, 1).astype(F32)).astype(BF)
    grad_out = summed(out_rows.reshape(-1, width))

    d_normed1_parts = []
    qkv_part = 0.0
    qkv_bias_part = 0.0
    gain1_part = 0.0
    shift1_part = 0.0
    for i in range(clips):
        normed, query, keys, values, tops, inverses, cosine, sine = kept[i]
        grad = jnp.concatenate(
            [pieces[0, i]] + [flip(pieces[m, i], SEQ, m) for m in range(1, seq)], axis=0
        )
        d_query, d_keys, d_values = attend_back(
            query, keys, values, grad, tops, inverses, head_size
        )
        d_mixed = jnp.concatenate(
            [
                turn(d_query, cosine, -sine, head_size),
                turn(d_keys, cosine, -sine, head_size),
                d_values,
            ],
            axis=1,
        ).astype(BF)
        qkv_part = qkv_part + dot(normed, d_mixed, TN)
        qkv_bias_part = qkv_bias_part + jnp.sum(d_mixed.astype(F32), axis=0)
        d_normed1 = dot(d_mixed, full_qkv, NT)
        unit, _ = normalise(x_all[i].astype(F32))
        gain1_part = gain1_part + jnp.sum(d_normed1 * unit, axis=0)
        shift1_part = shift1_part + jnp.sum(d_normed1, axis=0)
        d_normed1_parts.append(d_normed1.astype(BF))

    blocks = rows_by_distance(qkv_part.astype(BF), 2, 1, f, jnp.zeros_like(f))
    sums = []
    for order, part in zip(("xz", "zx"), blocks, strict=True):
        value = part.reshape((fsdp // 2, 2) + part.shape[2:])
        if order == "xz":
            value = scatter_dim(scatter_dim(value, "x", 1, False), "z", 0, True)
        else:
            value = scatter_dim(scatter_dim(value, "z", 0, False), "x", 0, True)
        sums.append(value)
    own_rows = jnp.concatenate(sums, axis=1).reshape(seq, -1, 3 * group)

    def rows_of(m):
        return lax.dynamic_index_in_dim(own_rows, s ^ m, 0, keepdims=False)

    arrived = jnp.stack([rows_of(0)] + [flip(rows_of(m), SEQ, m) for m in range(1, seq)])
    ordered = [
        lax.dynamic_index_in_dim(arrived, s ^ t, 0, keepdims=False).reshape(-1, 3, 1, group)
        for t in range(seq)
    ]
    grad_qkv = jnp.concatenate(ordered, axis=2).reshape(-1, 3 * width)

    halves = grad_up_half.reshape(2, -1, fsdp * outer, share)
    mine = lax.dynamic_index_in_dim(halves, c, 0, keepdims=False)
    other = flip(lax.dynamic_index_in_dim(halves, 1 - c, 0, keepdims=False), SEQ, 1)
    first = jnp.where(c == 0, mine, other)
    second = jnp.where(c == 0, other, mine)
    grad_up = jnp.stack([first, second], axis=2).reshape(-1, hidden)

    d_normed1 = jnp.stack([p.reshape(seq, tokens, width) for p in d_normed1_parts], axis=1)
    value = d_normed1.reshape((outer, 2) + d_normed1.shape[1:])
    value = scatter_dim(scatter_dim(value, "core", 1, False), "y", 0, True)
    unit1, inverse1 = normalise(x_own)
    d_unit1 = value.reshape(clips * tokens, width) * norm_gains[0]
    grad_input = (d_resid1 + norm_back(unit1, inverse1, d_unit1)).reshape(block_input.shape)

    qkv_slots = lax.dynamic_update_index_in_dim(
        jnp.zeros((3, seq, group), F32), qkv_bias_part.reshape(3, group), s, 1
    )
    up_slots = lax.dynamic_update_index_in_dim(
        jnp.zeros((fsdp * outer, 2, share), F32),
        up_bias_part.reshape(fsdp * outer, share),
        c,
        1,
    )
    devices = fsdp * seq
    rows = [
        gain1_part, gain2_part, shift1_part, shift2_part, out_bias_part, down_bias_part,
        qkv_slots.reshape(-1), up_slots.reshape(-1),
    ]
    rows = jnp.concatenate([r.reshape(devices, -1) for r in rows], axis=1)
    sums = lax.psum_scatter(rows, FSDP + SEQ, scatter_dimension=0, tiled=True)[0]
    one = width // devices
    grad_gains = sums[: 2 * one].reshape(2, one)
    grad_shifts = sums[2 * one : 4 * one].reshape(2, one)
    grad_proj_bias = sums[4 * one : 6 * one].reshape(2, one)
    grad_qkv_bias = sums[6 * one : 9 * one]
    grad_up_bias = sums[9 * one :]

    slots = jnp.full((seq, HEADS // seq), -jnp.inf, F32)
    slots = lax.dynamic_update_index_in_dim(slots, tops_own, s, 0)
    maxima = lax.pmax(slots.reshape(-1), FSDP + SEQ)
    threshold = clip_threshold[0]
    gamma = jnp.sqrt(threshold / jnp.maximum(maxima, threshold))
    columns = jnp.tile(jnp.repeat(gamma, head_size), 2)
    clipped = w_qkv[:, : 2 * width].astype(F32) * columns
    clipped_bias = qkv_bias[: 2 * width] * columns
    return (
        block_out.reshape(block_input.shape),
        grad_input,
        grad_qkv,
        grad_out,
        grad_up,
        grad_down,
        grad_gains,
        grad_shifts,
        grad_qkv_bias,
        grad_proj_bias,
        grad_up_bias,
        maxima,
        clipped,
        clipped_bias,
    )


def flip_one(value, name):
    return lax.ppermute(value, name, [(0, 1), (1, 0)])


def after(value, *others):
    return lax.optimization_barrier((value, *others))[0]


def after_all(values, *others):
    return lax.optimization_barrier((tuple(values), *others))[0]


def add_low(*terms):
    return functools.reduce(jnp.add, [t.astype(F32) for t in terms]).astype(BF)


def cost(microseconds):
    return pl.CostEstimate(
        flops=int(microseconds * 1e3), bytes_accessed=1 << 10, transcendentals=0
    )


def whole(shape):
    return pl.BlockSpec(shape, lambda *_: (0,) * len(shape))


def in_order(index, bit, axis):
    return jnp.where(bit == 0, index, jnp.flip(index, axis))


def swap_halves(values, head_size):
    half = head_size // 2
    lane = lax.broadcasted_iota(jnp.int32, (1, values.shape[1]), 1)
    width = values.shape[1]
    return jnp.where(
        lane % head_size < half,
        pltpu.roll(values, width - half, 1),
        pltpu.roll(values, half, 1),
    )


def first_norm_kernel(first, second, gain, shift, normed, unit):
    tokens = first.shape[0]
    for i, part in enumerate((first, second)):
        value, _ = normalise(part[...].astype(F32))
        here = slice(i * tokens, (i + 1) * tokens)
        unit[0, here, :] = value.astype(BF)
        normed[0, here, :] = (value * gain[...] + shift[...]).astype(BF)


def first_norm(first, second, gain, shift, clips):
    width = first.shape[1]
    tokens = first.shape[0] // (8 * clips) * 8
    block = pl.BlockSpec((tokens, width), lambda i: (i, 0))
    out = pl.BlockSpec((1, 2 * tokens, width), lambda i: (i, 0, 0))
    return pl.pallas_call(
        first_norm_kernel,
        grid=(clips,),
        in_specs=[block, block, whole((1, width)), whole((1, width))],
        out_specs=[out, out],
        out_shape=[jax.ShapeDtypeStruct((clips, 2 * tokens, width), BF)] * 2,
        compiler_params=params(),
        cost_estimate=cost(4),
        name="first_norm",
    )(first, second, gain, shift)


def own_columns(where, value, count, share):
    rows = value.shape[0]
    return pl.pallas_call(
        lambda w, source, target: copy_kernel(source, target),
        grid_spec=pltpu.PrefetchScalarGridSpec(
            num_scalar_prefetch=1,
            grid=(count,),
            in_specs=[
                pl.BlockSpec((rows, share), lambda k, w: (0, (k * 2 + w[1]) * 2 + w[2]))
            ],
            out_specs=pl.BlockSpec((rows, share), lambda k, w: (0, k)),
        ),
        out_shape=jax.ShapeDtypeStruct((rows, count * share), value.dtype),
        compiler_params=params(),
        cost_estimate=cost(3),
        name="own_columns",
    )(where, value)


def rotary_parts(head_size, lanes):
    half = 2 * head_size // 2
    table = rotary_table(head_size)
    repeats = lanes // head_size
    table = np.concatenate([np.tile(table[:, :half], (1, repeats)), np.tile(table[:, half:], (1, repeats))], axis=1)
    parts = []
    for _ in range(3):
        parts.append(table.astype(BF))
        table = table - parts[-1].astype(np.float32)
    return np.concatenate(parts, axis=1)


def spots_of(clip, clips, spots, tokens):
    lines = []
    for part in spots:
        width = part.shape[1]
        line = []
        for a in range(3):
            first = a * clips * tokens
            column = first % width + clip * tokens
            row = first // width
            line.append(part[row : row + 1, pl.ds(pl.multiple_of(column, tokens), tokens)])
        lines.append(jnp.concatenate(line, axis=0))
    return jnp.concatenate(lines, axis=1).astype(F32)


def rotary_of(coords, table):
    cells = lax.broadcasted_iota(jnp.int32, (GRID_SIDE, coords.shape[1]), 0).astype(F32)
    hot = [(coords[a : a + 1] == cells).astype(F32) for a in range(3)]
    hot = jnp.concatenate(hot, axis=0).astype(BF)
    width = table.shape[1] // 3
    both = sum(dot(hot, table[:, k * width : (k + 1) * width], TN) for k in range(3))
    return both[:, : width // 2], both[:, width // 2 :]


def heads_forward_kernel(
    head_size, blocks, where, first_rows, last_rows, near, beside, bias, table, *refs
):
    spots, refs = refs[:blocks], refs[blocks:]
    query, keys, values, out, tops, inverses, weights = refs
    levels, rows, width = near.shape
    length, lanes = query.shape[1:]
    spots = spots_of(pl.program_id(0), pl.num_programs(0), spots, length // blocks)
    cosine, sine = rotary_of(spots, table)

    @pl.when(pl.program_id(0) == 0)
    def _():
        for z in range(levels):
            for part, bit in ((near, 0), (beside, 1)):
                first = (z * 2 + (where[0] ^ bit)) * rows
                weights[pl.ds(pl.multiple_of(first, rows), rows), :] = part[z]

    mixed = [dot(part[0], weights[...], NN) + bias[...] for part in (first_rows, last_rows)]
    mixed = jnp.concatenate(mixed, axis=0)
    turned = [
        part * cosine + swap_halves(part, head_size) * sine
        for part in (mixed[:, :lanes], mixed[:, lanes : 2 * lanes])
    ]
    query[0], keys[0] = turned[0].astype(BF), turned[1].astype(BF)
    values[0] = mixed[:, 2 * lanes :].astype(BF)
    scale = jnp.asarray(head_size**-0.5, BF)
    chunk = length // 2
    tokens = length // blocks
    for i in range(2):
        rows_here = pl.ds(i * chunk, chunk)
        query_rows = query[0, rows_here, :]
        total = None
        for h in range(lanes // head_size):
            own_keys = keep_head(keys[0], h, head_size) * scale
            own_values = keep_head(values[0], h, head_size)
            scores = dot(own_keys, query_rows, NT)
            top = jnp.max(scores, axis=0, keepdims=True)
            exponent = jnp.exp(scores - top)
            inverse = 1.0 / jnp.sum(exponent, axis=0, keepdims=True)
            part = dot((exponent * inverse).astype(BF), own_values, TN)
            total = part if total is None else total + part
            tops[0, h : h + 1, rows_here] = top
            inverses[0, h : h + 1, rows_here] = inverse
        low = total.astype(BF)
        for b in range(blocks // 2):
            out[i * (blocks // 2) + b, 0] = low[b * tokens : (b + 1) * tokens]


def spot_block(x):
    return pl.BlockSpec((8, x.shape[1]), lambda i, w: (x.shape[0] // 8 - 1, 0))


def heads_forward(where, normed, near, beside, bias, table, x_blocks, blocks, head_size):
    clips, half, width = normed[0].shape
    length = 2 * half
    lanes = bias.shape[1] // 3
    pieces = near.shape[:2] + bias.shape[1:]
    clip = lambda *rest: pl.BlockSpec((1,) + rest, lambda i, w: (i,) + (0,) * len(rest))
    head = jax.ShapeDtypeStruct((clips, length, lanes), BF)
    stats = jax.ShapeDtypeStruct((clips, lanes // head_size, length), F32)
    return pl.pallas_call(
        functools.partial(heads_forward_kernel, head_size, blocks),
        grid_spec=pltpu.PrefetchScalarGridSpec(
            num_scalar_prefetch=1,
            grid=(clips,),
            in_specs=[
                clip(half, width),
                clip(half, width),
                whole(pieces),
                whole(pieces),
                whole(bias.shape),
                whole(table.shape),
            ]
            + [spot_block(x) for x in x_blocks],
            out_specs=[clip(length, lanes)] * 3
            + [
                pl.BlockSpec(
                    (blocks, 1, length // blocks, lanes), lambda i, w: (0, i, 0, 0)
                )
            ]
            + [clip(lanes // head_size, length)] * 2,
            scratch_shapes=[pltpu.VMEM((width, 3 * lanes), BF)],
        ),
        out_shape=[
            head,
            head,
            head,
            jax.ShapeDtypeStruct((blocks, clips, length // blocks, lanes), BF),
            stats,
            stats,
        ],
        compiler_params=params(),
        cost_estimate=cost(15),
        name="heads_forward",
    )(where, *normed, near, beside, bias, table, *x_blocks)


def out_row(z, x, where, rows):
    index = z * 2 + x
    return ((((index // 2) ^ where[3]) * 2) + index % 2) * rows


def project_kernel(where, *refs, groups):
    pieces, refs = refs[: 4 * groups], refs[4 * groups :]
    x_blocks, refs = refs[:4], refs[4:]
    own, other, bias, gain, shift = refs[:5]
    resid, attended, normed, weights, joined = refs[5:]
    levels, rows, share = own.shape[1:]
    step = pl.program_id(0)

    @pl.when(step == 0)
    def _():
        for core, part in ((0, own), (1, other)):
            column = (where[2] ^ core) * share
            column = pl.ds(pl.multiple_of(column, share), share)
            for far_x in range(2):
                for z in range(levels):
                    place = out_row(z, where[0] ^ far_x, where, rows)
                    place = pl.ds(pl.multiple_of(place, rows), rows)
                    weights[place, column] = part[far_x, z]

    lanes = pieces[0].shape[3]
    for h in range(groups):
        for m in range(4):
            first = (m * groups + h) * lanes
            joined[:, first : first + lanes] = pieces[h * 4 + m][0, 0]
    for b in range(4):

        @pl.when(step // 2 == b)
        def _(b=b):
            out = x_blocks[b][...].astype(F32)
            out = out + dot(joined[...], weights[...], NN) + bias[...]
            unit, _ = normalise(out)
            normed[...] = (unit * gain[...] + shift[...]).astype(BF)
            if b == 0:
                resid[...] = out
                attended[...] = joined[...]


def project(where, pieces, x_blocks, own, other, bias, gain, shift):
    clips, tokens, lanes = pieces[0][0].shape[1:]
    rows, width = clips * tokens, x_blocks[0].shape[1]
    piece_specs = [
        pl.BlockSpec((1, 1, tokens, lanes), lambda t, w, m=m: ((t // 2) ^ m, t % 2, 0, 0))
        for _ in pieces
        for m in range(4)
    ]
    x_specs = [
        pl.BlockSpec((tokens, width), lambda t, w, b=b: (jnp.clip(t - 2 * b, 0, 1), 0))
        for b in range(4)
    ]
    first = pl.BlockSpec((tokens, width), lambda t, w: (jnp.minimum(t, 1), 0))
    return pl.pallas_call(
        functools.partial(project_kernel, groups=len(pieces)),
        grid_spec=pltpu.PrefetchScalarGridSpec(
            num_scalar_prefetch=1,
            grid=(4 * clips,),
            in_specs=piece_specs
            + x_specs
            + [whole(own.shape), whole(other.shape)]
            + [whole((1, width))] * 3,
            out_specs=[
                first,
                first,
                pl.BlockSpec((tokens, width), lambda t, w: (t, 0)),
                whole((width, width)),
            ],
            scratch_shapes=[pltpu.VMEM((tokens, width), BF)],
        ),
        out_shape=[
            jax.ShapeDtypeStruct((rows, width), F32),
            jax.ShapeDtypeStruct((rows, width), BF),
            jax.ShapeDtypeStruct((4 * rows, width), BF),
            jax.ShapeDtypeStruct((width, width), BF),
        ],
        compiler_params=params(),
        cost_estimate=cost(13),
        name="project_out",
    )(where, *(p for group in pieces for p in group), *x_blocks, own, other, bias, gain, shift)


def gelu_pair(values):
    cumulative = 0.5 * (1.0 + lax.erf(values * np.float32(0.5**0.5)))
    density = jnp.exp(-0.5 * values * values) * np.float32((2.0 * np.pi) ** -0.5)
    return values * cumulative, cumulative + values * density


def up_kernel(
    where, normed, near, beside, bias, *refs
):
    grads, refs = refs[:4], refs[4:]
    activated, slope, columns, near_out, beside_out, held, low, sems = refs
    levels, rows, block = near.shape
    share = block // 2
    step = pl.program_id(0)
    tokens = normed.shape[0] // 4
    copies = [
        pltpu.make_async_copy(g, held.at[pl.ds(i * tokens, tokens)], sems.at[i])
        for i, g in enumerate(grads)
    ]

    @pl.when(step == 0)
    def _():
        for one in copies:
            one.start()

    for z in range(levels):
        for far_x, part in enumerate((near, beside)):
            first = (z * 2 + (where[0] ^ far_x)) * rows
            columns[pl.ds(pl.multiple_of(first, rows), rows), :] = part[z]
    for i in range(4):
        here = slice(i * tokens, (i + 1) * tokens)
        hidden = dot(normed[here, :], columns[...], NN) + bias[0]
        act, d_act = gelu_pair(hidden)
        activated[here, :] = act.astype(BF)
        slope[here, :] = d_act.astype(BF)

    @pl.when(step == 0)
    def _():
        for one in copies:
            one.wait()

    low[...] = dot(activated[...], held[...], TN).astype(BF)
    for far_x, out in enumerate((near_out, beside_out)):
        first = (where[0] ^ far_x) * share
        out[0] = low[pl.ds(pl.multiple_of(first, share), share), :]


def feed_up(where, normed, grads, pieces, bias):
    levels, rows, hidden = pieces[1].shape
    tokens, width = normed.shape
    block = hidden // levels
    by_column = pl.BlockSpec((levels, rows, block), lambda t, w: (0, 0, t))
    line = pl.BlockSpec((tokens, block), lambda t, w: (0, t))
    out = pl.BlockSpec((1, block // 2, width), lambda t, w: (t, 0, 0))
    return pl.pallas_call(
        up_kernel,
        grid_spec=pltpu.PrefetchScalarGridSpec(
            num_scalar_prefetch=1,
            grid=(levels,),
            in_specs=[whole((tokens, width)), by_column, by_column]
            + [pl.BlockSpec((1, 1, block), lambda t, w: (t, 0, 0))]
            + [pl.BlockSpec(memory_space=pl.ANY)] * 4,
            out_specs=[line, line, pl.BlockSpec((width, block), lambda t, w: (0, t)), out, out],
            scratch_shapes=[
                pltpu.VMEM((tokens, width), BF),
                pltpu.VMEM((block, width), BF),
                pltpu.SemaphoreType.DMA((4,)),
            ],
        ),
        out_shape=[jax.ShapeDtypeStruct((tokens, hidden), BF)] * 2
        + [jax.ShapeDtypeStruct((width, hidden), BF)]
        + [jax.ShapeDtypeStruct((levels, block // 2, width), BF)] * 2,
        compiler_params=params(),
        cost_estimate=cost(17),
        name="feed_up",
    )(where, normed, *pieces, bias, *grads)


def far_kernel(
    where, first_grad, last_grad, near, beside, slope, columns,
    first_back, last_back, weights, d_hidden, hidden, up,
):
    step = pl.program_id(0)
    steps = pl.num_programs(0) - 2
    share = near.shape[1]
    block = 2 * share
    tokens = first_grad.shape[0]

    @pl.when(step < steps)
    def _():
        for far_x, part in enumerate((near, beside)):
            first = (where[0] ^ far_x) * share
            weights[pl.ds(pl.multiple_of(first, share), share), :] = part[0]
        place = pl.ds(pl.multiple_of(step * block, block), block)
        up[:, place] = columns[...]
        for i, grad in enumerate((first_grad, last_grad)):
            here = slice(i * tokens, (i + 1) * tokens)
            d_act = dot(grad[...], weights[...], NT)
            low = (d_act * slope[here, :].astype(F32)).astype(BF)
            hidden[here, place] = low
            d_hidden[here, :] = low

    @pl.when(step == steps)
    def _():
        first_back[...] = dot(hidden[:tokens, :], up[...], NT)

    @pl.when(step == steps + 1)
    def _():
        last_back[...] = dot(hidden[tokens:, :], up[...], NT).astype(BF)


def feed_down_far(where, grads, pieces, slope, columns):
    levels, share, width = pieces[0].shape
    tokens = grads[0].shape[0]
    block = 2 * share
    hidden = levels * block
    at = lambda t: jnp.minimum(t, levels - 1)
    piece = pl.BlockSpec((1, share, width), lambda t, w: (at(t), 0, 0))
    return pl.pallas_call(
        far_kernel,
        grid_spec=pltpu.PrefetchScalarGridSpec(
            num_scalar_prefetch=1,
            grid=(levels + 2,),
            in_specs=[whole((tokens, width))] * 2
            + [piece, piece]
            + [
                pl.BlockSpec((2 * tokens, block), lambda t, w: (1, at(t))),
                pl.BlockSpec((width, block), lambda t, w: (0, at(t))),
            ],
            out_specs=[whole((tokens, width))] * 2
            + [
                pl.BlockSpec((block, width), lambda t, w: (at(t), 0)),
                pl.BlockSpec((2 * tokens, block), lambda t, w: (0, at(t))),
            ],
            scratch_shapes=[
                pltpu.VMEM((2 * tokens, hidden), BF),
                pltpu.VMEM((width, hidden), BF),
            ],
        ),
        out_shape=[
            jax.ShapeDtypeStruct((tokens, width), F32),
            jax.ShapeDtypeStruct((tokens, width), BF),
            jax.ShapeDtypeStruct((hidden, width), BF),
            jax.ShapeDtypeStruct((2 * tokens, hidden), BF),
        ],
        compiler_params=params(),
        cost_estimate=cost(8),
        name="feed_down_far",
    )(where, *grads, *pieces, slope, columns)


def near_kernel(
    where, normed, first_grad, last_grad, weights, slope, columns, far_hidden,
    first_back, last_back, sums, near_out, beside_out, flipped, hidden, up, product,
):
    step = pl.program_id(0)
    steps = pl.num_programs(0) - 2
    block = weights.shape[0]
    levels, rows = near_out.shape[:2]
    tokens = first_grad.shape[0]

    @pl.when(step == 0)
    def _():
        for i in range(4):
            here = slice(i * tokens, (i + 1) * tokens)
            flipped[:, here] = normed[here, :].T

    @pl.when(step < steps)
    def _():
        place = pl.ds(pl.multiple_of(step * block, block), block)
        up[:, place] = columns[...]
        parts = []
        for i, grad in enumerate((first_grad, last_grad)):
            here = slice(i * tokens, (i + 1) * tokens)
            d_act = dot(grad[...], weights[...], NT)
            low = (d_act * slope[here, :].astype(F32)).astype(BF)
            hidden[here, place] = low
            parts.append(low)
        parts.append(far_hidden[...])
        every = jnp.concatenate(parts, axis=0)
        sums[0] = jnp.sum(every.astype(F32), axis=0, keepdims=True)
        product[...] = dot(flipped[...], every, NN).astype(BF)
        for far_x, out in enumerate((near_out, beside_out)):
            for z in range(levels):
                first = (z * 2 + (where[0] ^ far_x)) * rows
                out[z] = product[pl.ds(pl.multiple_of(first, rows), rows), :]

    @pl.when(step == steps)
    def _():
        first_back[...] = dot(hidden[:tokens, :], up[...], NT)

    @pl.when(step == steps + 1)
    def _():
        last_back[...] = dot(hidden[tokens:, :], up[...], NT).astype(BF)


def feed_down_near(where, normed, grads, weights, slope, columns, far_hidden, levels):
    tokens, width = grads[0].shape
    hidden = weights.shape[0]
    block = hidden // levels
    rows = width // (2 * levels)
    at = lambda t: jnp.minimum(t, levels - 1)
    line = pl.BlockSpec((2 * tokens, block), lambda t, w: (0, at(t)))
    out = pl.BlockSpec((levels, rows, block), lambda t, w: (0, 0, at(t)))
    return pl.pallas_call(
        near_kernel,
        grid_spec=pltpu.PrefetchScalarGridSpec(
            num_scalar_prefetch=1,
            grid=(levels + 2,),
            in_specs=[whole((4 * tokens, width))]
            + [whole((tokens, width))] * 2
            + [
                pl.BlockSpec((block, width), lambda t, w: (at(t), 0)),
                line,
                pl.BlockSpec((width, block), lambda t, w: (0, at(t))),
                line,
            ],
            out_specs=[whole((tokens, width))] * 2
            + [pl.BlockSpec((1, 1, block), lambda t, w: (at(t), 0, 0)), out, out],
            scratch_shapes=[
                pltpu.VMEM((width, 4 * tokens), BF),
                pltpu.VMEM((2 * tokens, hidden), BF),
                pltpu.VMEM((width, hidden), BF),
                pltpu.VMEM((width, block), BF),
            ],
        ),
        out_shape=[
            jax.ShapeDtypeStruct((tokens, width), F32),
            jax.ShapeDtypeStruct((tokens, width), BF),
            jax.ShapeDtypeStruct((levels, 1, block), F32),
        ]
        + [jax.ShapeDtypeStruct((levels, rows, hidden), BF)] * 2,
        compiler_params=params(),
        cost_estimate=cost(12),
        name="feed_down_near",
    )(where, normed, *grads, weights, slope, columns, far_hidden)


def part_kernel(activated, weights, near, beside):
    out = dot(activated[...], weights[...], NN)

    @pl.when(pl.program_id(0) % 2 == 0)
    def _():
        near[0] = out

    @pl.when(pl.program_id(0) % 2 == 1)
    def _():
        beside[0] = out.astype(BF)


def feed_out(activated, weights):
    rows, (hidden, width) = activated.shape[0] // 4, weights.shape
    out = pl.BlockSpec((1, rows, width), lambda b: (b // 2, 0, 0))
    return pl.pallas_call(
        part_kernel,
        grid=(4,),
        in_specs=[pl.BlockSpec((rows, hidden), lambda b: (b, 0)), whole(weights.shape)],
        out_specs=[out, out],
        out_shape=[
            jax.ShapeDtypeStruct((2, rows, width), F32),
            jax.ShapeDtypeStruct((2, rows, width), BF),
        ],
        compiler_params=params(),
        cost_estimate=cost(7),
        name="feed_out",
    )(activated, weights)


def norm_back_kernel(
    where, own, arrived, far, resid, grad, gain, weights, d_resid, d_low, *rest
):
    outs, sums = rest[:-1], rest[-1]
    d_normed = own[...] + arrived[...].astype(F32) + far[...].astype(F32)
    unit, inverse = normalise(resid[...])
    wide = grad[...].astype(F32)
    out = wide + norm_back(unit, inverse, d_normed * gain[...])
    low = out.astype(BF)
    d_resid[...] = out
    d_low[...] = low
    parts = [d_normed * unit, d_normed, low.astype(F32), wide]
    parts = [jnp.sum(p, axis=0, keepdims=True) for p in parts]
    parts = jnp.concatenate(parts + [jnp.zeros_like(parts[0])] * 4, axis=0)

    @pl.when(pl.program_id(0) == 0)
    def _():
        sums[...] = parts

    @pl.when(pl.program_id(0) > 0)
    def _():
        sums[...] += parts

    d_attended = dot(low, weights[...], NT).astype(BF)
    for m, out in enumerate(outs):
        for h in range(out.shape[0]):
            lanes = out.shape[2]
            first = (m * out.shape[0] + h) * lanes
            out[h] = d_attended[:, first : first + lanes]


def second_norm_back(where, own, arrived, far, resid, grad, gain, weights, seq, groups):
    rows, width = resid.shape
    step = rows // 2
    lanes = width // (seq * groups)
    line = pl.BlockSpec((step, width), lambda i, w: (i, 0))
    return pl.pallas_call(
        norm_back_kernel,
        grid_spec=pltpu.PrefetchScalarGridSpec(
            num_scalar_prefetch=1,
            grid=(rows // step,),
            in_specs=[line] * 5 + [whole((1, width)), whole((width, width))],
            out_specs=[line, line]
            + [pl.BlockSpec((groups, step, lanes), lambda i, w: (0, i, 0))] * seq
            + [whole((8, width))],
        ),
        out_shape=[
            jax.ShapeDtypeStruct((rows, width), F32),
            jax.ShapeDtypeStruct((rows, width), BF),
        ]
        + [jax.ShapeDtypeStruct((groups, rows, lanes), BF)] * seq
        + [jax.ShapeDtypeStruct((8, width), F32)],
        compiler_params=params(),
        cost_estimate=cost(8),
        name="second_norm_back",
    )(where, own, arrived, far, resid, grad, gain, weights)


def out_grad_kernel(where, attended, grad, near, beside, product):
    product[...] = dot(attended[...], grad[...], TN).astype(BF)
    levels, _, lanes = near.shape[2:]
    rows = near.shape[3] * lanes // product.shape[1]
    for m in range(4):
        out = (near, beside)[m % 2]
        for far_x in range(2):
            for z in range(levels):
                first = out_row(z, where[0] ^ far_x, where, 4 * rows) + (where[3] ^ m) * rows
                here = pl.ds(pl.multiple_of(first, rows), rows)
                for k in range(product.shape[1] // lanes):
                    out[m // 2, far_x, z, k * rows : (k + 1) * rows, :] = product[
                        here, k * lanes : (k + 1) * lanes
                    ]


def out_grad(where, attended, grad, levels, lanes):
    width = grad.shape[1]
    shape = (2, 2, levels, width // (8 * levels) * (width // lanes), lanes)
    return pl.pallas_call(
        out_grad_kernel,
        grid_spec=pltpu.PrefetchScalarGridSpec(
            num_scalar_prefetch=1,
            grid=(1,),
            in_specs=[whole(attended.shape), whole(grad.shape)],
            out_specs=[whole(shape)] * 2,
            scratch_shapes=[pltpu.VMEM((width, width), BF)],
        ),
        out_shape=[jax.ShapeDtypeStruct(shape, BF)] * 2,
        compiler_params=params(),
        cost_estimate=cost(4),
        name="out_grad",
    )(where, attended, grad)


def heads_back_kernel(
    head_size, blocks, last, where, *refs
):
    pieces, refs = refs[:blocks], refs[blocks:]
    (query, keys, values, tops, inverses, table, *refs) = refs
    spots, (first_rows, last_rows, *rest) = refs[:blocks], refs[blocks:]
    if last:
        near0, near1, beside0, beside1, earlier, first_unit, last_unit, *rest = rest
        norm_sums2, up_sums, tops_row, earlier_sum, *rest = rest
        sent_back, sent_beside, near_grad, beside_grad, *rest = rest
        weights, joined, vectors, norm_sums, bias_sum, total, d_keys, d_values, grads = rest
    else:
        sent_back, near_grad, beside_grad, bias_sum, *rest = rest
        total, d_keys, d_values, grads = rest
    levels, rows = near_grad.shape[0], near_grad.shape[2]
    length, lanes = query.shape[1:]
    three = 3 * lanes
    tokens = length // blocks
    clip = pl.program_id(0)

    if last:

        @pl.when(clip == 0)
        def _():
            for z in range(levels):
                for far_x, parts in enumerate(((near0, near1), (beside0, beside1))):
                    first = (z * 2 + (where[0] ^ far_x)) * rows
                    here = pl.ds(pl.multiple_of(first, rows), rows)
                    for h, part in enumerate(parts):
                        weights[here, h * three : (h + 1) * three] = part[z]

    for b in range(blocks):
        grads[b * tokens : (b + 1) * tokens, :] = pieces[b][0]
    spots = spots_of(clip, pl.num_programs(0), spots, tokens)
    cosine, sine = rotary_of(spots, table)
    scale = jnp.asarray(head_size**-0.5, BF)
    chunk = length // 2
    parts = []
    for i in range(2):
        here = pl.ds(i * chunk, chunk)
        query_rows, grad_rows = query[0, here, :], grads[here, :]
        query_total = None
        for h in range(lanes // head_size):
            own_keys = keep_head(keys[0], h, head_size) * scale
            own_values = keep_head(values[0], h, head_size)
            scores = dot(own_keys, query_rows, NT)
            probs = jnp.exp(scores - tops[0, h : h + 1, here]) * inverses[0, h : h + 1, here]
            d_probs = dot(own_values, grad_rows, NT)
            delta = jnp.sum(probs * d_probs, axis=0, keepdims=True)
            d_scores = (probs * (d_probs - delta)).astype(BF)
            value_part = dot(probs.astype(BF), keep_head(grad_rows, h, head_size), NN)
            key_part = dot(d_scores, keep_head(query_rows, h, head_size) * scale, NN)
            query_part = dot(d_scores, own_keys, TN)
            if h == 0 and i == 0:
                d_values[...] = value_part
                d_keys[...] = key_part
            else:
                d_values[...] += value_part
                d_keys[...] += key_part
            query_total = query_part if query_total is None else query_total + query_part
        parts.append(query_total)
    d_query = jnp.concatenate(parts, axis=0)

    def back(part):
        return (part * cosine - swap_halves(part, head_size) * sine).astype(BF)

    d_mixed = jnp.concatenate(
        [back(d_query), back(d_keys[...]), d_values[...].astype(BF)], axis=1
    )
    sums = jnp.sum(d_mixed.astype(F32), axis=0, keepdims=True)
    half = length // 2
    part = dot(d_mixed[:half], first_rows[0], TN) + dot(d_mixed[half:], last_rows[0], TN)

    @pl.when(clip == 0)
    def _():
        bias_sum[...] = sums
        total[...] = part

    @pl.when(clip > 0)
    def _():
        bias_sum[...] += sums
        total[...] += part

    def put_grads(bit, out):
        for z in range(levels):
            first = (z * 2 + (where[0] ^ bit)) * rows
            out[z, :three, :] = total[:, pl.ds(pl.multiple_of(first, rows), rows)].astype(BF)

    if not last:
        sent_back[0] = d_mixed

        @pl.when(clip == pl.num_programs(0) - 1)
        def _():
            put_grads(0, near_grad)
            put_grads(1, beside_grad)

        return
    joined[:, :three] = earlier[0]
    joined[:, three:] = d_mixed
    both = 0.0
    for i, unit in enumerate((first_unit, last_unit)):
        d_normed = dot(joined[i * half : (i + 1) * half, :], weights[...], NT)
        two = [
            jnp.sum(d_normed * unit[0].astype(F32), axis=0, keepdims=True),
            jnp.sum(d_normed, axis=0, keepdims=True),
        ]
        both = both + jnp.concatenate(two + [jnp.zeros_like(two[0])] * 6, axis=0)
        low = d_normed.astype(BF)
        for b in range(blocks // 2):
            out = (sent_back, sent_beside)[b % 2]
            out[i * (blocks // 4) + b // 2, 0] = low[b * tokens : (b + 1) * tokens]

    @pl.when(clip == 0)
    def _():
        norm_sums[...] = both

    @pl.when(clip > 0)
    def _():
        norm_sums[...] += both

    @pl.when(clip == pl.num_programs(0) - 1)
    def _():
        vectors[...] = jnp.zeros_like(vectors)
        for f in range(2 * levels):
            here = slice(f * rows, (f + 1) * rows)
            for row, (source, at) in enumerate(
                ((norm_sums, 0), (norm_sums2, 0), (norm_sums, 1), (norm_sums2, 1),
                 (norm_sums2, 2), (norm_sums2, 3))
            ):
                vectors[f, row : row + 1, :] = source[at : at + 1, here]
            vectors[f, pl.ds(9 + where[1], 1), :] = up_sums[f // 2, :, (f % 2) * rows : (f % 2 + 1) * rows]
            vectors[f, VECTOR_ROWS - 1 : VECTOR_ROWS, :] = tops_row[...]
        for h, source in enumerate((earlier_sum, bias_sum)):
            for part in range(3):
                place = (part * blocks + where[1]) * 2 + h
                at = 6 + lax.rem(place, 3)
                vectors[place // 3, pl.ds(at, 1), :] = source[:, part * lanes : (part + 1) * lanes]
        put_grads(0, near_grad)
        put_grads(1, beside_grad)
        for z in range(levels):
            for bit, out in ((0, near_grad), (1, beside_grad)):
                out[z, three:, :] = vectors[z * 2 + (where[0] ^ bit)].astype(BF)


def heads_back(
    where, group, grads_in, saved, table, x_blocks, normed, levels, blocks, head_size,
    weights=(), earlier=None, unit=None, vectors=(),
):
    clips, half, width = normed[0].shape
    length, lanes = 2 * half, grads_in[0].shape[2]
    three, rows = 3 * lanes, width // (2 * levels)
    last = earlier is not None
    clip = lambda *rest: pl.BlockSpec((1,) + rest, lambda i, w: (i,) + (0,) * len(rest))
    by_block = lambda m, n: pl.BlockSpec(
        (m, 1, length // blocks, n), lambda i, w: (0, i, 0, 0)
    )
    stats = clip(lanes // head_size, length)
    query, keys, values, tops, inverses = saved
    grads = (levels, three + (VECTOR_ROWS + 2 if last else 0), rows)
    outs = [jax.ShapeDtypeStruct(grads, BF)] * 2
    out_specs = [whole(grads)] * 2
    piece = pl.BlockSpec((1, length // blocks, lanes), lambda i, w: (group, i, 0))
    in_specs = [piece] * blocks + [clip(length, lanes)] * 3 + [stats] * 2
    in_specs += [whole(table.shape)] + [spot_block(x) for x in x_blocks]
    in_specs += [clip(half, width)] * 2
    scratch = [
        pltpu.VMEM((three, width), F32),
        pltpu.VMEM((length, lanes), F32),
        pltpu.VMEM((length, lanes), F32),
        pltpu.VMEM((length, lanes), BF),
    ]
    if last:
        outs = [jax.ShapeDtypeStruct((blocks // 2, clips, length // blocks, width), BF)] * 2 + outs
        out_specs = [by_block(blocks // 2, width)] * 2 + out_specs
        in_specs += [whole(w.shape[:2] + (three,)) for w in weights]
        in_specs += [clip(length, three)] + [clip(half, width)] * 2
        in_specs += [whole(v.shape) for v in vectors]
        scratch = [
            pltpu.VMEM((width, 2 * three), BF),
            pltpu.VMEM((length, 2 * three), BF),
            pltpu.VMEM((2 * levels, VECTOR_ROWS + 2, lanes), F32),
            pltpu.VMEM((8, width), F32),
            pltpu.VMEM((1, three), F32),
        ] + scratch
    else:
        outs = [jax.ShapeDtypeStruct((clips, length, three), BF)] + outs
        outs += [jax.ShapeDtypeStruct((1, three), F32)]
        out_specs = [clip(length, three)] + out_specs + [whole((1, three))]
    return pl.pallas_call(
        functools.partial(heads_back_kernel, head_size, blocks, last),
        grid_spec=pltpu.PrefetchScalarGridSpec(
            num_scalar_prefetch=1,
            grid=(clips,),
            in_specs=in_specs,
            out_specs=out_specs,
            scratch_shapes=scratch,
        ),
        out_shape=outs,
        compiler_params=params(),
        cost_estimate=cost(22),
        name="heads_back",
    )(
        where, *grads_in, query, keys, values, tops, inverses, table, *x_blocks, *normed,
        *weights, *([earlier, *unit, *vectors] if last else []),
    )


def finish_out_kernel(resid, near, beside, far, bias, out):
    total = resid[...] + near[0] + beside[0].astype(F32) + far[...].astype(F32) + bias[...]
    out[...] = total.astype(BF)


def finish_out(resid, near, beside, far, bias):
    rows, width = resid.shape
    step = rows // 4
    line = pl.BlockSpec((step, width), lambda i: (i, 0))
    first = pl.BlockSpec((1, step, width), lambda i: (0, i, 0))
    return pl.pallas_call(
        finish_out_kernel,
        grid=(rows // step,),
        in_specs=[line, first, first, line, whole((1, width))],
        out_specs=line,
        out_shape=jax.ShapeDtypeStruct((rows, width), BF),
        compiler_params=params(),
        cost_estimate=cost(4),
        name="finish_out",
    )(resid, near, beside, far, bias)


def first_norm_back_kernel(near, far, x, d_resid, gain, out):
    d_normed = near[0].astype(F32) + far[...].astype(F32)
    unit, inverse = normalise(x[...].astype(F32))
    out[...] = d_resid[...] + norm_back(unit, inverse, d_normed * gain[...])


def first_norm_back(near, far, x, d_resid, gain):
    rows, width = x.shape
    step = rows // 4
    line = pl.BlockSpec((step, width), lambda i: (i, 0))
    return pl.pallas_call(
        first_norm_back_kernel,
        grid=(rows // step,),
        in_specs=[pl.BlockSpec((1, step, width), lambda i: (0, i, 0)), line, line, line]
        + [whole((1, width))],
        out_specs=line,
        out_shape=jax.ShapeDtypeStruct((rows, width), F32),
        compiler_params=params(),
        cost_estimate=cost(4),
        name="first_norm_back",
    )(near, far, x, d_resid, gain)


def pack_kernel(three, first, last, up, out, out_grads):
    levels, _, lanes = first.shape
    seq, rows = out.shape[0], up.shape[0] // out.shape[0]
    for h, part in enumerate((first, last)):
        total = part[0].astype(F32)
        for z in range(1, levels):
            total = total + part[z].astype(F32)
        if h == 0:
            for k in range(out_grads.shape[1] // lanes):
                block = total[three + k * rows : three + (k + 1) * rows]
                out_grads[:, k * lanes : (k + 1) * lanes] = block
        turned = total[:three].T.astype(BF)
        for t in range(seq):
            out[t, :rows, h * three : (h + 1) * three] = turned[t * rows : (t + 1) * rows]
    for t in range(seq):
        out[t, rows:, :lanes] = total[three:].astype(BF)
        out[t, :rows, 2 * three :] = up[t * rows : (t + 1) * rows]


def pack(first, last, up, seq, three):
    extra, rows = last.shape[1] - three, up.shape[0] // seq
    shape = (seq, rows + extra, 2 * three + up.shape[1])
    width = (first.shape[1] - three) * first.shape[2] // rows
    return pl.pallas_call(
        functools.partial(pack_kernel, three),
        out_shape=[jax.ShapeDtypeStruct(shape, BF), jax.ShapeDtypeStruct((rows, width), F32)],
        compiler_params=params(),
        cost_estimate=cost(4),
        name="pack",
    )(first, last, up)


def unpack_kernel(
    rows, count, packed, weights, bias, threshold, qkv, up, vectors, maxima, clipped, clipped_bias
):
    seq, lanes = packed.shape[0], vectors.shape[1]
    width = qkv.shape[1] // 3
    group = width // seq
    own_heads = HEADS // seq
    sums = None
    column = lax.broadcasted_iota(jnp.int32, (1, width), 1) // (width // HEADS)
    lane = lax.broadcasted_iota(jnp.int32, (1, lanes), 1)
    limit = threshold[...]
    best = jnp.full((1, lanes), -jnp.inf, F32)
    scales = jnp.ones((1, width), F32)
    for t in range(seq):
        for h in range(group // lanes):
            for part in range(3):
                at = (h * 3 + part) * lanes
                to = part * width + t * group + h * lanes
                qkv[:, to : to + lanes] = packed[t, :rows, at : at + lanes].astype(F32)
        for k in range(up.shape[1] // (seq * lanes)):
            at = (3 * group // lanes + k) * lanes
            to = (k * seq + t) * lanes
            up[:, to : to + lanes] = packed[t, :rows, at : at + lanes].astype(F32)
        extra = packed[t, rows:, :lanes].astype(F32)
        sums = extra if sums is None else sums + extra
        tops = extra[VECTOR_ROWS - 1 : VECTOR_ROWS]
        tops = tops + pltpu.roll(tops, lanes - own_heads, 1) + pltpu.roll(tops, lanes - 2 * own_heads, 1)
        for h in range(own_heads):
            here = (lane % (3 * own_heads) == h) & (lane < count * 3 * own_heads)
            top = jnp.max(jnp.where(here, tops, -jnp.inf), axis=1, keepdims=True)
            head = t * own_heads + h
            best = jnp.where(lane == head, top, best)
            gamma = jnp.sqrt(limit / jnp.maximum(top, limit))
            scales = jnp.where(column == head, gamma, scales)
    vectors[...] = sums
    maxima[...] = best
    for part in range(2):
        here = slice(part * width, (part + 1) * width)
        clipped[:, here] = weights[:, here].astype(F32) * scales
        clipped_bias[:, here] = bias[:, here] * scales


def unpack(packed, weights, bias, threshold, rows, count, hidden, lanes):
    width = weights.shape[1] // 3
    two = pl.BlockSpec((weights.shape[0], 2 * width), lambda i: (0, 0))
    return pl.pallas_call(
        functools.partial(unpack_kernel, rows, count),
        grid=(1,),
        in_specs=[whole(packed.shape), two, whole(bias.shape), whole(threshold.shape)],
        out_specs=[
            whole((rows, 3 * width)),
            whole((rows, hidden)),
            whole((packed.shape[1] - rows, lanes)),
            whole((1, lanes)),
            whole((weights.shape[0], 2 * width)),
            whole((1, 2 * width)),
        ],
        out_shape=[
            jax.ShapeDtypeStruct((rows, 3 * width), F32),
            jax.ShapeDtypeStruct((rows, hidden), F32),
            jax.ShapeDtypeStruct((packed.shape[1] - rows, lanes), F32),
            jax.ShapeDtypeStruct((1, lanes), F32),
            jax.ShapeDtypeStruct((weights.shape[0], 2 * width), F32),
            jax.ShapeDtypeStruct((1, 2 * width), F32),
        ],
        compiler_params=params(),
        cost_estimate=cost(4),
        name="unpack",
    )(packed, weights, bias, threshold)


VECTOR_ROWS = 14


def square_device(
    block_input,
    out_cotangent,
    positions,
    w_qkv,
    w_out,
    w_up,
    w_down,
    norm_gains,
    norm_shifts,
    qkv_bias,
    proj_bias,
    up_bias,
    clip_threshold,
):
    clips, tokens, width = block_input.shape
    fsdp, seq = axis_size(FSDP), axis_size(SEQ)
    levels, outer = fsdp // 2, seq // 2
    head_size = width // HEADS
    group = width // seq
    lanes = 128
    groups = group // lanes
    hidden = up_bias.shape[0]
    share = hidden // (fsdp * seq)
    length = tokens * seq
    rows = width // fsdp
    levels_index = lax.axis_index("z")
    x, y, c = lax.axis_index("x"), lax.axis_index("y"), lax.axis_index("core")
    s = y * 2 + c
    heads_where = jnp.stack([x, s]).astype(jnp.int32)
    where = jnp.stack([x, y, c, s]).astype(jnp.int32)
    x_own = block_input.reshape(clips * tokens, width)
    g_own = out_cotangent.reshape(clips * tokens, width)

    def copies(piece):
        return jnp.broadcast_to(piece[None], (levels,) + piece.shape)

    def over_z(piece):
        return lax.all_to_all(piece, "z", 0, 0, tiled=True)

    def heads_piece(h):
        firsts = [(part * seq + s) * group + h * lanes for part in range(3)]
        return [lax.dynamic_slice_in_dim(w_qkv, first, lanes, 1) for first in firsts]

    near0 = over_z(copies(jnp.concatenate(heads_piece(0), axis=1)))

    spots = positions.astype(BF).reshape(-1)
    count = spots.shape[0]
    spots = jnp.pad(spots, (0, 8 * width - count)).reshape(8, width)
    x_ext = jnp.concatenate([x_own, spots], axis=0)
    x_beside = flip_one(x_ext, "y")
    x_core = flip_one(x_ext, "core")

    near1 = lax.dynamic_slice_in_dim(w_out, c * 2 * group, 2 * group, 1)
    near1 = jnp.concatenate(heads_piece(1) + [near1, jnp.zeros((rows, lanes), BF)], axis=1)
    near1 = lax.all_gather(near1, "z", axis=0)
    up = own_columns(where, w_up, fsdp, share)
    up = lax.all_gather(after(up, x_beside), "z", axis=0)
    down = lax.dynamic_slice_in_dim(w_down, s * share, share, 0)
    down = lax.all_gather(after(down, x_beside), "z", axis=0)

    halves = [first_norm(x_ext, x_core, norm_gains[:1], norm_shifts[:1], clips)]
    beside0 = flip_one(near0, "x")
    x_far = flip_one(after(x_beside, near0), "core")
    halves.append(first_norm(x_beside, x_far, norm_gains[:1], norm_shifts[:1], clips))
    normed1, unit1 = zip(*halves, strict=True)
    x_blocks = (x_ext, x_core, x_beside, x_far)
    table = jnp.asarray(rotary_parts(head_size, lanes))
    g_beside = flip_one(after(g_own, x_beside), "y")
    near1 = after(near1, normed1[1])
    beside1 = flip_one(near1[..., : 3 * lanes], "x")

    own_bias = lax.dynamic_index_in_dim(
        qkv_bias.reshape(3, seq, groups, lanes), s, 1, keepdims=False
    )

    def forward(h, near, beside):
        return heads_forward(
            heads_where, normed1, near, beside, own_bias[:, h].reshape(1, -1),
            table, x_blocks, seq, head_size,
        )

    *saved0, out0, tops0, inverses0 = forward(0, near0, after(beside0, g_beside))
    saved0 += [tops0, inverses0]
    out0 = after(out0, beside1)
    out0_beside = flip_one(out0, "y")
    out0_core = flip_one(out0, "core")
    own_out = near1[..., 3 * lanes : 3 * lanes + 2 * group]
    own_out = (own_out, flip_one(own_out, "x"))

    *saved1, out1, tops1, inverses1 = forward(1, near1, beside1)
    saved1 += [tops1, inverses1]
    out1 = after(out1, out0_beside, out0_core, own_out[1])
    up = (up, flip_one(after(up, tops1), "x"))
    out1_beside = flip_one(out1, "y")
    out1_core = flip_one(out1, "core")
    out0_far = flip_one(after(out0_beside, tops1), "core")
    own_out = jnp.stack(own_out)
    other_out = flip_one(after(own_out, tops1), "core")
    out1_far = flip_one(out1_beside, "core")
    g_core = flip_one(after(g_own, out1_beside), "core")
    g_far = flip_one(after(g_beside, out1_beside), "core")
    pieces0 = (out0, out0_core, out0_beside, out0_far)
    pieces1 = (out1, out1_core, out1_beside, out1_far)
    down = (down, flip_one(after(down, out1_beside), "x"))
    tops_own = jnp.concatenate([jnp.max(t, axis=(0, 2)) for t in (tops0, tops1)])

    resid1, attended_own, normed2, full_out = project(
        where, (pieces0, pieces1), x_blocks, own_out, other_out,
        proj_bias[:1], norm_gains[1:], norm_shifts[1:],
    )

    bias = up_bias.reshape(levels, 2, seq, share)
    bias = lax.dynamic_index_in_dim(bias, s, 2, keepdims=False).reshape(levels, 1, 2 * share)
    grads = (g_own, g_core, g_beside, g_far)
    activated, slope, columns, down_near, down_beside = feed_up(where, normed2, grads, up, bias)
    down_beside = flip_one(down_beside, "x")
    far_back, far_other, full_down, far_hidden = feed_down_far(
        where, grads[2:], down, slope, columns
    )
    far_back = add_low(far_back, flip_one(far_other, "core"))
    far_hidden = after(far_hidden, far_back)
    far_back = flip_one(far_back, "y")
    own_back, other_back, up_sums, up_near, up_beside = feed_down_near(
        where, normed2, grads[:2], full_down, slope, columns, far_hidden, levels
    )
    other_back = flip_one(after(other_back, far_back, down_beside), "core")
    up_beside = flip_one(up_beside, "x")
    part_near, part_beside = feed_out(after(activated, up_sums), full_down)
    part_beside = flip_one(part_beside, "core")
    down_sum = add_low(down_near, after(down_beside, up_sums))
    d_resid1, d_resid1_low, *rest = second_norm_back(
        where, own_back, after(other_back, part_near), far_back, resid1, g_own,
        norm_gains[1:], full_out, seq, groups,
    )
    d_attended, sums2 = rest[:-1], rest[-1]
    d_heads = [d_attended[0]] + [flip(d_attended[m], SEQ, m) for m in range(1, seq)]
    grad_down = lax.psum_scatter(down_sum, "z", scatter_dimension=0, tiled=True)
    grad_down = grad_down.reshape(share, width).astype(F32)
    up_sum = add_low(up_near, after(up_beside, d_resid1_low))
    out_near, out_beside = out_grad(where, attended_own, d_resid1_low, levels, lanes)
    part_far = add_low(part_near[1], part_beside[1])
    out_beside = flip_one(after(out_beside, part_far, *d_heads[1:]), "core")

    tops_row, rest = [], tops_own
    for _ in range(3):
        tops_row.append(lax.reduce_precision(rest, 8, 7))
        rest = rest - tops_row[-1]
    tops_row = lax.dynamic_update_slice_in_dim(
        jnp.zeros((lanes,), F32), jnp.concatenate(tops_row), (levels_index * 2 + x) * 12, 0
    )[None]

    out_sum = add_low(out_near, out_beside)
    d_heads = after_all(d_heads, down_sum, up_sum, out_sum)
    up_sum = lax.psum_scatter(after(up_sum, d_heads[2]), "z", scatter_dimension=0, tiled=True)
    up_sum = up_sum.reshape(rows, fsdp * share)
    mixed0, near_grad0, beside_grad0, bias_sum0 = heads_back(
        heads_where, 0, d_heads, saved0, table, x_blocks, normed1, levels, seq, head_size
    )
    out_far = flip_one(out_sum[1], "y")
    part_far = flip_one(after(part_far, out_far), "y")
    out_sum = add_low(out_sum[0], after(out_far, bias_sum0))
    near_grad0 = jnp.concatenate([near_grad0, out_sum[0]], axis=1)
    beside_grad0 = jnp.concatenate([beside_grad0, out_sum[1]], axis=1)
    beside_grad0 = flip_one(beside_grad0, "x")
    last, last_beside, near_grad1, beside_grad1 = heads_back(
        heads_where, 1, after_all(d_heads, grad_down), saved1, table, x_blocks, normed1,
        levels, seq, head_size, (near0, near1, beside0, beside1), mixed0, unit1,
        (sums2, up_sums, tops_row, bias_sum0),
    )
    qkv_sum0 = add_low(near_grad0, beside_grad0)
    last_beside = flip_one(after(last_beside, qkv_sum0, up_sum, part_far), "core")
    beside_grad1 = flip_one(after(beside_grad1, qkv_sum0, up_sum), "x")
    qkv_sum0 = over_z(qkv_sum0)
    near_blocks = add_low(last, last_beside)
    far_block = flip_one(after(near_blocks[1], beside_grad1), "y")
    block_out = finish_out(
        after(resid1, near_blocks), part_near, part_beside, part_far, proj_bias[1:]
    )
    qkv_sum1 = over_z(add_low(near_grad1, beside_grad1))
    grad_input = first_norm_back(
        near_blocks.reshape(2, clips * tokens, width), far_block.reshape(x_own.shape),
        x_own, d_resid1, norm_gains[:1],
    ).reshape(block_input.shape)

    one = rows // seq
    packed, grad_out = pack(after(qkv_sum0, block_out), qkv_sum1, up_sum, seq, 3 * lanes)
    packed = lax.all_to_all(after(packed, far_block, block_out), SEQ, 0, 0, tiled=True)
    grad_qkv, grad_up, vectors, maxima, clipped, clipped_bias = unpack(
        packed, w_qkv, qkv_bias[None], clip_threshold[None], one, fsdp, hidden, lanes
    )
    maxima, clipped_bias = maxima[0, :HEADS], clipped_bias[0]
    lines = lax.dynamic_slice_in_dim(vectors[:6], s * one, one, 1)
    grad_gains, grad_shifts, grad_proj_bias = lines[:2], lines[2:4], lines[4:]
    grad_qkv_bias = lax.dynamic_slice_in_dim(vectors[6:9].reshape(-1), s * 3 * one, 3 * one)
    grad_up_bias = lax.dynamic_index_in_dim(vectors, 9 + s, 0, keepdims=False)

    return (
        block_out.reshape(block_input.shape),
        grad_input,
        grad_qkv,
        grad_out,
        grad_up,
        grad_down,
        grad_gains,
        grad_shifts,
        grad_qkv_bias,
        grad_proj_bias,
        grad_up_bias,
        maxima,
        clipped,
        clipped_bias,
    )


def on_device(block_input, *rest):
    fsdp, seq = axis_size(FSDP), axis_size(SEQ)
    width, hidden = block_input.shape[2], rest[-2].shape[0]
    square = seq == 4 and fsdp % 4 == 0 and fsdp == 8 and width == 256 * seq and hidden % (128 * fsdp * seq) == 0
    square = square and width % (128 * fsdp) == 0
    return (square_device if square else general_device)(block_input, *rest)


def solution(mesh):
    fsdp, seq = mesh.shape["fsdp"], mesh.shape["seq"]
    fine = Mesh(mesh.devices.reshape(fsdp // 2, 2, seq // 2, 2), FSDP + SEQ)
    in_specs = (
        P(FSDP, SEQ, None),
        P(FSDP, SEQ, None),
        P(None, FSDP, SEQ),
        P(FSDP, None),
        P(FSDP, None),
        P(FSDP, None),
        P(FSDP, None),
        P(),
        P(),
        P(),
        P(),
        P(),
        P(),
    )
    out_specs = (
        P(FSDP, SEQ, None),
        P(FSDP, SEQ, None),
        P(FSDP + SEQ, None),
        P(FSDP + SEQ, None),
        P(FSDP + SEQ, None),
        P(FSDP + SEQ, None),
        P(None, FSDP + SEQ),
        P(None, FSDP + SEQ),
        P(FSDP + SEQ),
        P(None, FSDP + SEQ),
        P(FSDP + SEQ),
        P(),
        P(FSDP, None),
        P(),
    )
    return jax.shard_map(
        on_device, mesh=fine, in_specs=in_specs, out_specs=out_specs, check_vma=False
    )
```

```python
import functools

import jax
import jax.numpy as jnp
import numpy as np
from jax import lax
from jax.experimental import pallas as pl
from jax.experimental.pallas import tpu as pltpu
from jax.sharding import Mesh
from jax.sharding import PartitionSpec as P

HEADS = 16
EPSILON = 1e-06
ROPE_BASE = 100.0
GRID_SIDE = 16

FSDP = ("z", "x")
SEQ = ("y", "core")

BF = jnp.bfloat16
F32 = jnp.float32
NN = (((1,), (0,)), ((), ()))
NT = (((1,), (1,)), ((), ()))
TN = (((0,), (0,)), ((), ()))


def dot(left, right, dims):
    return lax.dot_general(left, right, dims, preferred_element_type=F32)


def params(megabytes=62):
    return pltpu.CompilerParams(vmem_limit_bytes=megabytes << 20)


def axis_size(names):
    size = 1
    for name in names:
        size *= lax.axis_size(name)
    return size


def flip(value, axis, mask):
    size = axis_size(axis)
    return lax.ppermute(value, axis, [(i, i ^ mask) for i in range(size)])


def dim_of(name):
    inner = 2
    if name == "x":
        return FSDP, 1, inner
    if name == "z":
        return FSDP, inner, axis_size(FSDP) // inner
    if name == "core":
        return SEQ, 1, inner
    return SEQ, inner, axis_size(SEQ) // inner


def gather_dim(value, name, axis):
    mesh_axis, stride, size = dim_of(name)
    parts = [value] + [flip(value, mesh_axis, k * stride) for k in range(1, size)]
    return jnp.stack(parts, axis)


def scatter_dim(value, name, axis, last):
    mesh_axis, stride, size = dim_of(name)
    total = lax.index_in_dim(value, 0, axis, keepdims=False).astype(F32)
    for k in range(1, size):
        part = lax.index_in_dim(value, k, axis, keepdims=False)
        total = total + flip(part, mesh_axis, k * stride).astype(F32)
    return total if last else total.astype(BF)


def copy_kernel(source, target):
    target[...] = source[...].reshape(target.shape)


def gather_order_kernel(pieces, shift, *refs):
    sources, target = refs[:-1], refs[-1]
    width = target.shape[1] // (len(sources) * pieces)
    for o, source in enumerate(sources):
        for y in range(pieces):
            first = (o * pieces + y) * width
            target[:, first : first + width] = source[0, y ^ shift[1]]


def weights_in_order(parts, fsdp_index, y_index):
    count, pieces, rows, width = parts[0].shape
    total = len(parts) * pieces * width
    where = jnp.stack([fsdp_index, y_index]).astype(jnp.int32)

    def body(shift, *refs):
        gather_order_kernel(pieces, shift, *refs)

    return pl.pallas_call(
        body,
        grid_spec=pltpu.PrefetchScalarGridSpec(
            num_scalar_prefetch=1,
            grid=(count,),
            in_specs=[
                pl.BlockSpec((1, pieces, rows, width), lambda j, s: (j ^ s[0], 0, 0, 0))
                for _ in parts
            ],
            out_specs=pl.BlockSpec((rows, total), lambda j, s: (j, 0)),
        ),
        out_shape=jax.ShapeDtypeStruct((count * rows, total), parts[0].dtype),
        compiler_params=params(),
    )(where, *parts)


def rows_by_distance(value, orders, pieces, fsdp_index, y_index):
    count = axis_size(FSDP)
    rows, width = value.shape[0] // (count * pieces), value.shape[1]
    share = width // orders
    if rows % 16:
        view = value.reshape(count, pieces, rows, orders, share)
        view = jnp.take(view, jnp.arange(count) ^ fsdp_index, axis=0)
        view = jnp.take(view, jnp.arange(pieces) ^ y_index, axis=1)
        return [view[:, :, :, o] for o in range(orders)]
    where = jnp.stack([fsdp_index, y_index]).astype(jnp.int32)

    def body(shift, source, *targets):
        for o, target in enumerate(targets):
            target[0, 0] = source[:, o * share : (o + 1) * share]

    return pl.pallas_call(
        body,
        grid_spec=pltpu.PrefetchScalarGridSpec(
            num_scalar_prefetch=1,
            grid=(count, pieces),
            in_specs=[
                pl.BlockSpec(
                    (rows, width),
                    lambda j, y, s: ((j ^ s[0]) * pieces + (y ^ s[1]), 0),
                )
            ],
            out_specs=[
                pl.BlockSpec((1, 1, rows, share), lambda j, y, s: (j, y, 0, 0))
            ]
            * orders,
        ),
        out_shape=[
            jax.ShapeDtypeStruct((count, pieces, rows, share), value.dtype)
        ]
        * orders,
        compiler_params=params(),
    )(where, value)


def columns_in_order(value, shift):
    count, rows, width = value.shape
    if width % 128:
        ordered = jnp.take(value, jnp.arange(count) ^ shift, axis=0)
        return jnp.moveaxis(ordered, 0, 1).reshape(rows, count * width)
    return pl.pallas_call(
        lambda s, source, target: copy_kernel(source, target),
        grid_spec=pltpu.PrefetchScalarGridSpec(
            num_scalar_prefetch=1,
            grid=(count,),
            in_specs=[pl.BlockSpec((1, rows, width), lambda j, s: (j ^ s[0], 0, 0))],
            out_specs=pl.BlockSpec((rows, width), lambda j, s: (0, j)),
        ),
        out_shape=jax.ShapeDtypeStruct((rows, count * width), value.dtype),
        compiler_params=params(),
    )(shift.reshape(1).astype(jnp.int32), value)


def columns_by_distance(value, count, shift):
    rows, width = value.shape[0], value.shape[1] // count
    if width % 128:
        blocks = jnp.moveaxis(value.reshape(rows, count, width), 1, 0)
        return jnp.take(blocks, jnp.arange(count) ^ shift, axis=0)
    return pl.pallas_call(
        lambda s, source, target: copy_kernel(source, target),
        grid_spec=pltpu.PrefetchScalarGridSpec(
            num_scalar_prefetch=1,
            grid=(count,),
            in_specs=[pl.BlockSpec((rows, width), lambda j, s: (0, j ^ s[0]))],
            out_specs=pl.BlockSpec((1, rows, width), lambda j, s: (j, 0, 0)),
        ),
        out_shape=jax.ShapeDtypeStruct((count, rows, width), value.dtype),
        compiler_params=params(),
    )(shift.reshape(1).astype(jnp.int32), value)


def keep_head(value, head, head_size):
    lane = lax.broadcasted_iota(jnp.int32, (1, value.shape[1]), 1)
    return jnp.where(lane // head_size == head, value, jnp.zeros_like(value))


def attend_kernel(head_size, chunk, query, keys, values, out, tops, inverses):
    length, width = keys.shape
    scale = jnp.asarray(head_size**-0.5, BF)
    for h in range(width // head_size):
        own_keys = keep_head(keys[...], h, head_size) * scale
        own_values = keep_head(values[...], h, head_size)
        for i in range(length // chunk):
            rows = pl.ds(i * chunk, chunk)
            scores = dot(own_keys, query[rows, :], NT)
            top = jnp.max(scores, axis=0, keepdims=True)
            exponent = jnp.exp(scores - top)
            inverse = 1.0 / jnp.sum(exponent, axis=0, keepdims=True)
            part = dot((exponent * inverse).astype(BF), own_values, TN)
            if h == 0:
                out[rows, :] = part.astype(BF)
            else:
                out[rows, :] = (out[rows, :].astype(F32) + part).astype(BF)
            tops[0, h : h + 1, rows] = top
            inverses[0, h : h + 1, rows] = inverse


def attend(query, keys, values, head_size):
    length, width = query.shape
    block = min(128, width)
    wide = pl.BlockSpec((length, block), lambda h: (0, h))
    flat = pl.BlockSpec((1, block // head_size, length), lambda h: (h, 0, 0))
    stats = jax.ShapeDtypeStruct((width // block, block // head_size, length), F32)
    return pl.pallas_call(
        functools.partial(attend_kernel, head_size, min(512, length)),
        grid=(width // block,),
        in_specs=[wide] * 3,
        out_specs=[wide, flat, flat],
        out_shape=[jax.ShapeDtypeStruct((length, width), BF), stats, stats],
        compiler_params=params(),
    )(query, keys, values)


def attend_back_kernel(
    head_size, chunk, query, keys, values, grad, tops, inverses, d_query, d_keys, d_values
):
    length, width = keys.shape
    scale = jnp.asarray(head_size**-0.5, BF)
    for h in range(width // head_size):
        own_keys = keep_head(keys[...], h, head_size) * scale
        own_values = keep_head(values[...], h, head_size)
        for i in range(length // chunk):
            rows = pl.ds(i * chunk, chunk)
            query_rows, grad_rows = query[rows, :], grad[rows, :]
            scores = dot(own_keys, query_rows, NT)
            probs = jnp.exp(scores - tops[0, h : h + 1, rows]) * inverses[0, h : h + 1, rows]
            d_probs = dot(own_values, grad_rows, NT)
            delta = jnp.sum(probs * d_probs, axis=0, keepdims=True)
            d_scores = (probs * (d_probs - delta)).astype(BF)
            value_part = dot(probs.astype(BF), keep_head(grad_rows, h, head_size), NN)
            key_part = dot(d_scores, keep_head(query_rows, h, head_size) * scale, NN)
            query_part = dot(d_scores, own_keys, TN)
            if h == 0 and i == 0:
                d_values[...] = value_part
                d_keys[...] = key_part
            else:
                d_values[...] += value_part
                d_keys[...] += key_part
            if h == 0:
                d_query[rows, :] = query_part
            else:
                d_query[rows, :] += query_part


def attend_back(query, keys, values, grad, tops, inverses, head_size):
    length, width = query.shape
    block = min(128, width)
    wide = pl.BlockSpec((length, block), lambda h: (0, h))
    flat = pl.BlockSpec((1, block // head_size, length), lambda h: (h, 0, 0))
    return pl.pallas_call(
        functools.partial(attend_back_kernel, head_size, min(512, length)),
        grid=(width // block,),
        in_specs=[wide] * 4 + [flat] * 2,
        out_specs=[wide] * 3,
        out_shape=[jax.ShapeDtypeStruct((length, width), F32)] * 3,
        compiler_params=params(),
    )(query, keys, values, grad, tops, inverses)


def rotary_table(head_size):
    half = head_size // 2
    pair = np.arange(half)
    bands = (half + 2) // 3
    frequency = np.power(np.float32(ROPE_BASE), -(pair // 3).astype(np.float32) / bands)
    angles = np.arange(GRID_SIDE, dtype=np.float32)[:, None] * frequency[None, :]
    chosen = (pair % 3)[None, None, :] == np.arange(3)[:, None, None]

    def table(of):
        return np.where(chosen, of[None], 0.0).reshape(3 * GRID_SIDE, half)

    cosine, sine = table(np.cos(angles)), table(np.sin(angles))
    return np.concatenate([cosine, cosine, -sine, sine], axis=1).astype(np.float32)


def rotary_rows(coords, head_size):
    cells = jnp.arange(GRID_SIDE)
    hot = (coords[:, :, None] == cells).astype(F32)
    hot = jnp.transpose(hot, (1, 0, 2)).reshape(coords.shape[1], 3 * GRID_SIDE)
    both = jnp.dot(hot, rotary_table(head_size), precision=lax.Precision.HIGHEST)
    return both[:, :head_size], both[:, head_size:]


def half_swap(values, head_size):
    length, width = values.shape
    halves = values.reshape(length, width // head_size, 2, head_size // 2)
    return halves[:, :, ::-1, :].reshape(length, width)


def turn(values, cosine, sine, head_size):
    repeats = values.shape[1] // head_size
    return values * jnp.tile(cosine, (1, repeats)) + half_swap(values, head_size) * jnp.tile(
        sine, (1, repeats)
    )


def normalise(values):
    row_mean = jnp.mean(values, axis=-1, keepdims=True)
    centred = values - row_mean
    row_var = jnp.mean(centred * centred, axis=-1, keepdims=True)
    inverse = lax.rsqrt(row_var + EPSILON)
    return centred * inverse, inverse


def norm_back(unit, inverse, d_unit):
    return inverse * (
        d_unit
        - jnp.mean(d_unit, axis=-1, keepdims=True)
        - unit * jnp.mean(d_unit * unit, axis=-1, keepdims=True)
    )


def gelu_exact(values_in):
    return jax.nn.gelu(values_in, approximate=False)


def general_device(
    block_input,
    out_cotangent,
    positions,
    w_qkv,
    w_out,
    w_up,
    w_down,
    norm_gains,
    norm_shifts,
    qkv_bias,
    proj_bias,
    up_bias,
    clip_threshold,
):
    clips, tokens, width = block_input.shape
    fsdp, seq = axis_size(FSDP), axis_size(SEQ)
    outer = seq // 2
    head_size = width // HEADS
    group = width // seq
    hidden = up_bias.shape[0]
    share = hidden // (fsdp * seq)
    length = tokens * seq
    f = lax.axis_index(FSDP)
    s = lax.axis_index(SEQ)
    y, c = s // 2, s % 2

    def along_seq(value):
        rows = gather_dim(value, "y", 0)
        return gather_dim(rows, "core", 1).reshape((seq,) + value.shape)

    x_all = [along_seq(block_input[i]).reshape(length, width) for i in range(clips)]
    coords_all = jnp.moveaxis(along_seq(positions), 0, 2).reshape(3, clips, length)

    own_heads = lax.dynamic_index_in_dim(
        w_qkv.reshape(-1, 3, seq, group), s, 2, keepdims=False
    ).reshape(-1, 3 * group)
    halves = []
    for o, order in enumerate(("zx", "xz")):
        piece = own_heads[:, o * (3 * group // 2) : (o + 1) * (3 * group // 2)]
        shape = (fsdp, 1) + piece.shape
        if order == "zx":
            piece = gather_dim(gather_dim(piece, "z", 0), "x", 1)
        else:
            piece = gather_dim(gather_dim(piece, "x", 0), "z", 0)
        halves.append(piece.reshape(shape))
    full_qkv = weights_in_order(halves, f, jnp.zeros_like(f))

    def gathered(local):
        rows, columns = local.shape
        part = columns // (2 * outer)
        views = local.reshape(rows, 2, outer, part)
        parts = []
        for o, order in enumerate(("zxy", "zyx")):
            piece = lax.dynamic_index_in_dim(views[:, o], y, 1, keepdims=False)
            piece = gather_dim(piece, "z", 0)
            if order == "zxy":
                piece = gather_dim(gather_dim(piece, "x", 1), "y", 2)
            else:
                piece = gather_dim(gather_dim(piece, "y", 1), "x", 1)
            parts.append(piece.reshape(fsdp, outer, rows, part))
        return weights_in_order(parts, f, y)

    def summed(partial):
        parts = rows_by_distance(partial, 2, outer, f, y)
        sums = []
        for order, part in zip(("yxz", "xyz"), parts, strict=True):
            value = part.reshape((fsdp // 2, 2) + part.shape[1:])
            if order == "yxz":
                value = scatter_dim(scatter_dim(value, "y", 2, False), "x", 1, False)
            else:
                value = scatter_dim(scatter_dim(value, "x", 1, False), "y", 1, False)
            sums.append(scatter_dim(value, "z", 0, True))
        return jnp.concatenate(sums, axis=1)

    def core_part(value, axis):
        shape = value.shape
        view = value.reshape(shape[:axis] + (-1, 2, share) + shape[axis + 1 :])
        view = lax.dynamic_index_in_dim(view, c, axis + 1, keepdims=False)
        return view.reshape(shape[:axis] + (shape[axis] // 2,) + shape[axis + 1 :])

    full_out = gathered(w_out)
    full_up = gathered(core_part(w_up, 1))
    full_down = gathered(core_part(w_down, 0))
    own_up_bias = core_part(up_bias, 0)

    own_bias = lax.dynamic_index_in_dim(qkv_bias.reshape(3, seq, group), s, 1, keepdims=False)
    kept = []
    attended_parts = []
    for i in range(clips):
        unit, inverse = normalise(x_all[i].astype(F32))
        normed = (unit * norm_gains[0] + norm_shifts[0]).astype(BF)
        mixed = dot(normed, full_qkv, NN) + own_bias.reshape(-1)
        cosine, sine = rotary_rows(coords_all[:, i], head_size)
        query = turn(mixed[:, :group], cosine, sine, head_size).astype(BF)
        keys = turn(mixed[:, group : 2 * group], cosine, sine, head_size).astype(BF)
        values = mixed[:, 2 * group :].astype(BF)
        attended, tops, inverses = attend(query, keys, values, head_size)
        kept.append((normed, query, keys, values, tops, inverses, cosine, sine))
        blocks = attended.reshape(seq, tokens, group)
        attended_parts.append(
            jnp.stack([blocks[0]] + [flip(blocks[m], SEQ, m) for m in range(1, seq)])
        )
    attended_own = columns_in_order(
        jnp.concatenate(attended_parts, axis=1), s
    )
    tops_own = functools.reduce(
        jnp.maximum, [jnp.max(k[4], axis=2).reshape(-1) for k in kept]
    )

    x_own = block_input.reshape(clips * tokens, width).astype(F32)
    g_own = out_cotangent.reshape(clips * tokens, width)
    resid1 = x_own + dot(attended_own, full_out, NN) + proj_bias[0]
    unit2, inverse2 = normalise(resid1)
    normed2 = (unit2 * norm_gains[1] + norm_shifts[1]).astype(BF)

    def pair(value):
        return jnp.concatenate([value, flip(value, SEQ, 1)], axis=0)

    def pair_sum(value):
        half = value.shape[0] // 2
        return value[:half] + flip(value[half:], SEQ, 1)

    normed2_chip = pair(normed2)
    g_chip = pair(g_own)
    hidden_pre = dot(normed2_chip, full_up, NN) + own_up_bias
    activated, gelu_pull = jax.vjp(gelu_exact, hidden_pre)
    activated = activated.astype(BF)
    block_out = (resid1 + pair_sum(dot(activated, full_down, NN)) + proj_bias[1]).astype(BF)

    grad_down = summed(dot(activated, g_chip, TN).astype(BF))
    d_hidden = gelu_pull(dot(g_chip, full_down, NT))[0].astype(BF)
    grad_up_half = summed(dot(normed2_chip, d_hidden, TN).astype(BF))
    up_bias_part = jnp.sum(d_hidden.astype(F32), axis=0)
    d_normed2 = pair_sum(dot(d_hidden, full_up, NT))
    gain2_part = jnp.sum(d_normed2 * unit2, axis=0)
    shift2_part = jnp.sum(d_normed2, axis=0)
    g_wide = g_own.astype(F32)
    down_bias_part = jnp.sum(g_wide, axis=0)
    d_resid1 = g_wide + norm_back(unit2, inverse2, d_normed2 * norm_gains[1])
    d_resid1_low = d_resid1.astype(BF)
    out_bias_part = jnp.sum(d_resid1_low.astype(F32), axis=0)

    d_attended = dot(d_resid1_low, full_out, NT).astype(BF)
    pieces = columns_by_distance(d_attended, seq, s).reshape(seq, clips, tokens, group)

    out_rows = dot(attended_own, d_resid1_low, TN).astype(BF)
    out_rows = out_rows.reshape(-1, 2, width // (fsdp * seq), width)
    mine = lax.dynamic_index_in_dim(out_rows, c, 1, keepdims=False)
    theirs = lax.dynamic_index_in_dim(out_rows, 1 - c, 1, keepdims=False)
    out_rows = (mine.astype(F32) + flip(theirs, SEQ, 1).astype(F32)).astype(BF)
    grad_out = summed(out_rows.reshape(-1, width))

    d_normed1_parts = []
    qkv_part = 0.0
    qkv_bias_part = 0.0
    gain1_part = 0.0
    shift1_part = 0.0
    for i in range(clips):
        normed, query, keys, values, tops, inverses, cosine, sine = kept[i]
        grad = jnp.concatenate(
            [pieces[0, i]] + [flip(pieces[m, i], SEQ, m) for m in range(1, seq)], axis=0
        )
        d_query, d_keys, d_values = attend_back(
            query, keys, values, grad, tops, inverses, head_size
        )
        d_mixed = jnp.concatenate(
            [
                turn(d_query, cosine, -sine, head_size),
                turn(d_keys, cosine, -sine, head_size),
                d_values,
            ],
            axis=1,
        ).astype(BF)
        qkv_part = qkv_part + dot(normed, d_mixed, TN)
        qkv_bias_part = qkv_bias_part + jnp.sum(d_mixed.astype(F32), axis=0)
        d_normed1 = dot(d_mixed, full_qkv, NT)
        unit, _ = normalise(x_all[i].astype(F32))
        gain1_part = gain1_part + jnp.sum(d_normed1 * unit, axis=0)
        shift1_part = shift1_part + jnp.sum(d_normed1, axis=0)
        d_normed1_parts.append(d_normed1.astype(BF))

    blocks = rows_by_distance(qkv_part.astype(BF), 2, 1, f, jnp.zeros_like(f))
    sums = []
    for order, part in zip(("xz", "zx"), blocks, strict=True):
        value = part.reshape((fsdp // 2, 2) + part.shape[2:])
        if order == "xz":
            value = scatter_dim(scatter_dim(value, "x", 1, False), "z", 0, True)
        else:
            value = scatter_dim(scatter_dim(value, "z", 0, False), "x", 0, True)
        sums.append(value)
    own_rows = jnp.concatenate(sums, axis=1).reshape(seq, -1, 3 * group)

    def rows_of(m):
        return lax.dynamic_index_in_dim(own_rows, s ^ m, 0, keepdims=False)

    arrived = jnp.stack([rows_of(0)] + [flip(rows_of(m), SEQ, m) for m in range(1, seq)])
    ordered = [
        lax.dynamic_index_in_dim(arrived, s ^ t, 0, keepdims=False).reshape(-1, 3, 1, group)
        for t in range(seq)
    ]
    grad_qkv = jnp.concatenate(ordered, axis=2).reshape(-1, 3 * width)

    halves = grad_up_half.reshape(2, -1, fsdp * outer, share)
    mine = lax.dynamic_index_in_dim(halves, c, 0, keepdims=False)
    other = flip(lax.dynamic_index_in_dim(halves, 1 - c, 0, keepdims=False), SEQ, 1)
    first = jnp.where(c == 0, mine, other)
    second = jnp.where(c == 0, other, mine)
    grad_up = jnp.stack([first, second], axis=2).reshape(-1, hidden)

    d_normed1 = jnp.stack([p.reshape(seq, tokens, width) for p in d_normed1_parts], axis=1)
    value = d_normed1.reshape((outer, 2) + d_normed1.shape[1:])
    value = scatter_dim(scatter_dim(value, "core", 1, False), "y", 0, True)
    unit1, inverse1 = normalise(x_own)
    d_unit1 = value.reshape(clips * tokens, width) * norm_gains[0]
    grad_input = (d_resid1 + norm_back(unit1, inverse1, d_unit1)).reshape(block_input.shape)

    qkv_slots = lax.dynamic_update_index_in_dim(
        jnp.zeros((3, seq, group), F32), qkv_bias_part.reshape(3, group), s, 1
    )
    up_slots = lax.dynamic_update_index_in_dim(
        jnp.zeros((fsdp * outer, 2, share), F32),
        up_bias_part.reshape(fsdp * outer, share),
        c,
        1,
    )
    devices = fsdp * seq
    rows = [
        gain1_part, gain2_part, shift1_part, shift2_part, out_bias_part, down_bias_part,
        qkv_slots.reshape(-1), up_slots.reshape(-1),
    ]
    rows = jnp.concatenate([r.reshape(devices, -1) for r in rows], axis=1)
    sums = lax.psum_scatter(rows, FSDP + SEQ, scatter_dimension=0, tiled=True)[0]
    one = width // devices
    grad_gains = sums[: 2 * one].reshape(2, one)
    grad_shifts = sums[2 * one : 4 * one].reshape(2, one)
    grad_proj_bias = sums[4 * one : 6 * one].reshape(2, one)
    grad_qkv_bias = sums[6 * one : 9 * one]
    grad_up_bias = sums[9 * one :]

    slots = jnp.full((seq, HEADS // seq), -jnp.inf, F32)
    slots = lax.dynamic_update_index_in_dim(slots, tops_own, s, 0)
    maxima = lax.pmax(slots.reshape(-1), FSDP + SEQ)
    threshold = clip_threshold[0]
    gamma = jnp.sqrt(threshold / jnp.maximum(maxima, threshold))
    columns = jnp.tile(jnp.repeat(gamma, head_size), 2)
    clipped = w_qkv[:, : 2 * width].astype(F32) * columns
    clipped_bias = qkv_bias[: 2 * width] * columns
    return (
        block_out.reshape(block_input.shape),
        grad_input,
        grad_qkv,
        grad_out,
        grad_up,
        grad_down,
        grad_gains,
        grad_shifts,
        grad_qkv_bias,
        grad_proj_bias,
        grad_up_bias,
        maxima,
        clipped,
        clipped_bias,
    )


def flip_one(value, name):
    return lax.ppermute(value, name, [(0, 1), (1, 0)])


def after(value, *others):
    return lax.optimization_barrier((value, *others))[0]


def after_all(values, *others):
    return lax.optimization_barrier((tuple(values), *others))[0]


def add_low(*terms):
    return functools.reduce(jnp.add, [t.astype(F32) for t in terms]).astype(BF)


def cost(microseconds):
    return pl.CostEstimate(
        flops=int(microseconds * 1e3), bytes_accessed=1 << 10, transcendentals=0
    )


ANYWHERE = pl.BlockSpec(memory_space=pl.ANY)


def loads(sems, first, pairs):
    return [
        pltpu.make_async_copy(source, target, sems.at[first + i])
        for i, (source, target) in enumerate(pairs)
    ]


def start(copies):
    for one in copies:
        one.start()


def wait(copies):
    for one in copies:
        one.wait()


def by_rows(where_x, near, beside, target):
    levels, rows = near.shape[:2]
    pairs = []
    for z in range(levels):
        for far_x, part in enumerate((near, beside)):
            first = pl.multiple_of((z * 2 + (where_x ^ far_x)) * rows, rows)
            pairs.append((part.at[z], target.at[pl.ds(first, rows)]))
    return pairs


def whole(shape):
    return pl.BlockSpec(shape, lambda *_: (0,) * len(shape))


def in_order(index, bit, axis):
    return jnp.where(bit == 0, index, jnp.flip(index, axis))


def swap_halves(values, head_size):
    half = head_size // 2
    lane = lax.broadcasted_iota(jnp.int32, (1, values.shape[1]), 1)
    width = values.shape[1]
    return jnp.where(
        lane % head_size < half,
        pltpu.roll(values, width - half, 1),
        pltpu.roll(values, half, 1),
    )


def first_norm_kernel(first, second, gain, shift, normed, unit):
    tokens = first.shape[0]
    for i, part in enumerate((first, second)):
        value, _ = normalise(part[...].astype(F32))
        here = slice(i * tokens, (i + 1) * tokens)
        unit[0, here, :] = value.astype(BF)
        normed[0, here, :] = (value * gain[...] + shift[...]).astype(BF)


def first_norm(first, second, gain, shift, clips):
    width = first.shape[1]
    tokens = first.shape[0] // (8 * clips) * 8
    block = pl.BlockSpec((tokens, width), lambda i: (i, 0))
    out = pl.BlockSpec((1, 2 * tokens, width), lambda i: (i, 0, 0))
    return pl.pallas_call(
        first_norm_kernel,
        grid=(clips,),
        in_specs=[block, block, whole((1, width)), whole((1, width))],
        out_specs=[out, out],
        out_shape=[jax.ShapeDtypeStruct((clips, 2 * tokens, width), BF)] * 2,
        compiler_params=params(),
        cost_estimate=cost(4),
        name="first_norm",
    )(first, second, gain, shift)


def prepare_kernel(where, *refs):
    pieces, refs = refs[:6], refs[6:]
    out, x, spots, first, second, x_ext = refs
    lanes = pieces[0].shape[1]
    for z in range(first.shape[0]):
        for k in range(3):
            first[z, :, k * lanes : (k + 1) * lanes] = pieces[k][...]
    for k in range(3):
        second[:, k * lanes : (k + 1) * lanes] = pieces[3 + k][...]
    rest = second.shape[1] - out.shape[1]
    second[:, 3 * lanes : rest] = jnp.zeros_like(second[:, 3 * lanes : rest])
    second[:, rest:] = out[...]
    tokens = x.shape[0]
    x_ext[:tokens] = x[...]
    x_ext[tokens:] = spots[...]


def prepare(where, w_qkv, w_out, x, spots, levels, lanes):
    rows, width = w_out.shape
    tokens = x.shape[0]
    groups = width // (4 * lanes)
    blocks = [
        pl.BlockSpec(
            (rows, lanes),
            lambda i, w, part=part, h=h: (0, (part * 4 + w[3]) * groups + h),
        )
        for h in range(groups)
        for part in range(3)
    ]
    return pl.pallas_call(
        prepare_kernel,
        grid_spec=pltpu.PrefetchScalarGridSpec(
            num_scalar_prefetch=1,
            grid=(1,),
            in_specs=blocks
            + [
                pl.BlockSpec((rows, width // 2), lambda i, w: (0, w[2])),
                whole(x.shape),
                whole(spots.shape),
            ],
            out_specs=[
                whole((levels, rows, 3 * lanes)),
                whole((rows, width)),
                whole((tokens + 8, width)),
            ],
        ),
        out_shape=[
            jax.ShapeDtypeStruct((levels, rows, 3 * lanes), BF),
            jax.ShapeDtypeStruct((rows, width), BF),
            jax.ShapeDtypeStruct((tokens + 8, width), BF),
        ],
        compiler_params=params(),
        cost_estimate=cost(3),
        name="prepare",
    )(where, *[w_qkv] * len(blocks), w_out, x, spots)


def own_columns(where, value, count, share):
    rows = value.shape[0]
    return pl.pallas_call(
        lambda w, source, target: copy_kernel(source, target),
        grid_spec=pltpu.PrefetchScalarGridSpec(
            num_scalar_prefetch=1,
            grid=(count,),
            in_specs=[
                pl.BlockSpec((rows, share), lambda k, w: (0, (k * 2 + w[1]) * 2 + w[2]))
            ],
            out_specs=pl.BlockSpec((rows, share), lambda k, w: (0, k)),
        ),
        out_shape=jax.ShapeDtypeStruct((rows, count * share), value.dtype),
        compiler_params=params(),
        cost_estimate=cost(3),
        name="own_columns",
    )(where, value)


def rotary_parts(head_size, lanes):
    half = 2 * head_size // 2
    table = rotary_table(head_size)
    repeats = lanes // head_size
    table = np.concatenate([np.tile(table[:, :half], (1, repeats)), np.tile(table[:, half:], (1, repeats))], axis=1)
    parts = []
    for _ in range(3):
        parts.append(table.astype(BF))
        table = table - parts[-1].astype(np.float32)
    return np.concatenate(parts, axis=0)


def spots_of(clip, clips, spots, tokens):
    lines = []
    for part in spots:
        width = part.shape[1]
        line = []
        for a in range(3):
            first = a * clips * tokens
            column = first % width + clip * tokens
            row = first // width
            line.append(part[row : row + 1, pl.ds(pl.multiple_of(column, tokens), tokens)])
        lines.append(jnp.concatenate(line, axis=0))
    return jnp.concatenate(lines, axis=1).astype(F32)


def rotary_of(coords, table):
    cells = lax.broadcasted_iota(jnp.int32, (GRID_SIDE, coords.shape[1]), 0).astype(F32)
    hot = [(coords[a : a + 1] == cells).astype(F32) for a in range(3)]
    hot = jnp.concatenate(hot * 3, axis=0).astype(BF)
    width = table.shape[1] // 2
    both = dot(hot, table[...], TN)
    return both[:, :width], both[:, width:]


def heads_forward_kernel(
    head_size, blocks, where, first_rows, last_rows, near, beside, bias, table, *refs
):
    spots, refs = refs[:blocks], refs[blocks:]
    extra, refs = refs[: (len(refs) - 7) // 2], refs[(len(refs) - 7) // 2 :]
    query, keys, values, out, tops, inverses, *extra_out, weights = refs
    levels, rows, width = near.shape
    length, lanes = query.shape[1:]
    spots = spots_of(pl.program_id(0), pl.num_programs(0), spots, length // blocks)
    cosine, sine = rotary_of(spots, table)

    @pl.when(pl.program_id(0) == 0)
    def _():
        for z in range(levels):
            for part, bit in ((near, 0), (beside, 1)):
                first = (z * 2 + (where[0] ^ bit)) * rows
                weights[pl.ds(pl.multiple_of(first, rows), rows), :] = part[z]
        for source, target in zip(extra, extra_out, strict=True):
            target[...] = source[...]

    mixed = [dot(part[0], weights[...], NN) + bias[...] for part in (first_rows, last_rows)]
    mixed = jnp.concatenate(mixed, axis=0)
    turned = [
        part * cosine + swap_halves(part, head_size) * sine
        for part in (mixed[:, :lanes], mixed[:, lanes : 2 * lanes])
    ]
    query[0], keys[0] = turned[0].astype(BF), turned[1].astype(BF)
    values[0] = mixed[:, 2 * lanes :].astype(BF)
    scale = jnp.asarray(head_size**-0.5, BF)
    chunk = length // 2
    tokens = length // blocks
    for i in range(2):
        rows_here = pl.ds(i * chunk, chunk)
        query_rows = query[0, rows_here, :]
        total = None
        for h in range(lanes // head_size):
            own_keys = keep_head(keys[0], h, head_size) * scale
            own_values = keep_head(values[0], h, head_size)
            scores = dot(own_keys, query_rows, NT)
            top = jnp.max(scores, axis=0, keepdims=True)
            exponent = jnp.exp(scores - top)
            inverse = 1.0 / jnp.sum(exponent, axis=0, keepdims=True)
            part = dot((exponent * inverse).astype(BF), own_values, TN)
            total = part if total is None else total + part
            tops[0, h : h + 1, rows_here] = top
            inverses[0, h : h + 1, rows_here] = inverse
        low = total.astype(BF)
        for b in range(blocks // 2):
            out[i * (blocks // 2) + b, 0] = low[b * tokens : (b + 1) * tokens]


def spot_block(x):
    return pl.BlockSpec((8, x.shape[1]), lambda i, w: (x.shape[0] // 8 - 1, 0))


def heads_forward(where, normed, near, beside, bias, table, x_blocks, blocks, head_size, *extra):
    clips, half, width = normed[0].shape
    length = 2 * half
    lanes = bias.shape[1] // 3
    pieces = near.shape[:2] + bias.shape[1:]
    second = [e.shape[:2] + (e.shape[2] // 2,) for e in extra]
    clip = lambda *rest: pl.BlockSpec((1,) + rest, lambda i, w: (i,) + (0,) * len(rest))
    head = jax.ShapeDtypeStruct((clips, length, lanes), BF)
    stats = jax.ShapeDtypeStruct((clips, lanes // head_size, length), F32)
    return pl.pallas_call(
        functools.partial(heads_forward_kernel, head_size, blocks),
        grid_spec=pltpu.PrefetchScalarGridSpec(
            num_scalar_prefetch=1,
            grid=(clips,),
            in_specs=[
                clip(half, width),
                clip(half, width),
                whole(pieces),
                whole(pieces),
                whole(bias.shape),
                whole(table.shape),
            ]
            + [spot_block(x) for x in x_blocks]
            + [pl.BlockSpec(shape, lambda i, w: (0, 0, 1)) for shape in second],
            out_specs=[clip(length, lanes)] * 3
            + [
                pl.BlockSpec(
                    (blocks, 1, length // blocks, lanes), lambda i, w: (0, i, 0, 0)
                )
            ]
            + [clip(lanes // head_size, length)] * 2
            + [whole(shape) for shape in second],
            scratch_shapes=[pltpu.VMEM((width, 3 * lanes), BF)],
        ),
        out_shape=[
            head,
            head,
            head,
            jax.ShapeDtypeStruct((blocks, clips, length // blocks, lanes), BF),
            stats,
            stats,
        ]
        + [jax.ShapeDtypeStruct(shape, BF) for shape in second],
        compiler_params=params(),
        cost_estimate=cost(15),
        name="heads_forward",
    )(where, *normed, near, beside, bias, table, *x_blocks, *extra)


def out_row(z, x, where, rows):
    index = z * 2 + x
    return ((((index // 2) ^ where[3]) * 2) + index % 2) * rows


def put_out_weights(where, own, other, weights):
    levels, rows, share = own[0].shape
    for core, parts in ((0, own), (1, other)):
        column = (where[2] ^ core) * share
        column = pl.ds(pl.multiple_of(column, share), share)
        for far_x, part in enumerate(parts):
            for z in range(levels):
                place = out_row(z, where[0] ^ far_x, where, rows)
                place = pl.ds(pl.multiple_of(place, rows), rows)
                weights[place, column] = part[z]


def project_kernel(where, *refs, groups):
    pieces, refs = refs[: 4 * groups], refs[4 * groups :]
    x_blocks, refs = refs[:4], refs[4:]
    own, other, (bias, gain, shift, *refs) = refs[:2], refs[2:4], refs[4:]
    resid, attended, normed, weights_out, weights, joined, held, kept, sems = refs
    step = pl.program_id(0)
    clips, tokens, lanes = pieces[0].shape[1:]
    rows, width = clips * tokens, weights.shape[1]
    per = 4 * groups + 1
    copies = []
    for b in range(4):
        pairs = [(x_blocks[b].at[pl.ds(0, rows)], held.at[b])]
        for h in range(groups):
            for m in range(4):
                column = pl.ds((m * groups + h) * lanes, lanes)
                pairs.append((pieces[h * 4 + m].at[b ^ m], joined.at[b, :, :, column]))
        copies.append(loads(sems, b * per, pairs))
    save = loads(sems, 4 * per, [(weights, weights_out), (kept, resid)])

    @pl.when(step == 0)
    def _():
        for group in copies:
            start(group)
        put_out_weights(where, own, other, weights)
        save[0].start()

    for b in range(4):

        @pl.when(step == b)
        def _(b=b):
            wait(copies[b])

    mixed = joined[step].reshape(rows, width)
    out = held[step].astype(F32) + dot(mixed, weights[...], NN) + bias[...]
    unit, _ = normalise(out)
    normed[...] = (unit * gain[...] + shift[...]).astype(BF)

    @pl.when(step == 0)
    def _():
        kept[...] = out
        attended[...] = mixed
        save[1].start()

    @pl.when(step == 3)
    def _():
        wait(save)


def project(where, pieces, x_blocks, own, other, bias, gain, shift):
    clips, tokens, lanes = pieces[0][0].shape[1:]
    rows, width = clips * tokens, x_blocks[0].shape[1]
    groups = len(pieces)
    return pl.pallas_call(
        functools.partial(project_kernel, groups=groups),
        grid_spec=pltpu.PrefetchScalarGridSpec(
            num_scalar_prefetch=1,
            grid=(4,),
            in_specs=[ANYWHERE] * (4 * groups + 4)
            + [whole(own[0].shape)] * 4
            + [whole((1, width))] * 3,
            out_specs=[
                ANYWHERE,
                whole((rows, width)),
                pl.BlockSpec((rows, width), lambda t, w: (t, 0)),
                ANYWHERE,
            ],
            scratch_shapes=[
                pltpu.VMEM((width, width), BF),
                pltpu.VMEM((4, clips, tokens, width), BF),
                pltpu.VMEM((4, rows, width), BF),
                pltpu.VMEM((rows, width), F32),
                pltpu.SemaphoreType.DMA((4 * (4 * groups + 1) + 2,)),
            ],
        ),
        out_shape=[
            jax.ShapeDtypeStruct((rows, width), F32),
            jax.ShapeDtypeStruct((rows, width), BF),
            jax.ShapeDtypeStruct((4 * rows, width), BF),
            jax.ShapeDtypeStruct((width, width), BF),
        ],
        compiler_params=params(),
        cost_estimate=cost(13),
        name="project_out",
    )(where, *(p for group in pieces for p in group), *x_blocks, *own, *other, bias, gain, shift)


def gelu_pair(values):
    cumulative = 0.5 * (1.0 + lax.erf(values * np.float32(0.5**0.5)))
    density = jnp.exp(-0.5 * values * values) * np.float32((2.0 * np.pi) ** -0.5)
    return values * cumulative, cumulative + values * density


def up_kernel(where, normed, near, beside, bias, *refs):
    grads, refs = refs[:4], refs[4:]
    activated, slope, near_out, beside_out, rows_held, columns, held, low, sems = refs
    levels = near.shape[0]
    block = activated.shape[1]
    share = block // 2
    step = pl.program_id(0)
    tokens = grads[0].shape[0]
    here = [pl.ds(i * tokens, tokens) for i in range(4)]
    weight_copies = loads(sems, 0, by_rows(where[0], near, beside, columns))
    count = len(weight_copies)
    row_copies = loads(sems, count, [(normed.at[h], rows_held.at[h]) for h in here])
    grad_copies = loads(sems, count + 4, [(g, held.at[h]) for g, h in zip(grads, here)])

    @pl.when(step == 0)
    def _():
        start(weight_copies)
        start(row_copies)
        start(grad_copies)
        wait(weight_copies)
        wait(row_copies)

    column = pl.ds(pl.multiple_of(step * block, block), block)
    for i in range(4):
        hidden = dot(rows_held[here[i], :], columns[:, column], NN) + bias[0]
        act, d_act = gelu_pair(hidden)
        activated[here[i], :] = act.astype(BF)
        slope[here[i], :] = d_act.astype(BF)

    @pl.when(step == 0)
    def _():
        wait(grad_copies)

    low[...] = dot(activated[...], held[...], TN).astype(BF)
    for far_x, out in enumerate((near_out, beside_out)):
        first = (where[0] ^ far_x) * share
        out[0] = low[pl.ds(pl.multiple_of(first, share), share), :]


def feed_up(where, normed, grads, pieces, bias):
    levels, rows, hidden = pieces[1].shape
    tokens, width = normed.shape
    block = hidden // levels
    line = pl.BlockSpec((tokens, block), lambda t, w: (0, t))
    out = pl.BlockSpec((1, block // 2, width), lambda t, w: (t, 0, 0))
    return pl.pallas_call(
        up_kernel,
        grid_spec=pltpu.PrefetchScalarGridSpec(
            num_scalar_prefetch=1,
            grid=(levels,),
            in_specs=[ANYWHERE] * 3
            + [pl.BlockSpec((1, 1, block), lambda t, w: (t, 0, 0))]
            + [ANYWHERE] * 4,
            out_specs=[line, line, out, out],
            scratch_shapes=[
                pltpu.VMEM((tokens, width), BF),
                pltpu.VMEM((width, hidden), BF),
                pltpu.VMEM((tokens, width), BF),
                pltpu.VMEM((block, width), BF),
                pltpu.SemaphoreType.DMA((2 * levels + 8,)),
            ],
        ),
        out_shape=[jax.ShapeDtypeStruct((tokens, hidden), BF)] * 2
        + [jax.ShapeDtypeStruct((levels, block // 2, width), BF)] * 2,
        compiler_params=params(),
        cost_estimate=cost(17),
        name="feed_up",
    )(where, normed, *pieces, bias, *grads)


def far_kernel(
    where, first_grad, last_grad, near, beside, up_near, up_beside, slope,
    first_back, last_back, d_hidden, grads, down, up, slopes, hidden, sems,
):
    step = pl.program_id(0)
    steps = pl.num_programs(0) - 1
    tokens = first_grad.shape[0]
    block = d_hidden.shape[1]
    pairs = [(first_grad, grads.at[pl.ds(0, tokens)]), (last_grad, grads.at[pl.ds(tokens, tokens)])]
    pairs += by_rows(where[0], near, beside, down)
    first_copies = loads(sems, 0, pairs)
    count = len(first_copies)
    columns = [pl.ds(k * block, block) for k in range(steps)]
    rows = pl.ds(2 * tokens, 2 * tokens)
    slope_copies = loads(sems, count, [(slope.at[rows, k], slopes.at[:, k]) for k in columns])
    up_copies = loads(sems, count + steps, by_rows(where[0], up_near, up_beside, up))

    @pl.when(step == 0)
    def _():
        start(first_copies)
        start(slope_copies)
        start(up_copies)
        wait(first_copies)

    for k in range(steps):

        @pl.when(step == k)
        def _(k=k):
            slope_copies[k].wait()

    @pl.when(step < steps)
    def _():
        place = pl.ds(pl.multiple_of(step * block, block), block)
        for i in range(2):
            here = slice(i * tokens, (i + 1) * tokens)
            d_act = dot(grads[here, :], down[place, :], NT)
            low = (d_act * slopes[here, place].astype(F32)).astype(BF)
            hidden[here, place] = low
            d_hidden[here, :] = low

    @pl.when(step == steps)
    def _():
        wait(up_copies)
        first_back[...] = dot(hidden[:tokens, :], up[...], NT).astype(BF)
        last_back[...] = dot(hidden[tokens:, :], up[...], NT).astype(BF)


def feed_down_far(where, grads, pieces, up_pieces, slope):
    levels, share, width = pieces[0].shape
    tokens = grads[0].shape[0]
    hidden = slope.shape[1]
    steps = 2
    block = hidden // steps
    return pl.pallas_call(
        far_kernel,
        grid_spec=pltpu.PrefetchScalarGridSpec(
            num_scalar_prefetch=1,
            grid=(steps + 1,),
            in_specs=[ANYWHERE] * 7,
            out_specs=[whole((tokens, width))] * 2
            + [pl.BlockSpec((2 * tokens, block), lambda t, w: (0, jnp.minimum(t, steps - 1)))],
            scratch_shapes=[
                pltpu.VMEM((2 * tokens, width), BF),
                pltpu.VMEM((hidden, width), BF),
                pltpu.VMEM((width, hidden), BF),
                pltpu.VMEM((2 * tokens, hidden), BF),
                pltpu.VMEM((2 * tokens, hidden), BF),
                pltpu.SemaphoreType.DMA((2 + 4 * levels + steps,)),
            ],
        ),
        out_shape=[
            jax.ShapeDtypeStruct((tokens, width), BF),
            jax.ShapeDtypeStruct((tokens, width), BF),
            jax.ShapeDtypeStruct((2 * tokens, hidden), BF),
        ],
        compiler_params=params(),
        cost_estimate=cost(8),
        name="feed_down_far",
    )(where, *grads, *pieces, *up_pieces, slope)


def near_kernel(
    where, normed, first_grad, last_grad, near, beside, up_near, up_beside, slope, far_hidden,
    activated, first_back, last_back, own_part, part1, part2, part3, sums, near_out, beside_out,
    grads, down, up, slopes, far, acts, rows_held, flipped, hidden, product, own_held, held, sems,
):
    step = pl.program_id(0)
    steps = 2
    levels, rows, block = near_out.shape
    tokens = first_grad.shape[0]
    pairs = [(first_grad, grads.at[pl.ds(0, tokens)]), (last_grad, grads.at[pl.ds(tokens, tokens)])]
    pairs += by_rows(where[0], near, beside, down)
    first_copies = loads(sems, 0, pairs)
    count = len(first_copies)
    columns = [pl.ds(k * block, block) for k in range(steps)]
    mine = pl.ds(0, 2 * tokens)
    pairs = [(slope.at[mine, k], slopes.at[:, k]) for k in columns]
    slope_copies = loads(sems, count, pairs)
    far_copies = loads(sems, count + 2, [(far_hidden.at[:, k], far.at[:, k]) for k in columns])
    rest = [(normed, rows_held), (activated, acts)]
    rest = loads(sems, count + 4, rest + by_rows(where[0], up_near, up_beside, up))
    count += 4 + len(rest)
    out_pairs = [(held.at[0], first_back), (held.at[1], last_back), (own_held, own_part)]
    out_pairs += [(held.at[2 + i], part) for i, part in enumerate((part1, part2, part3))]
    saves = loads(sems, count, out_pairs)

    @pl.when(step == 0)
    def _():
        start(first_copies)
        start(slope_copies[:1])
        start(rest[:1])
        start(far_copies[:1])
        start(slope_copies[1:])
        start(far_copies[1:])
        start(rest[2:])
        start(rest[1:2])
        wait(first_copies)

    for k in range(steps):

        @pl.when(step == k)
        def _(k=k):
            slope_copies[k].wait()

    @pl.when(step < steps)
    def _():
        place = pl.ds(pl.multiple_of(step * block, block), block)
        parts = []
        for i in range(2):
            here = slice(i * tokens, (i + 1) * tokens)
            d_act = dot(grads[here, :], down[place, :], NT)
            low = (d_act * slopes[here, place].astype(F32)).astype(BF)
            hidden[here, place] = low
            parts.append(low)

        @pl.when(step == 0)
        def _():
            rest[0].wait()
            for i in range(4):
                here = slice(i * tokens, (i + 1) * tokens)
                flipped[:, here] = rows_held[here, :].T
            far_copies[0].wait()

        @pl.when(step == 1)
        def _():
            far_copies[1].wait()

        parts.append(far[:, place])
        every = jnp.concatenate(parts, axis=0)
        sums[0] = jnp.sum(every.astype(F32), axis=0, keepdims=True)
        product[...] = dot(flipped[...], every, NN).astype(BF)
        for far_x, out in enumerate((near_out, beside_out)):
            for z in range(levels):
                first = (z * 2 + (where[0] ^ far_x)) * rows
                out[z] = product[pl.ds(pl.multiple_of(first, rows), rows), :]

    @pl.when(step == steps)
    def _():
        wait(rest[2:])
        for i in range(2):
            here = slice(i * tokens, (i + 1) * tokens)
            held[i] = dot(hidden[here, :], up[...], NT).astype(BF)
            saves[i].start()
        rest[1].wait()

    @pl.when(step == steps + 1)
    def _():
        own_held[...] = dot(acts[:tokens, :], down[...], NN)
        saves[2].start()
        held[2] = dot(acts[tokens : 2 * tokens, :], down[...], NN).astype(BF)
        saves[3].start()

    @pl.when(step == steps + 2)
    def _():
        for i in (1, 2):
            here = slice((1 + i) * tokens, (2 + i) * tokens)
            held[2 + i] = dot(acts[here, :], down[...], NN).astype(BF)
            saves[3 + i].start()
        wait(saves)


def feed_down_near(where, normed, grads, pieces, up_pieces, slope, far_hidden, activated):
    tokens, width = grads[0].shape
    levels, share, _ = pieces[0].shape
    hidden = slope.shape[1]
    steps = 2
    block = hidden // steps
    rows = width // (2 * levels)
    at = lambda t: jnp.minimum(t, steps - 1)
    out = pl.BlockSpec((levels, rows, block), lambda t, w: (0, 0, at(t)))
    return pl.pallas_call(
        near_kernel,
        grid_spec=pltpu.PrefetchScalarGridSpec(
            num_scalar_prefetch=1,
            grid=(steps + 3,),
            in_specs=[ANYWHERE] * 10,
            out_specs=[ANYWHERE] * 6
            + [pl.BlockSpec((1, 1, block), lambda t, w: (at(t), 0, 0)), out, out],
            scratch_shapes=[
                pltpu.VMEM((2 * tokens, width), BF),
                pltpu.VMEM((hidden, width), BF),
                pltpu.VMEM((width, hidden), BF),
                pltpu.VMEM((2 * tokens, hidden), BF),
                pltpu.VMEM((2 * tokens, hidden), BF),
                pltpu.VMEM((4 * tokens, hidden), BF),
                pltpu.VMEM((4 * tokens, width), BF),
                pltpu.VMEM((width, 4 * tokens), BF),
                pltpu.VMEM((2 * tokens, hidden), BF),
                pltpu.VMEM((width, block), BF),
                pltpu.VMEM((tokens, width), F32),
                pltpu.VMEM((5, tokens, width), BF),
                pltpu.SemaphoreType.DMA((2 + 4 * levels + 4 + 2 + 6,)),
            ],
        ),
        out_shape=[jax.ShapeDtypeStruct((tokens, width), BF)] * 2
        + [jax.ShapeDtypeStruct((tokens, width), kind) for kind in (F32, BF, BF, BF)]
        + [jax.ShapeDtypeStruct((steps, 1, block), F32)]
        + [jax.ShapeDtypeStruct((levels, rows, hidden), BF)] * 2,
        compiler_params=params(),
        cost_estimate=cost(12),
        name="feed_down_near",
    )(where, normed, *grads, *pieces, *up_pieces, slope, far_hidden, activated)


def norm_back_kernel(
    where, own, arrived, far, resid, grad, gain, weights, d_resid, d_low, *rest
):
    outs, sums = rest[:-1], rest[-1]
    d_normed = own[...].astype(F32) + arrived[...].astype(F32) + far[...].astype(F32)
    unit, inverse = normalise(resid[...])
    wide = grad[...].astype(F32)
    out = wide + norm_back(unit, inverse, d_normed * gain[...])
    low = out.astype(BF)
    d_resid[...] = out
    d_low[...] = low
    parts = [d_normed * unit, d_normed, low.astype(F32), wide]
    parts = [jnp.sum(p, axis=0, keepdims=True) for p in parts]
    parts = jnp.concatenate(parts + [jnp.zeros_like(parts[0])] * 4, axis=0)

    @pl.when(pl.program_id(0) == 0)
    def _():
        sums[...] = parts

    @pl.when(pl.program_id(0) > 0)
    def _():
        sums[...] += parts

    d_attended = dot(low, weights[...], NT).astype(BF)
    for m, out in enumerate(outs):
        for h in range(out.shape[0]):
            lanes = out.shape[2]
            first = (m * out.shape[0] + h) * lanes
            out[h] = d_attended[:, first : first + lanes]


def second_norm_back(where, own, arrived, far, resid, grad, gain, weights, seq, groups):
    rows, width = resid.shape
    step = rows // 2
    lanes = width // (seq * groups)
    line = pl.BlockSpec((step, width), lambda i, w: (i, 0))
    return pl.pallas_call(
        norm_back_kernel,
        grid_spec=pltpu.PrefetchScalarGridSpec(
            num_scalar_prefetch=1,
            grid=(rows // step,),
            in_specs=[line] * 5 + [whole((1, width)), whole((width, width))],
            out_specs=[line, line]
            + [pl.BlockSpec((groups, step, lanes), lambda i, w: (0, i, 0))] * seq
            + [whole((8, width))],
        ),
        out_shape=[
            jax.ShapeDtypeStruct((rows, width), F32),
            jax.ShapeDtypeStruct((rows, width), BF),
        ]
        + [jax.ShapeDtypeStruct((groups, rows, lanes), BF)] * seq
        + [jax.ShapeDtypeStruct((8, width), F32)],
        compiler_params=params(),
        cost_estimate=cost(8),
        name="second_norm_back",
    )(where, own, arrived, far, resid, grad, gain, weights)


def out_grad_kernel(where, attended, grad, near, beside, product):
    product[...] = dot(attended[...], grad[...], TN).astype(BF)
    levels, _, _, lanes = near.shape[1:]
    rows = near.shape[3] * lanes // product.shape[1]
    for m in range(4):
        out = (near, beside)[m % 2]
        for far_x in range(2):
            for z in range(levels):
                first = out_row(z, where[0] ^ far_x, where, 4 * rows) + (where[3] ^ m) * rows
                here = pl.ds(pl.multiple_of(first, rows), rows)
                for k in range(product.shape[1] // lanes):
                    out[m // 2, z, far_x, k * rows : (k + 1) * rows, :] = product[
                        here, k * lanes : (k + 1) * lanes
                    ]


def out_grad(where, attended, grad, levels, lanes):
    width = grad.shape[1]
    shape = (2, levels, 2, width // (8 * levels) * (width // lanes), lanes)
    return pl.pallas_call(
        out_grad_kernel,
        grid_spec=pltpu.PrefetchScalarGridSpec(
            num_scalar_prefetch=1,
            grid=(1,),
            in_specs=[whole(attended.shape), whole(grad.shape)],
            out_specs=[whole(shape)] * 2,
            scratch_shapes=[pltpu.VMEM((width, width), BF)],
        ),
        out_shape=[jax.ShapeDtypeStruct(shape, BF)] * 2,
        compiler_params=params(),
        cost_estimate=cost(4),
        name="out_grad",
    )(where, attended, grad)


def heads_back_kernel(
    head_size, blocks, last, where, *refs
):
    pieces, refs = refs[:blocks], refs[blocks:]
    (query, keys, values, tops, inverses, table, *refs) = refs
    spots, (first_rows, last_rows, *rest) = refs[:blocks], refs[blocks:]
    *rest, rows_held, sems = rest
    if last:
        *rest, unit_held = rest
        near0, near1, beside0, beside1, earlier, first_unit, last_unit, *rest = rest
        norm_sums2, up_line, tops_row, earlier_sum, *rest = rest
        sent_back, sent_beside, near_grad, beside_grad, *rest = rest
        weights, joined, vectors, norm_sums, bias_sum, total, d_keys, d_values, grads = rest
    else:
        sent_back, near_grad, bias_sum, *rest = rest
        total, d_keys, d_values, grads = rest
    levels, rows = near_grad.shape[0], near_grad.shape[-1]
    length, lanes = query.shape[1:]
    three = 3 * lanes
    tokens = length // blocks
    clip = pl.program_id(0)

    half = length // 2
    pairs = []
    for i, part in enumerate((first_rows, last_rows)):
        pairs.append((part.at[clip], rows_held.at[pl.ds(i * half, half)]))
    if last:
        for i, part in enumerate((first_unit, last_unit)):
            pairs.append((part.at[clip], unit_held.at[pl.ds(i * half, half)]))
        pairs.append((earlier.at[clip], joined.at[:, pl.ds(0, three)]))
    copies = [pltpu.make_async_copy(a, b, sems.at[i]) for i, (a, b) in enumerate(pairs)]
    for one in copies:
        one.start()
    weight_copies = []
    if last:
        for z in range(levels):
            for far_x, parts in enumerate(((near0, near1), (beside0, beside1))):
                first = (z * 2 + (where[0] ^ far_x)) * rows
                here = pl.ds(pl.multiple_of(first, rows), rows)
                for h, part in enumerate(parts):
                    weight_copies.append(
                        pltpu.make_async_copy(
                            part.at[z, :, pl.ds(0, three)],
                            weights.at[here, pl.ds(h * three, three)],
                            sems.at[len(pairs) + len(weight_copies)],
                        )
                    )

        @pl.when(clip == 0)
        def _():
            for one in weight_copies:
                one.start()

    for b in range(blocks):
        grads[b * tokens : (b + 1) * tokens, :] = pieces[b][0]
    spots = spots_of(clip, pl.num_programs(0), spots, tokens)
    cosine, sine = rotary_of(spots, table)
    scale = jnp.asarray(head_size**-0.5, BF)
    chunk = length // 2
    parts = []
    for i in range(2):
        here = pl.ds(i * chunk, chunk)
        query_rows, grad_rows = query[0, here, :], grads[here, :]
        query_total = None
        for h in range(lanes // head_size):
            own_keys = keep_head(keys[0], h, head_size) * scale
            own_values = keep_head(values[0], h, head_size)
            scores = dot(own_keys, query_rows, NT)
            probs = jnp.exp(scores - tops[0, h : h + 1, here]) * inverses[0, h : h + 1, here]
            d_probs = dot(own_values, grad_rows, NT)
            delta = jnp.sum(probs * d_probs, axis=0, keepdims=True)
            d_scores = (probs * (d_probs - delta)).astype(BF)
            value_part = dot(probs.astype(BF), keep_head(grad_rows, h, head_size), NN)
            key_part = dot(d_scores, keep_head(query_rows, h, head_size) * scale, NN)
            query_part = dot(d_scores, own_keys, TN)
            if h == 0 and i == 0:
                d_values[...] = value_part
                d_keys[...] = key_part
            else:
                d_values[...] += value_part
                d_keys[...] += key_part
            query_total = query_part if query_total is None else query_total + query_part
        parts.append(query_total)
    d_query = jnp.concatenate(parts, axis=0)

    def back(part):
        return (part * cosine - swap_halves(part, head_size) * sine).astype(BF)

    d_mixed = jnp.concatenate(
        [back(d_query), back(d_keys[...]), d_values[...].astype(BF)], axis=1
    )
    sums = jnp.sum(d_mixed.astype(F32), axis=0, keepdims=True)
    for one in copies:
        one.wait()
    part = dot(d_mixed, rows_held[...], TN)

    @pl.when(clip == 0)
    def _():
        bias_sum[...] = sums
        total[...] = part

    @pl.when(clip > 0)
    def _():
        bias_sum[...] += sums
        total[...] += part

    def put_grads(bit, out):
        for z in range(levels):
            first = (z * 2 + (where[0] ^ bit)) * rows
            out[z, :three, :] = total[:, pl.ds(pl.multiple_of(first, rows), rows)].astype(BF)

    if not last:
        sent_back[0] = d_mixed

        @pl.when(clip == pl.num_programs(0) - 1)
        def _():
            put_grads(0, near_grad.at[:, 0])
            put_grads(1, near_grad.at[:, 1])

        return
    joined[:, three:] = d_mixed

    @pl.when(clip == 0)
    def _():
        for one in weight_copies:
            one.wait()

    both = 0.0
    for i in range(2):
        d_normed = dot(joined[i * half : (i + 1) * half, :], weights[...], NT)
        two = [
            jnp.sum(
                d_normed * unit_held[i * half : (i + 1) * half, :].astype(F32), axis=0, keepdims=True
            ),
            jnp.sum(d_normed, axis=0, keepdims=True),
        ]
        both = both + jnp.concatenate(two + [jnp.zeros_like(two[0])] * 6, axis=0)
        low = d_normed.astype(BF)
        for b in range(blocks // 2):
            out = (sent_back, sent_beside)[b % 2]
            out[i * (blocks // 4) + b // 2, 0] = low[b * tokens : (b + 1) * tokens]

    @pl.when(clip == 0)
    def _():
        norm_sums[...] = both

    @pl.when(clip > 0)
    def _():
        norm_sums[...] += both

    @pl.when(clip == pl.num_programs(0) - 1)
    def _():
        vectors[...] = jnp.zeros_like(vectors)
        for f in range(2 * levels):
            here = slice(f * rows, (f + 1) * rows)
            for row, (source, at) in enumerate(
                ((norm_sums, 0), (norm_sums2, 0), (norm_sums, 1), (norm_sums2, 1),
                 (norm_sums2, 2), (norm_sums2, 3))
            ):
                vectors[f, row : row + 1, :] = source[at : at + 1, here]
            vectors[f, pl.ds(9 + where[1], 1), :] = up_line[:, f * rows : (f + 1) * rows]
            vectors[f, VECTOR_ROWS - 1 : VECTOR_ROWS, :] = tops_row[...]
        for h, source in enumerate((earlier_sum, bias_sum)):
            for part in range(3):
                place = (part * blocks + where[1]) * 2 + h
                at = 6 + lax.rem(place, 3)
                vectors[place // 3, pl.ds(at, 1), :] = source[:, part * lanes : (part + 1) * lanes]
        put_grads(0, near_grad)
        put_grads(1, beside_grad)
        for z in range(levels):
            for bit, out in ((0, near_grad), (1, beside_grad)):
                out[z, three:, :] = vectors[z * 2 + (where[0] ^ bit)].astype(BF)


def heads_back(
    where, group, grads_in, saved, table, x_blocks, normed, levels, blocks, head_size,
    weights=(), earlier=None, unit=None, vectors=(),
):
    clips, half, width = normed[0].shape
    length, lanes = 2 * half, grads_in[0].shape[2]
    three, rows = 3 * lanes, width // (2 * levels)
    last = earlier is not None
    clip = lambda *rest: pl.BlockSpec((1,) + rest, lambda i, w: (i,) + (0,) * len(rest))
    by_block = lambda m, n: pl.BlockSpec(
        (m, 1, length // blocks, n), lambda i, w: (0, i, 0, 0)
    )
    stats = clip(lanes // head_size, length)
    query, keys, values, tops, inverses = saved
    grads = [(levels, three + VECTOR_ROWS + 2, rows)] * 2 if last else [(levels, 2, three, rows)]
    outs = [jax.ShapeDtypeStruct(shape, BF) for shape in grads]
    out_specs = [whole(shape) for shape in grads]
    piece = pl.BlockSpec((1, length // blocks, lanes), lambda i, w: (group, i, 0))
    anywhere = pl.BlockSpec(memory_space=pl.ANY)
    in_specs = [piece] * blocks + [clip(length, lanes)] * 3 + [stats] * 2
    in_specs += [whole(table.shape)] + [spot_block(x) for x in x_blocks]
    in_specs += [anywhere] * 2
    scratch = [
        pltpu.VMEM((three, width), F32),
        pltpu.VMEM((length, lanes), F32),
        pltpu.VMEM((length, lanes), F32),
        pltpu.VMEM((length, lanes), BF),
    ]
    if last:
        outs = [jax.ShapeDtypeStruct((blocks // 2, clips, length // blocks, width), BF)] * 2 + outs
        out_specs = [by_block(blocks // 2, width)] * 2 + out_specs
        in_specs += [anywhere] * (len(weights) + 3)
        in_specs += [whole(v.shape) for v in vectors]
        scratch = [
            pltpu.VMEM((width, 2 * three), BF),
            pltpu.VMEM((length, 2 * three), BF),
            pltpu.VMEM((2 * levels, VECTOR_ROWS + 2, lanes), F32),
            pltpu.VMEM((8, width), F32),
            pltpu.VMEM((1, three), F32),
        ] + scratch
        scratch += [pltpu.VMEM((length, width), BF)]
    else:
        outs = [jax.ShapeDtypeStruct((clips, length, three), BF)] + outs
        outs += [jax.ShapeDtypeStruct((1, three), F32)]
        out_specs = [clip(length, three)] + out_specs + [whole((1, three))]
    scratch += [pltpu.VMEM((length, width), BF), pltpu.SemaphoreType.DMA((5 + 4 * levels,))]
    return pl.pallas_call(
        functools.partial(heads_back_kernel, head_size, blocks, last),
        grid_spec=pltpu.PrefetchScalarGridSpec(
            num_scalar_prefetch=1,
            grid=(clips,),
            in_specs=in_specs,
            out_specs=out_specs,
            scratch_shapes=scratch,
        ),
        out_shape=outs,
        compiler_params=params(),
        cost_estimate=cost(22),
        name="heads_back",
    )(
        where, *grads_in, query, keys, values, tops, inverses, table, *x_blocks, *normed,
        *weights, *([earlier, *unit, *vectors] if last else []),
    )


def finish_out_kernel(resid, near, beside, far, bias, out):
    total = resid[...] + near[...] + beside[...].astype(F32) + far[...].astype(F32) + bias[...]
    out[...] = total.astype(BF)


def finish_out(resid, near, beside, far, bias):
    rows, width = resid.shape
    step = rows // 4
    line = pl.BlockSpec((step, width), lambda i: (i, 0))
    return pl.pallas_call(
        finish_out_kernel,
        grid=(rows // step,),
        in_specs=[line] * 4 + [whole((1, width))],
        out_specs=line,
        out_shape=jax.ShapeDtypeStruct((rows, width), BF),
        compiler_params=params(),
        cost_estimate=cost(4),
        name="finish_out",
    )(resid, near, beside, far, bias)


def first_norm_back_kernel(own, beside, far, x, d_resid, gain, out):
    d_normed = own[0, 0].astype(F32) + beside[0, 0].astype(F32) + far[...].astype(F32)
    unit, inverse = normalise(x[...].astype(F32))
    out[...] = d_resid[...] + norm_back(unit, inverse, d_normed * gain[...])


def first_norm_back(own, beside, far, x, d_resid, gain):
    rows, width = x.shape
    _, clips, tokens, _ = own.shape
    line = pl.BlockSpec((tokens, width), lambda i: (i, 0))
    first = pl.BlockSpec((1, 1, tokens, width), lambda i: (0, i, 0, 0))
    return pl.pallas_call(
        first_norm_back_kernel,
        grid=(clips,),
        in_specs=[first, first, line, line, line] + [whole((1, width))],
        out_specs=line,
        out_shape=jax.ShapeDtypeStruct((rows, width), F32),
        compiler_params=params(),
        cost_estimate=cost(4),
        name="first_norm_back",
    )(own, beside, far, x, d_resid, gain)


def pack_kernel(three, first, last, up, out, out_grads):
    lanes = first.shape[2]
    seq, rows = out.shape[0], up.shape[0] // out.shape[0]
    for h, part in enumerate((first, last)):
        total = part[0].astype(F32)
        for z in range(1, part.shape[0]):
            total = total + part[z].astype(F32)
        if h == 0:
            for k in range(out_grads.shape[1] // lanes):
                block = total[three + k * rows : three + (k + 1) * rows]
                out_grads[:, k * lanes : (k + 1) * lanes] = block
        turned = total[:three].T.astype(BF)
        for t in range(seq):
            out[t, :rows, h * three : (h + 1) * three] = turned[t * rows : (t + 1) * rows]
    for t in range(seq):
        out[t, rows:, :lanes] = total[three:].astype(BF)
        out[t, :rows, 2 * three :] = up[t * rows : (t + 1) * rows]


def pack(first, last, up, seq, three):
    extra, rows = last.shape[1] - three, up.shape[0] // seq
    shape = (seq, rows + extra, 2 * three + up.shape[1])
    width = (first.shape[1] - three) * first.shape[2] // rows
    return pl.pallas_call(
        functools.partial(pack_kernel, three),
        out_shape=[jax.ShapeDtypeStruct(shape, BF), jax.ShapeDtypeStruct((rows, width), F32)],
        compiler_params=params(),
        cost_estimate=cost(4),
        name="pack",
    )(first, last, up)


def unpack_kernel(
    rows, count, where, packed, weights, bias, threshold, qkv, up, gains, shifts, biases, qkv_line,
    up_line, maxima, clipped, clipped_bias
):
    seq, lanes = packed.shape[0], maxima.shape[1]
    width = qkv.shape[1] // 3
    group = width // seq
    own_heads = HEADS // seq
    sums = None
    column = lax.broadcasted_iota(jnp.int32, (1, width), 1) // (width // HEADS)
    lane = lax.broadcasted_iota(jnp.int32, (1, lanes), 1)
    limit = threshold[...]
    best = jnp.full((1, lanes), -jnp.inf, F32)
    scales = jnp.ones((1, width), F32)
    for t in range(seq):
        for h in range(group // lanes):
            for part in range(3):
                at = (h * 3 + part) * lanes
                to = part * width + t * group + h * lanes
                qkv[:, to : to + lanes] = packed[t, :rows, at : at + lanes].astype(F32)
        for k in range(up.shape[1] // (seq * lanes)):
            at = (3 * group // lanes + k) * lanes
            to = (k * seq + t) * lanes
            up[:, to : to + lanes] = packed[t, :rows, at : at + lanes].astype(F32)
        extra = packed[t, rows:, :lanes].astype(F32)
        sums = extra if sums is None else sums + extra
        tops = extra[VECTOR_ROWS - 1 : VECTOR_ROWS]
        tops = tops + pltpu.roll(tops, lanes - own_heads, 1) + pltpu.roll(tops, lanes - 2 * own_heads, 1)
        for h in range(own_heads):
            here = (lane % (3 * own_heads) == h) & (lane < count * 3 * own_heads)
            top = jnp.max(jnp.where(here, tops, -jnp.inf), axis=1, keepdims=True)
            head = t * own_heads + h
            best = jnp.where(lane == head, top, best)
            gamma = jnp.sqrt(limit / jnp.maximum(top, limit))
            scales = jnp.where(column == head, gamma, scales)
    lines = pltpu.roll(sums[:8], lanes - where[3] * rows, 1)
    for i, out in enumerate((gains, shifts, biases)):
        out[...] = lines[2 * i : 2 * i + 2, :rows]
    line = jnp.concatenate([sums[i : i + 1] for i in (6, 7, 8)], axis=1)
    line = pltpu.roll(jnp.broadcast_to(line, (8, 3 * lanes)), 3 * lanes - where[3] * 3 * rows, 1)
    qkv_line[...] = line[:1, : 3 * rows]
    line = sums[9:10]
    for t in range(1, seq):
        line = jnp.where(where[3] == t, sums[9 + t : 10 + t], line)
    up_line[...] = line
    maxima[...] = best
    for part in range(2):
        here = slice(part * width, (part + 1) * width)
        clipped[:, here] = weights[:, here].astype(F32) * scales
        clipped_bias[:, here] = bias[:, here] * scales


def unpack(where, packed, weights, bias, threshold, rows, count, hidden, lanes):
    width = weights.shape[1] // 3
    two = (weights.shape[0], 2 * width)
    shapes = [
        (rows, 3 * width), (rows, hidden), (2, rows), (2, rows), (2, rows), (1, 3 * rows), (1, lanes),
        (1, lanes), two, (1, 2 * width),
    ]
    return pl.pallas_call(
        functools.partial(unpack_kernel, rows, count),
        grid_spec=pltpu.PrefetchScalarGridSpec(
            num_scalar_prefetch=1,
            grid=(1,),
            in_specs=[whole(packed.shape), whole(two), whole(bias.shape), whole(threshold.shape)],
            out_specs=[whole(shape) for shape in shapes],
        ),
        out_shape=[jax.ShapeDtypeStruct(shape, F32) for shape in shapes],
        compiler_params=params(),
        cost_estimate=cost(4),
        name="unpack",
    )(where, packed, weights, bias, threshold)


VECTOR_ROWS = 14


def square_device(
    block_input,
    out_cotangent,
    positions,
    w_qkv,
    w_out,
    w_up,
    w_down,
    norm_gains,
    norm_shifts,
    qkv_bias,
    proj_bias,
    up_bias,
    clip_threshold,
):
    clips, tokens, width = block_input.shape
    fsdp, seq = axis_size(FSDP), axis_size(SEQ)
    levels, outer = fsdp // 2, seq // 2
    head_size = width // HEADS
    group = width // seq
    lanes = 128
    groups = group // lanes
    hidden = up_bias.shape[0]
    share = hidden // (fsdp * seq)
    length = tokens * seq
    rows = width // fsdp
    levels_index = lax.axis_index("z")
    x, y, c = lax.axis_index("x"), lax.axis_index("y"), lax.axis_index("core")
    s = y * 2 + c
    heads_where = jnp.stack([x, s]).astype(jnp.int32)
    where = jnp.stack([x, y, c, s]).astype(jnp.int32)
    x_own = block_input.reshape(clips * tokens, width)
    g_own = out_cotangent.reshape(clips * tokens, width)

    def copies(piece):
        return jnp.broadcast_to(piece[None], (levels,) + piece.shape)

    def over_z(piece):
        return lax.all_to_all(piece, "z", 0, 0, tiled=True)

    spots = positions.astype(BF).reshape(-1)
    spots = jnp.pad(spots, (0, 8 * width - spots.shape[0])).reshape(8, width)
    near0, near1, x_ext = prepare(where, w_qkv, w_out, x_own, spots, levels, lanes)
    x_beside = flip_one(x_ext, "y")
    near0 = over_z(near0)
    x_core = flip_one(x_ext, "core")

    near1 = lax.all_gather(near1, "z", axis=0)
    up = own_columns(where, w_up, fsdp, share)
    down = lax.dynamic_slice_in_dim(w_down, s * share, share, 0)

    halves = [first_norm(x_ext, x_core, norm_gains[:1], norm_shifts[:1], clips)]
    beside0 = flip_one(near0, "x")
    x_far = flip_one(after(x_beside, near0, halves[0][0], up), "core")
    up = lax.all_gather(after(up, x_beside), "z", axis=0)
    down = lax.all_gather(after(down, x_beside), "z", axis=0)
    halves.append(first_norm(x_beside, x_far, norm_gains[:1], norm_shifts[:1], clips))
    normed1, unit1 = zip(*halves, strict=True)
    x_blocks = (x_ext, x_core, x_beside, x_far)
    table = jnp.asarray(rotary_parts(head_size, lanes))
    near1 = after(near1, normed1[1])
    beside1 = flip_one(near1[..., : 3 * lanes], "x")

    own_bias = lax.dynamic_index_in_dim(
        qkv_bias.reshape(3, seq, groups, lanes), s, 1, keepdims=False
    )

    def forward(h, near, beside, *extra):
        return heads_forward(
            heads_where, normed1, near, beside, own_bias[:, h].reshape(1, -1),
            table, x_blocks, seq, head_size, *extra,
        )

    bias = up_bias.reshape(levels, 2, seq, share)
    bias = lax.dynamic_index_in_dim(bias, s, 2, keepdims=False).reshape(levels, 1, 2 * share)
    *saved0, out0, tops0, inverses0, own_out = forward(0, near0, after(beside0, bias), near1)
    saved0 += [tops0, inverses0]
    out0 = after(out0, beside1)
    out0_beside = flip_one(out0, "y")
    out0_core = flip_one(out0, "core")
    own_out = (own_out, flip_one(own_out, "x"))

    *saved1, out1, tops1, inverses1 = forward(1, near1, beside1)
    saved1 += [tops1, inverses1]
    out1 = after(out1, out0_beside, out0_core, own_out[1])
    up = (up, flip_one(after(up, tops1), "x"))
    out1_beside = flip_one(out1, "y")
    out1_core = flip_one(out1, "core")
    out0_far = flip_one(after(out0_beside, tops1), "core")
    other_out = [flip_one(after(part, tops1), "core") for part in own_out]
    out1_far = flip_one(out1_beside, "core")
    g_beside = flip_one(after(g_own, out1_beside), "y")
    g_core = flip_one(after(g_own, out1_beside), "core")
    pieces0 = (out0, out0_core, out0_beside, out0_far)
    pieces1 = (out1, out1_core, out1_beside, out1_far)
    down = (down, flip_one(after(down, out1_beside), "x"))
    tops_own = jnp.concatenate([jnp.max(t, axis=(0, 2)) for t in (tops0, tops1)])

    resid1, attended_own, normed2, full_out = project(
        where, (pieces0, pieces1), x_blocks, own_out, other_out,
        proj_bias[:1], norm_gains[1:], norm_shifts[1:],
    )

    g_far = flip_one(after(g_beside, normed2), "core")
    grads = (g_own, g_core, g_beside, g_far)
    activated, slope, down_near, down_beside = feed_up(where, normed2, grads, up, bias)
    down_beside = flip_one(down_beside, "x")
    far_back, far_other, far_hidden = feed_down_far(
        where, grads[2:], down, up, slope
    )
    far_back = add_low(far_back, flip_one(far_other, "core"))
    far_hidden = after(far_hidden, far_back)
    far_back = flip_one(far_back, "y")
    (own_back, other_back, part_near, part_beside, far_near, far_beside,
     up_sums, up_near, up_beside) = feed_down_near(
        where, normed2, grads[:2], down, up, slope, far_hidden, activated
    )
    up_beside = flip_one(up_beside, "x")
    part_beside = flip_one(part_beside, "core")
    far_beside = flip_one(far_beside, "core")
    down_sum = add_low(down_near, after(down_beside, up_sums))
    other_back = flip_one(after(other_back, far_back, down_sum), "core")
    d_resid1, d_resid1_low, *rest = second_norm_back(
        where, own_back, after(other_back, part_near), far_back, resid1, g_own,
        norm_gains[1:], full_out, seq, groups,
    )
    d_attended, sums2 = rest[:-1], rest[-1]
    d_heads = [d_attended[0]] + [flip(d_attended[m], SEQ, m) for m in range(1, seq)]
    grad_down = lax.psum_scatter(down_sum, "z", scatter_dimension=0, tiled=True)
    grad_down = grad_down.reshape(share, width).astype(F32)
    up_sum = add_low(up_near, after(up_beside, d_resid1_low))
    out_near, out_beside = out_grad(where, attended_own, d_resid1_low, levels, lanes)
    part_far = add_low(far_near, far_beside)
    out_beside = flip_one(after(out_beside, part_far, *d_heads[1:]), "core")

    tops_row, rest = [], tops_own
    for _ in range(3):
        tops_row.append(lax.reduce_precision(rest, 8, 7))
        rest = rest - tops_row[-1]
    tops_row = lax.dynamic_update_slice_in_dim(
        jnp.zeros((lanes,), F32), jnp.concatenate(tops_row), (levels_index * 2 + x) * 12, 0
    )[None]

    out_sum = add_low(out_near, out_beside)
    d_heads = after_all(d_heads, down_sum, up_sum, out_sum)
    up_sum = lax.psum_scatter(after(up_sum, d_heads[2]), "z", scatter_dimension=0, tiled=True)
    up_sum = up_sum.reshape(rows, fsdp * share)
    mixed0, qkv_sum0, bias_sum0 = heads_back(
        heads_where, 0, d_heads, saved0, table, x_blocks, normed1, levels, seq, head_size
    )
    out_far = flip_one(out_sum[1], "y")
    part_far = flip_one(after(part_far, out_far), "y")
    out_sum = add_low(out_sum[0], after(out_far, bias_sum0))
    qkv_sum0 = jnp.concatenate([qkv_sum0, out_sum], axis=2)
    qkv_sum0 = lax.psum_scatter(qkv_sum0, "z", scatter_dimension=0, tiled=True)[0]
    last, last_beside, near_grad1, beside_grad1 = heads_back(
        heads_where, 1, after_all(d_heads, grad_down), saved1, table, x_blocks, normed1,
        levels, seq, head_size, (near0, near1, beside0, beside1), mixed0, unit1,
        (sums2, up_sums.reshape(1, -1), tops_row, bias_sum0),
    )
    last_beside = flip_one(after(last_beside, qkv_sum0, up_sum, part_far), "core")
    beside_grad1 = flip_one(after(beside_grad1, qkv_sum0, up_sum), "x")
    far_block = add_low(last[1], last_beside[1])
    beside_sum0 = flip_one(qkv_sum0[1], "x")
    sent_block = after(far_block, beside_grad1).reshape(x_own.shape)
    far_block = flip_one(sent_block, "y")
    block_out = finish_out(
        after(resid1, sent_block), part_near, part_beside, part_far, proj_bias[1:]
    )
    qkv_sum1 = over_z(add_low(near_grad1, beside_grad1))
    grad_input = first_norm_back(
        last, last_beside, far_block, x_own, d_resid1, norm_gains[:1],
    ).reshape(block_input.shape)

    one = rows // seq
    first = jnp.stack([after(qkv_sum0[0], block_out), beside_sum0])
    packed, grad_out = pack(first, qkv_sum1, up_sum, seq, 3 * lanes)
    packed = lax.all_to_all(after(packed, far_block, block_out), SEQ, 0, 0, tiled=True)
    (grad_qkv, grad_up, grad_gains, grad_shifts, grad_proj_bias, grad_qkv_bias, grad_up_bias,
     maxima, clipped, clipped_bias) = unpack(
        where, packed, w_qkv, qkv_bias[None], clip_threshold[None], one, fsdp, hidden, lanes
    )
    grad_qkv_bias, grad_up_bias = grad_qkv_bias[0], grad_up_bias[0]
    maxima, clipped_bias = maxima[0, :HEADS], clipped_bias[0]
    return (
        block_out.reshape(block_input.shape),
        grad_input,
        grad_qkv,
        grad_out,
        grad_up,
        grad_down,
        grad_gains,
        grad_shifts,
        grad_qkv_bias,
        grad_proj_bias,
        grad_up_bias,
        maxima,
        clipped,
        clipped_bias,
    )


def on_device(block_input, *rest):
    fsdp, seq = axis_size(FSDP), axis_size(SEQ)
    width, hidden = block_input.shape[2], rest[-2].shape[0]
    square = seq == 4 and fsdp % 4 == 0 and fsdp == 8 and width == 256 * seq and hidden % (128 * fsdp * seq) == 0
    square = square and width % (128 * fsdp) == 0
    return (square_device if square else general_device)(block_input, *rest)


def solution(mesh):
    fsdp, seq = mesh.shape["fsdp"], mesh.shape["seq"]
    fine = Mesh(mesh.devices.reshape(fsdp // 2, 2, seq // 2, 2), FSDP + SEQ)
    in_specs = (
        P(FSDP, SEQ, None),
        P(FSDP, SEQ, None),
        P(None, FSDP, SEQ),
        P(FSDP, None),
        P(FSDP, None),
        P(FSDP, None),
        P(FSDP, None),
        P(),
        P(),
        P(),
        P(),
        P(),
        P(),
    )
    out_specs = (
        P(FSDP, SEQ, None),
        P(FSDP, SEQ, None),
        P(FSDP + SEQ, None),
        P(FSDP + SEQ, None),
        P(FSDP + SEQ, None),
        P(FSDP + SEQ, None),
        P(None, FSDP + SEQ),
        P(None, FSDP + SEQ),
        P(FSDP + SEQ),
        P(None, FSDP + SEQ),
        P(FSDP + SEQ),
        P(),
        P(FSDP, None),
        P(),
    )
    return jax.shard_map(
        on_device, mesh=fine, in_specs=in_specs, out_specs=out_specs, check_vma=False
    )
```

```python
import functools

import jax
import jax.numpy as jnp
import numpy as np
from jax import lax
from jax.experimental import pallas as pl
from jax.experimental.pallas import tpu as pltpu
from jax.sharding import Mesh
from jax.sharding import PartitionSpec as P

HEADS = 16
EPSILON = 1e-06
ROPE_BASE = 100.0
GRID_SIDE = 16

FSDP = ("z", "x")
SEQ = ("y", "core")

BF = jnp.bfloat16
F32 = jnp.float32
NN = (((1,), (0,)), ((), ()))
NT = (((1,), (1,)), ((), ()))
TN = (((0,), (0,)), ((), ()))


def dot(left, right, dims):
    return lax.dot_general(left, right, dims, preferred_element_type=F32)


def params(megabytes=62):
    return pltpu.CompilerParams(vmem_limit_bytes=megabytes << 20)


def axis_size(names):
    size = 1
    for name in names:
        size *= lax.axis_size(name)
    return size


def flip(value, axis, mask):
    size = axis_size(axis)
    return lax.ppermute(value, axis, [(i, i ^ mask) for i in range(size)])


def dim_of(name):
    inner = 2
    if name == "x":
        return FSDP, 1, inner
    if name == "z":
        return FSDP, inner, axis_size(FSDP) // inner
    if name == "core":
        return SEQ, 1, inner
    return SEQ, inner, axis_size(SEQ) // inner


def gather_dim(value, name, axis):
    mesh_axis, stride, size = dim_of(name)
    parts = [value] + [flip(value, mesh_axis, k * stride) for k in range(1, size)]
    return jnp.stack(parts, axis)


def scatter_dim(value, name, axis, last):
    mesh_axis, stride, size = dim_of(name)
    total = lax.index_in_dim(value, 0, axis, keepdims=False).astype(F32)
    for k in range(1, size):
        part = lax.index_in_dim(value, k, axis, keepdims=False)
        total = total + flip(part, mesh_axis, k * stride).astype(F32)
    return total if last else total.astype(BF)


def copy_kernel(source, target):
    target[...] = source[...].reshape(target.shape)


def gather_order_kernel(pieces, shift, *refs):
    sources, target = refs[:-1], refs[-1]
    width = target.shape[1] // (len(sources) * pieces)
    for o, source in enumerate(sources):
        for y in range(pieces):
            first = (o * pieces + y) * width
            target[:, first : first + width] = source[0, y ^ shift[1]]


def weights_in_order(parts, fsdp_index, y_index):
    count, pieces, rows, width = parts[0].shape
    total = len(parts) * pieces * width
    where = jnp.stack([fsdp_index, y_index]).astype(jnp.int32)

    def body(shift, *refs):
        gather_order_kernel(pieces, shift, *refs)

    return pl.pallas_call(
        body,
        grid_spec=pltpu.PrefetchScalarGridSpec(
            num_scalar_prefetch=1,
            grid=(count,),
            in_specs=[
                pl.BlockSpec((1, pieces, rows, width), lambda j, s: (j ^ s[0], 0, 0, 0))
                for _ in parts
            ],
            out_specs=pl.BlockSpec((rows, total), lambda j, s: (j, 0)),
        ),
        out_shape=jax.ShapeDtypeStruct((count * rows, total), parts[0].dtype),
        compiler_params=params(),
    )(where, *parts)


def rows_by_distance(value, orders, pieces, fsdp_index, y_index):
    count = axis_size(FSDP)
    rows, width = value.shape[0] // (count * pieces), value.shape[1]
    share = width // orders
    if rows % 16:
        view = value.reshape(count, pieces, rows, orders, share)
        view = jnp.take(view, jnp.arange(count) ^ fsdp_index, axis=0)
        view = jnp.take(view, jnp.arange(pieces) ^ y_index, axis=1)
        return [view[:, :, :, o] for o in range(orders)]
    where = jnp.stack([fsdp_index, y_index]).astype(jnp.int32)

    def body(shift, source, *targets):
        for o, target in enumerate(targets):
            target[0, 0] = source[:, o * share : (o + 1) * share]

    return pl.pallas_call(
        body,
        grid_spec=pltpu.PrefetchScalarGridSpec(
            num_scalar_prefetch=1,
            grid=(count, pieces),
            in_specs=[
                pl.BlockSpec(
                    (rows, width),
                    lambda j, y, s: ((j ^ s[0]) * pieces + (y ^ s[1]), 0),
                )
            ],
            out_specs=[
                pl.BlockSpec((1, 1, rows, share), lambda j, y, s: (j, y, 0, 0))
            ]
            * orders,
        ),
        out_shape=[
            jax.ShapeDtypeStruct((count, pieces, rows, share), value.dtype)
        ]
        * orders,
        compiler_params=params(),
    )(where, value)


def columns_in_order(value, shift):
    count, rows, width = value.shape
    if width % 128:
        ordered = jnp.take(value, jnp.arange(count) ^ shift, axis=0)
        return jnp.moveaxis(ordered, 0, 1).reshape(rows, count * width)
    return pl.pallas_call(
        lambda s, source, target: copy_kernel(source, target),
        grid_spec=pltpu.PrefetchScalarGridSpec(
            num_scalar_prefetch=1,
            grid=(count,),
            in_specs=[pl.BlockSpec((1, rows, width), lambda j, s: (j ^ s[0], 0, 0))],
            out_specs=pl.BlockSpec((rows, width), lambda j, s: (0, j)),
        ),
        out_shape=jax.ShapeDtypeStruct((rows, count * width), value.dtype),
        compiler_params=params(),
    )(shift.reshape(1).astype(jnp.int32), value)


def columns_by_distance(value, count, shift):
    rows, width = value.shape[0], value.shape[1] // count
    if width % 128:
        blocks = jnp.moveaxis(value.reshape(rows, count, width), 1, 0)
        return jnp.take(blocks, jnp.arange(count) ^ shift, axis=0)
    return pl.pallas_call(
        lambda s, source, target: copy_kernel(source, target),
        grid_spec=pltpu.PrefetchScalarGridSpec(
            num_scalar_prefetch=1,
            grid=(count,),
            in_specs=[pl.BlockSpec((rows, width), lambda j, s: (0, j ^ s[0]))],
            out_specs=pl.BlockSpec((1, rows, width), lambda j, s: (j, 0, 0)),
        ),
        out_shape=jax.ShapeDtypeStruct((count, rows, width), value.dtype),
        compiler_params=params(),
    )(shift.reshape(1).astype(jnp.int32), value)


def keep_head(value, head, head_size):
    lane = lax.broadcasted_iota(jnp.int32, (1, value.shape[1]), 1)
    return jnp.where(lane // head_size == head, value, jnp.zeros_like(value))


def attend_kernel(head_size, chunk, query, keys, values, out, tops, inverses):
    length, width = keys.shape
    scale = jnp.asarray(head_size**-0.5, BF)
    for h in range(width // head_size):
        own_keys = keep_head(keys[...], h, head_size) * scale
        own_values = keep_head(values[...], h, head_size)
        for i in range(length // chunk):
            rows = pl.ds(i * chunk, chunk)
            scores = dot(own_keys, query[rows, :], NT)
            top = jnp.max(scores, axis=0, keepdims=True)
            exponent = jnp.exp(scores - top)
            inverse = 1.0 / jnp.sum(exponent, axis=0, keepdims=True)
            part = dot((exponent * inverse).astype(BF), own_values, TN)
            if h == 0:
                out[rows, :] = part.astype(BF)
            else:
                out[rows, :] = (out[rows, :].astype(F32) + part).astype(BF)
            tops[0, h : h + 1, rows] = top
            inverses[0, h : h + 1, rows] = inverse


def attend(query, keys, values, head_size):
    length, width = query.shape
    block = min(128, width)
    wide = pl.BlockSpec((length, block), lambda h: (0, h))
    flat = pl.BlockSpec((1, block // head_size, length), lambda h: (h, 0, 0))
    stats = jax.ShapeDtypeStruct((width // block, block // head_size, length), F32)
    return pl.pallas_call(
        functools.partial(attend_kernel, head_size, min(512, length)),
        grid=(width // block,),
        in_specs=[wide] * 3,
        out_specs=[wide, flat, flat],
        out_shape=[jax.ShapeDtypeStruct((length, width), BF), stats, stats],
        compiler_params=params(),
    )(query, keys, values)


def attend_back_kernel(
    head_size, chunk, query, keys, values, grad, tops, inverses, d_query, d_keys, d_values
):
    length, width = keys.shape
    scale = jnp.asarray(head_size**-0.5, BF)
    for h in range(width // head_size):
        own_keys = keep_head(keys[...], h, head_size) * scale
        own_values = keep_head(values[...], h, head_size)
        for i in range(length // chunk):
            rows = pl.ds(i * chunk, chunk)
            query_rows, grad_rows = query[rows, :], grad[rows, :]
            scores = dot(own_keys, query_rows, NT)
            probs = jnp.exp(scores - tops[0, h : h + 1, rows]) * inverses[0, h : h + 1, rows]
            d_probs = dot(own_values, grad_rows, NT)
            delta = jnp.sum(probs * d_probs, axis=0, keepdims=True)
            d_scores = (probs * (d_probs - delta)).astype(BF)
            value_part = dot(probs.astype(BF), keep_head(grad_rows, h, head_size), NN)
            key_part = dot(d_scores, keep_head(query_rows, h, head_size) * scale, NN)
            query_part = dot(d_scores, own_keys, TN)
            if h == 0 and i == 0:
                d_values[...] = value_part
                d_keys[...] = key_part
            else:
                d_values[...] += value_part
                d_keys[...] += key_part
            if h == 0:
                d_query[rows, :] = query_part
            else:
                d_query[rows, :] += query_part


def attend_back(query, keys, values, grad, tops, inverses, head_size):
    length, width = query.shape
    block = min(128, width)
    wide = pl.BlockSpec((length, block), lambda h: (0, h))
    flat = pl.BlockSpec((1, block // head_size, length), lambda h: (h, 0, 0))
    return pl.pallas_call(
        functools.partial(attend_back_kernel, head_size, min(512, length)),
        grid=(width // block,),
        in_specs=[wide] * 4 + [flat] * 2,
        out_specs=[wide] * 3,
        out_shape=[jax.ShapeDtypeStruct((length, width), F32)] * 3,
        compiler_params=params(),
    )(query, keys, values, grad, tops, inverses)


def rotary_table(head_size):
    half = head_size // 2
    pair = np.arange(half)
    bands = (half + 2) // 3
    frequency = np.power(np.float32(ROPE_BASE), -(pair // 3).astype(np.float32) / bands)
    angles = np.arange(GRID_SIDE, dtype=np.float32)[:, None] * frequency[None, :]
    chosen = (pair % 3)[None, None, :] == np.arange(3)[:, None, None]

    def table(of):
        return np.where(chosen, of[None], 0.0).reshape(3 * GRID_SIDE, half)

    cosine, sine = table(np.cos(angles)), table(np.sin(angles))
    return np.concatenate([cosine, cosine, -sine, sine], axis=1).astype(np.float32)


def rotary_rows(coords, head_size):
    cells = jnp.arange(GRID_SIDE)
    hot = (coords[:, :, None] == cells).astype(F32)
    hot = jnp.transpose(hot, (1, 0, 2)).reshape(coords.shape[1], 3 * GRID_SIDE)
    both = jnp.dot(hot, rotary_table(head_size), precision=lax.Precision.HIGHEST)
    return both[:, :head_size], both[:, head_size:]


def half_swap(values, head_size):
    length, width = values.shape
    halves = values.reshape(length, width // head_size, 2, head_size // 2)
    return halves[:, :, ::-1, :].reshape(length, width)


def turn(values, cosine, sine, head_size):
    repeats = values.shape[1] // head_size
    return values * jnp.tile(cosine, (1, repeats)) + half_swap(values, head_size) * jnp.tile(
        sine, (1, repeats)
    )


def normalise(values):
    row_mean = jnp.mean(values, axis=-1, keepdims=True)
    centred = values - row_mean
    row_var = jnp.mean(centred * centred, axis=-1, keepdims=True)
    inverse = lax.rsqrt(row_var + EPSILON)
    return centred * inverse, inverse


def norm_back(unit, inverse, d_unit):
    return inverse * (
        d_unit
        - jnp.mean(d_unit, axis=-1, keepdims=True)
        - unit * jnp.mean(d_unit * unit, axis=-1, keepdims=True)
    )


def gelu_exact(values_in):
    return jax.nn.gelu(values_in, approximate=False)


def general_device(
    block_input,
    out_cotangent,
    positions,
    w_qkv,
    w_out,
    w_up,
    w_down,
    norm_gains,
    norm_shifts,
    qkv_bias,
    proj_bias,
    up_bias,
    clip_threshold,
):
    clips, tokens, width = block_input.shape
    fsdp, seq = axis_size(FSDP), axis_size(SEQ)
    outer = seq // 2
    head_size = width // HEADS
    group = width // seq
    hidden = up_bias.shape[0]
    share = hidden // (fsdp * seq)
    length = tokens * seq
    f = lax.axis_index(FSDP)
    s = lax.axis_index(SEQ)
    y, c = s // 2, s % 2

    def along_seq(value):
        rows = gather_dim(value, "y", 0)
        return gather_dim(rows, "core", 1).reshape((seq,) + value.shape)

    x_all = [along_seq(block_input[i]).reshape(length, width) for i in range(clips)]
    coords_all = jnp.moveaxis(along_seq(positions), 0, 2).reshape(3, clips, length)

    own_heads = lax.dynamic_index_in_dim(
        w_qkv.reshape(-1, 3, seq, group), s, 2, keepdims=False
    ).reshape(-1, 3 * group)
    halves = []
    for o, order in enumerate(("zx", "xz")):
        piece = own_heads[:, o * (3 * group // 2) : (o + 1) * (3 * group // 2)]
        shape = (fsdp, 1) + piece.shape
        if order == "zx":
            piece = gather_dim(gather_dim(piece, "z", 0), "x", 1)
        else:
            piece = gather_dim(gather_dim(piece, "x", 0), "z", 0)
        halves.append(piece.reshape(shape))
    full_qkv = weights_in_order(halves, f, jnp.zeros_like(f))

    def gathered(local):
        rows, columns = local.shape
        part = columns // (2 * outer)
        views = local.reshape(rows, 2, outer, part)
        parts = []
        for o, order in enumerate(("zxy", "zyx")):
            piece = lax.dynamic_index_in_dim(views[:, o], y, 1, keepdims=False)
            piece = gather_dim(piece, "z", 0)
            if order == "zxy":
                piece = gather_dim(gather_dim(piece, "x", 1), "y", 2)
            else:
                piece = gather_dim(gather_dim(piece, "y", 1), "x", 1)
            parts.append(piece.reshape(fsdp, outer, rows, part))
        return weights_in_order(parts, f, y)

    def summed(partial):
        parts = rows_by_distance(partial, 2, outer, f, y)
        sums = []
        for order, part in zip(("yxz", "xyz"), parts, strict=True):
            value = part.reshape((fsdp // 2, 2) + part.shape[1:])
            if order == "yxz":
                value = scatter_dim(scatter_dim(value, "y", 2, False), "x", 1, False)
            else:
                value = scatter_dim(scatter_dim(value, "x", 1, False), "y", 1, False)
            sums.append(scatter_dim(value, "z", 0, True))
        return jnp.concatenate(sums, axis=1)

    def core_part(value, axis):
        shape = value.shape
        view = value.reshape(shape[:axis] + (-1, 2, share) + shape[axis + 1 :])
        view = lax.dynamic_index_in_dim(view, c, axis + 1, keepdims=False)
        return view.reshape(shape[:axis] + (shape[axis] // 2,) + shape[axis + 1 :])

    full_out = gathered(w_out)
    full_up = gathered(core_part(w_up, 1))
    full_down = gathered(core_part(w_down, 0))
    own_up_bias = core_part(up_bias, 0)

    own_bias = lax.dynamic_index_in_dim(qkv_bias.reshape(3, seq, group), s, 1, keepdims=False)
    kept = []
    attended_parts = []
    for i in range(clips):
        unit, inverse = normalise(x_all[i].astype(F32))
        normed = (unit * norm_gains[0] + norm_shifts[0]).astype(BF)
        mixed = dot(normed, full_qkv, NN) + own_bias.reshape(-1)
        cosine, sine = rotary_rows(coords_all[:, i], head_size)
        query = turn(mixed[:, :group], cosine, sine, head_size).astype(BF)
        keys = turn(mixed[:, group : 2 * group], cosine, sine, head_size).astype(BF)
        values = mixed[:, 2 * group :].astype(BF)
        attended, tops, inverses = attend(query, keys, values, head_size)
        kept.append((normed, query, keys, values, tops, inverses, cosine, sine))
        blocks = attended.reshape(seq, tokens, group)
        attended_parts.append(
            jnp.stack([blocks[0]] + [flip(blocks[m], SEQ, m) for m in range(1, seq)])
        )
    attended_own = columns_in_order(
        jnp.concatenate(attended_parts, axis=1), s
    )
    tops_own = functools.reduce(
        jnp.maximum, [jnp.max(k[4], axis=2).reshape(-1) for k in kept]
    )

    x_own = block_input.reshape(clips * tokens, width).astype(F32)
    g_own = out_cotangent.reshape(clips * tokens, width)
    resid1 = x_own + dot(attended_own, full_out, NN) + proj_bias[0]
    unit2, inverse2 = normalise(resid1)
    normed2 = (unit2 * norm_gains[1] + norm_shifts[1]).astype(BF)

    def pair(value):
        return jnp.concatenate([value, flip(value, SEQ, 1)], axis=0)

    def pair_sum(value):
        half = value.shape[0] // 2
        return value[:half] + flip(value[half:], SEQ, 1)

    normed2_chip = pair(normed2)
    g_chip = pair(g_own)
    hidden_pre = dot(normed2_chip, full_up, NN) + own_up_bias
    activated, gelu_pull = jax.vjp(gelu_exact, hidden_pre)
    activated = activated.astype(BF)
    block_out = (resid1 + pair_sum(dot(activated, full_down, NN)) + proj_bias[1]).astype(BF)

    grad_down = summed(dot(activated, g_chip, TN).astype(BF))
    d_hidden = gelu_pull(dot(g_chip, full_down, NT))[0].astype(BF)
    grad_up_half = summed(dot(normed2_chip, d_hidden, TN).astype(BF))
    up_bias_part = jnp.sum(d_hidden.astype(F32), axis=0)
    d_normed2 = pair_sum(dot(d_hidden, full_up, NT))
    gain2_part = jnp.sum(d_normed2 * unit2, axis=0)
    shift2_part = jnp.sum(d_normed2, axis=0)
    g_wide = g_own.astype(F32)
    down_bias_part = jnp.sum(g_wide, axis=0)
    d_resid1 = g_wide + norm_back(unit2, inverse2, d_normed2 * norm_gains[1])
    d_resid1_low = d_resid1.astype(BF)
    out_bias_part = jnp.sum(d_resid1_low.astype(F32), axis=0)

    d_attended = dot(d_resid1_low, full_out, NT).astype(BF)
    pieces = columns_by_distance(d_attended, seq, s).reshape(seq, clips, tokens, group)

    out_rows = dot(attended_own, d_resid1_low, TN).astype(BF)
    out_rows = out_rows.reshape(-1, 2, width // (fsdp * seq), width)
    mine = lax.dynamic_index_in_dim(out_rows, c, 1, keepdims=False)
    theirs = lax.dynamic_index_in_dim(out_rows, 1 - c, 1, keepdims=False)
    out_rows = (mine.astype(F32) + flip(theirs, SEQ, 1).astype(F32)).astype(BF)
    grad_out = summed(out_rows.reshape(-1, width))

    d_normed1_parts = []
    qkv_part = 0.0
    qkv_bias_part = 0.0
    gain1_part = 0.0
    shift1_part = 0.0
    for i in range(clips):
        normed, query, keys, values, tops, inverses, cosine, sine = kept[i]
        grad = jnp.concatenate(
            [pieces[0, i]] + [flip(pieces[m, i], SEQ, m) for m in range(1, seq)], axis=0
        )
        d_query, d_keys, d_values = attend_back(
            query, keys, values, grad, tops, inverses, head_size
        )
        d_mixed = jnp.concatenate(
            [
                turn(d_query, cosine, -sine, head_size),
                turn(d_keys, cosine, -sine, head_size),
                d_values,
            ],
            axis=1,
        ).astype(BF)
        qkv_part = qkv_part + dot(normed, d_mixed, TN)
        qkv_bias_part = qkv_bias_part + jnp.sum(d_mixed.astype(F32), axis=0)
        d_normed1 = dot(d_mixed, full_qkv, NT)
        unit, _ = normalise(x_all[i].astype(F32))
        gain1_part = gain1_part + jnp.sum(d_normed1 * unit, axis=0)
        shift1_part = shift1_part + jnp.sum(d_normed1, axis=0)
        d_normed1_parts.append(d_normed1.astype(BF))

    blocks = rows_by_distance(qkv_part.astype(BF), 2, 1, f, jnp.zeros_like(f))
    sums = []
    for order, part in zip(("xz", "zx"), blocks, strict=True):
        value = part.reshape((fsdp // 2, 2) + part.shape[2:])
        if order == "xz":
            value = scatter_dim(scatter_dim(value, "x", 1, False), "z", 0, True)
        else:
            value = scatter_dim(scatter_dim(value, "z", 0, False), "x", 0, True)
        sums.append(value)
    own_rows = jnp.concatenate(sums, axis=1).reshape(seq, -1, 3 * group)

    def rows_of(m):
        return lax.dynamic_index_in_dim(own_rows, s ^ m, 0, keepdims=False)

    arrived = jnp.stack([rows_of(0)] + [flip(rows_of(m), SEQ, m) for m in range(1, seq)])
    ordered = [
        lax.dynamic_index_in_dim(arrived, s ^ t, 0, keepdims=False).reshape(-1, 3, 1, group)
        for t in range(seq)
    ]
    grad_qkv = jnp.concatenate(ordered, axis=2).reshape(-1, 3 * width)

    halves = grad_up_half.reshape(2, -1, fsdp * outer, share)
    mine = lax.dynamic_index_in_dim(halves, c, 0, keepdims=False)
    other = flip(lax.dynamic_index_in_dim(halves, 1 - c, 0, keepdims=False), SEQ, 1)
    first = jnp.where(c == 0, mine, other)
    second = jnp.where(c == 0, other, mine)
    grad_up = jnp.stack([first, second], axis=2).reshape(-1, hidden)

    d_normed1 = jnp.stack([p.reshape(seq, tokens, width) for p in d_normed1_parts], axis=1)
    value = d_normed1.reshape((outer, 2) + d_normed1.shape[1:])
    value = scatter_dim(scatter_dim(value, "core", 1, False), "y", 0, True)
    unit1, inverse1 = normalise(x_own)
    d_unit1 = value.reshape(clips * tokens, width) * norm_gains[0]
    grad_input = (d_resid1 + norm_back(unit1, inverse1, d_unit1)).reshape(block_input.shape)

    qkv_slots = lax.dynamic_update_index_in_dim(
        jnp.zeros((3, seq, group), F32), qkv_bias_part.reshape(3, group), s, 1
    )
    up_slots = lax.dynamic_update_index_in_dim(
        jnp.zeros((fsdp * outer, 2, share), F32),
        up_bias_part.reshape(fsdp * outer, share),
        c,
        1,
    )
    devices = fsdp * seq
    rows = [
        gain1_part, gain2_part, shift1_part, shift2_part, out_bias_part, down_bias_part,
        qkv_slots.reshape(-1), up_slots.reshape(-1),
    ]
    rows = jnp.concatenate([r.reshape(devices, -1) for r in rows], axis=1)
    sums = lax.psum_scatter(rows, FSDP + SEQ, scatter_dimension=0, tiled=True)[0]
    one = width // devices
    grad_gains = sums[: 2 * one].reshape(2, one)
    grad_shifts = sums[2 * one : 4 * one].reshape(2, one)
    grad_proj_bias = sums[4 * one : 6 * one].reshape(2, one)
    grad_qkv_bias = sums[6 * one : 9 * one]
    grad_up_bias = sums[9 * one :]

    slots = jnp.full((seq, HEADS // seq), -jnp.inf, F32)
    slots = lax.dynamic_update_index_in_dim(slots, tops_own, s, 0)
    maxima = lax.pmax(slots.reshape(-1), FSDP + SEQ)
    threshold = clip_threshold[0]
    gamma = jnp.sqrt(threshold / jnp.maximum(maxima, threshold))
    columns = jnp.tile(jnp.repeat(gamma, head_size), 2)
    clipped = w_qkv[:, : 2 * width].astype(F32) * columns
    clipped_bias = qkv_bias[: 2 * width] * columns
    return (
        block_out.reshape(block_input.shape),
        grad_input,
        grad_qkv,
        grad_out,
        grad_up,
        grad_down,
        grad_gains,
        grad_shifts,
        grad_qkv_bias,
        grad_proj_bias,
        grad_up_bias,
        maxima,
        clipped,
        clipped_bias,
    )


def flip_one(value, name):
    return lax.ppermute(value, name, [(0, 1), (1, 0)])


def after(value, *others):
    return lax.optimization_barrier((value, *others))[0]


def after_all(values, *others):
    return lax.optimization_barrier((tuple(values), *others))[0]


def add_low(*terms):
    return functools.reduce(jnp.add, [t.astype(F32) for t in terms]).astype(BF)


def cost(microseconds):
    return pl.CostEstimate(
        flops=int(microseconds * 0.2e9), bytes_accessed=1 << 10, transcendentals=0
    )


ANYWHERE = pl.BlockSpec(memory_space=pl.ANY)


def loads(sems, first, pairs):
    return [
        pltpu.make_async_copy(source, target, sems.at[first + i])
        for i, (source, target) in enumerate(pairs)
    ]


def start(copies):
    for one in copies:
        one.start()


def wait(copies):
    for one in copies:
        one.wait()


def by_rows(where_x, near, beside, target):
    levels, rows = near.shape[:2]
    pairs = []
    for z in range(levels):
        for far_x, part in enumerate((near, beside)):
            first = pl.multiple_of((z * 2 + (where_x ^ far_x)) * rows, rows)
            pairs.append((part.at[z], target.at[pl.ds(first, rows)]))
    return pairs


def whole(shape):
    return pl.BlockSpec(shape, lambda *_: (0,) * len(shape))


def in_order(index, bit, axis):
    return jnp.where(bit == 0, index, jnp.flip(index, axis))


def swap_halves(values, head_size):
    half = head_size // 2
    lane = lax.broadcasted_iota(jnp.int32, (1, values.shape[1]), 1)
    width = values.shape[1]
    return jnp.where(
        lane % head_size < half,
        pltpu.roll(values, width - half, 1),
        pltpu.roll(values, half, 1),
    )


def first_norm_kernel(first, second, gain, shift, normed, unit):
    tokens = first.shape[0]
    for i, part in enumerate((first, second)):
        value, _ = normalise(part[...].astype(F32))
        here = slice(i * tokens, (i + 1) * tokens)
        unit[0, here, :] = value.astype(BF)
        normed[0, here, :] = (value * gain[...] + shift[...]).astype(BF)


def first_norm(first, second, gain, shift, clips):
    width = first.shape[1]
    tokens = first.shape[0] // (8 * clips) * 8
    block = pl.BlockSpec((tokens, width), lambda i: (i, 0))
    out = pl.BlockSpec((1, 2 * tokens, width), lambda i: (i, 0, 0))
    return pl.pallas_call(
        first_norm_kernel,
        grid=(clips,),
        in_specs=[block, block, whole((1, width)), whole((1, width))],
        out_specs=[out, out],
        out_shape=[jax.ShapeDtypeStruct((clips, 2 * tokens, width), BF)] * 2,
        compiler_params=params(),
        cost_estimate=cost(4),
        name="first_norm",
    )(first, second, gain, shift)


def prepare_kernel(where, *refs):
    pieces, refs = refs[:6], refs[6:]
    out, x, spots, first, second, x_ext = refs
    lanes = pieces[0].shape[1]
    for z in range(first.shape[0]):
        for k in range(3):
            first[z, :, k * lanes : (k + 1) * lanes] = pieces[k][...]
    for k in range(3):
        second[:, k * lanes : (k + 1) * lanes] = pieces[3 + k][...]
    rest = second.shape[1] - out.shape[1]
    second[:, 3 * lanes : rest] = jnp.zeros_like(second[:, 3 * lanes : rest])
    second[:, rest:] = out[...]
    tokens = x.shape[0]
    x_ext[:tokens] = x[...]
    x_ext[tokens:] = spots[...]


def prepare(where, w_qkv, w_out, x, spots, levels, lanes):
    rows, width = w_out.shape
    tokens = x.shape[0]
    groups = width // (4 * lanes)
    blocks = [
        pl.BlockSpec(
            (rows, lanes),
            lambda i, w, part=part, h=h: (0, (part * 4 + w[3]) * groups + h),
        )
        for h in range(groups)
        for part in range(3)
    ]
    return pl.pallas_call(
        prepare_kernel,
        grid_spec=pltpu.PrefetchScalarGridSpec(
            num_scalar_prefetch=1,
            grid=(1,),
            in_specs=blocks
            + [
                pl.BlockSpec((rows, width // 2), lambda i, w: (0, w[2])),
                whole(x.shape),
                whole(spots.shape),
            ],
            out_specs=[
                whole((levels, rows, 3 * lanes)),
                whole((rows, width)),
                whole((tokens + 8, width)),
            ],
        ),
        out_shape=[
            jax.ShapeDtypeStruct((levels, rows, 3 * lanes), BF),
            jax.ShapeDtypeStruct((rows, width), BF),
            jax.ShapeDtypeStruct((tokens + 8, width), BF),
        ],
        compiler_params=params(),
        cost_estimate=cost(3),
        name="prepare",
    )(where, *[w_qkv] * len(blocks), w_out, x, spots)


def own_columns(where, value, count, share):
    rows = value.shape[0]
    return pl.pallas_call(
        lambda w, source, target: copy_kernel(source, target),
        grid_spec=pltpu.PrefetchScalarGridSpec(
            num_scalar_prefetch=1,
            grid=(count,),
            in_specs=[
                pl.BlockSpec((rows, share), lambda k, w: (0, (k * 2 + w[1]) * 2 + w[2]))
            ],
            out_specs=pl.BlockSpec((rows, share), lambda k, w: (0, k)),
        ),
        out_shape=jax.ShapeDtypeStruct((rows, count * share), value.dtype),
        compiler_params=params(),
        cost_estimate=cost(3),
        name="own_columns",
    )(where, value)


def rotary_parts(head_size, lanes):
    half = 2 * head_size // 2
    table = rotary_table(head_size)
    repeats = lanes // head_size
    table = np.concatenate([np.tile(table[:, :half], (1, repeats)), np.tile(table[:, half:], (1, repeats))], axis=1)
    parts = []
    for _ in range(3):
        parts.append(table.astype(BF))
        table = table - parts[-1].astype(np.float32)
    return np.concatenate(parts, axis=0)


def spots_of(clip, clips, spots, tokens):
    lines = []
    for part in spots:
        width = part.shape[1]
        line = []
        for a in range(3):
            first = a * clips * tokens
            column = first % width + clip * tokens
            row = first // width
            line.append(part[row : row + 1, pl.ds(pl.multiple_of(column, tokens), tokens)])
        lines.append(jnp.concatenate(line, axis=0))
    return jnp.concatenate(lines, axis=1).astype(F32)


def rotary_of(coords, table):
    cells = lax.broadcasted_iota(jnp.int32, (GRID_SIDE, coords.shape[1]), 0).astype(F32)
    hot = [(coords[a : a + 1] == cells).astype(F32) for a in range(3)]
    hot = jnp.concatenate(hot * 3, axis=0).astype(BF)
    width = table.shape[1] // 2
    both = dot(hot, table[...], TN)
    return both[:, :width], both[:, width:]


def heads_forward_kernel(
    head_size, blocks, where, first_rows, last_rows, near, beside, bias, table, *refs
):
    spots, refs = refs[:blocks], refs[blocks:]
    extra, refs = refs[: (len(refs) - 7) // 2], refs[(len(refs) - 7) // 2 :]
    query, keys, values, out, tops, inverses, *extra_out, weights = refs
    levels, rows, width = near.shape
    length, lanes = query.shape[1:]
    spots = spots_of(pl.program_id(0), pl.num_programs(0), spots, length // blocks)
    cosine, sine = rotary_of(spots, table)

    @pl.when(pl.program_id(0) == 0)
    def _():
        for z in range(levels):
            for part, bit in ((near, 0), (beside, 1)):
                first = (z * 2 + (where[0] ^ bit)) * rows
                weights[pl.ds(pl.multiple_of(first, rows), rows), :] = part[z]
        for source, target in zip(extra, extra_out, strict=True):
            target[...] = source[...]

    mixed = [dot(part[0], weights[...], NN) + bias[...] for part in (first_rows, last_rows)]
    mixed = jnp.concatenate(mixed, axis=0)
    turned = [
        part * cosine + swap_halves(part, head_size) * sine
        for part in (mixed[:, :lanes], mixed[:, lanes : 2 * lanes])
    ]
    query[0], keys[0] = turned[0].astype(BF), turned[1].astype(BF)
    values[0] = mixed[:, 2 * lanes :].astype(BF)
    scale = jnp.asarray(head_size**-0.5, BF)
    chunk = length // 2
    tokens = length // blocks
    for i in range(2):
        rows_here = pl.ds(i * chunk, chunk)
        query_rows = query[0, rows_here, :]
        total = None
        for h in range(lanes // head_size):
            own_keys = keep_head(keys[0], h, head_size) * scale
            own_values = keep_head(values[0], h, head_size)
            scores = dot(own_keys, query_rows, NT)
            top = jnp.max(scores, axis=0, keepdims=True)
            exponent = jnp.exp(scores - top)
            inverse = 1.0 / jnp.sum(exponent, axis=0, keepdims=True)
            part = dot((exponent * inverse).astype(BF), own_values, TN)
            total = part if total is None else total + part
            tops[0, h : h + 1, rows_here] = top
            inverses[0, h : h + 1, rows_here] = inverse
        low = total.astype(BF)
        for b in range(blocks // 2):
            out[i * (blocks // 2) + b, 0] = low[b * tokens : (b + 1) * tokens]


def spot_block(x):
    return pl.BlockSpec((8, x.shape[1]), lambda i, w: (x.shape[0] // 8 - 1, 0))


def heads_forward(where, normed, near, beside, bias, table, x_blocks, blocks, head_size, *extra):
    clips, half, width = normed[0].shape
    length = 2 * half
    lanes = bias.shape[1] // 3
    pieces = near.shape[:2] + bias.shape[1:]
    second = [e.shape[:2] + (e.shape[2] // 2,) for e in extra]
    clip = lambda *rest: pl.BlockSpec((1,) + rest, lambda i, w: (i,) + (0,) * len(rest))
    head = jax.ShapeDtypeStruct((clips, length, lanes), BF)
    stats = jax.ShapeDtypeStruct((clips, lanes // head_size, length), F32)
    return pl.pallas_call(
        functools.partial(heads_forward_kernel, head_size, blocks),
        grid_spec=pltpu.PrefetchScalarGridSpec(
            num_scalar_prefetch=1,
            grid=(clips,),
            in_specs=[
                clip(half, width),
                clip(half, width),
                whole(pieces),
                whole(pieces),
                whole(bias.shape),
                whole(table.shape),
            ]
            + [spot_block(x) for x in x_blocks]
            + [pl.BlockSpec(shape, lambda i, w: (0, 0, 1)) for shape in second],
            out_specs=[clip(length, lanes)] * 3
            + [
                pl.BlockSpec(
                    (blocks, 1, length // blocks, lanes), lambda i, w: (0, i, 0, 0)
                )
            ]
            + [clip(lanes // head_size, length)] * 2
            + [whole(shape) for shape in second],
            scratch_shapes=[pltpu.VMEM((width, 3 * lanes), BF)],
        ),
        out_shape=[
            head,
            head,
            head,
            jax.ShapeDtypeStruct((blocks, clips, length // blocks, lanes), BF),
            stats,
            stats,
        ]
        + [jax.ShapeDtypeStruct(shape, BF) for shape in second],
        compiler_params=params(),
        cost_estimate=cost(15),
        name="heads_forward",
    )(where, *normed, near, beside, bias, table, *x_blocks, *extra)


def out_row(z, x, where, rows):
    index = z * 2 + x
    return ((((index // 2) ^ where[3]) * 2) + index % 2) * rows


def put_out_weights(where, own, other, weights):
    levels, rows, share = own[0].shape
    for core, parts in ((0, own), (1, other)):
        column = (where[2] ^ core) * share
        column = pl.ds(pl.multiple_of(column, share), share)
        for far_x, part in enumerate(parts):
            for z in range(levels):
                place = out_row(z, where[0] ^ far_x, where, rows)
                place = pl.ds(pl.multiple_of(place, rows), rows)
                weights[place, column] = part[z]


def project_kernel(where, *refs, groups):
    pieces, refs = refs[: 4 * groups], refs[4 * groups :]
    x_blocks, refs = refs[:4], refs[4:]
    own, other, (bias, gain, shift, *refs) = refs[:2], refs[2:4], refs[4:]
    resid, attended, normed, weights_out, weights, joined, held, kept, sems = refs
    step = pl.program_id(0)
    clips, tokens, lanes = pieces[0].shape[1:]
    rows, width = clips * tokens, weights.shape[1]
    per = 4 * groups + 1
    copies = []
    for b in range(4):
        pairs = [(x_blocks[b].at[pl.ds(0, rows)], held.at[b])]
        for h in range(groups):
            for m in range(4):
                column = pl.ds((m * groups + h) * lanes, lanes)
                pairs.append((pieces[h * 4 + m].at[b ^ m], joined.at[b, :, :, column]))
        copies.append(loads(sems, b * per, pairs))
    save = loads(sems, 4 * per, [(weights, weights_out), (kept, resid)])

    @pl.when(step == 0)
    def _():
        for group in copies:
            start(group)
        put_out_weights(where, own, other, weights)
        save[0].start()

    for b in range(4):

        @pl.when(step == b)
        def _(b=b):
            wait(copies[b])

    mixed = joined[step].reshape(rows, width)
    out = held[step].astype(F32) + dot(mixed, weights[...], NN) + bias[...]
    unit, _ = normalise(out)
    normed[...] = (unit * gain[...] + shift[...]).astype(BF)

    @pl.when(step == 0)
    def _():
        kept[...] = out
        attended[...] = mixed
        save[1].start()

    @pl.when(step == 3)
    def _():
        wait(save)


def project(where, pieces, x_blocks, own, other, bias, gain, shift):
    clips, tokens, lanes = pieces[0][0].shape[1:]
    rows, width = clips * tokens, x_blocks[0].shape[1]
    groups = len(pieces)
    return pl.pallas_call(
        functools.partial(project_kernel, groups=groups),
        grid_spec=pltpu.PrefetchScalarGridSpec(
            num_scalar_prefetch=1,
            grid=(4,),
            in_specs=[ANYWHERE] * (4 * groups + 4)
            + [whole(own[0].shape)] * 4
            + [whole((1, width))] * 3,
            out_specs=[
                ANYWHERE,
                whole((rows, width)),
                pl.BlockSpec((rows, width), lambda t, w: (t, 0)),
                ANYWHERE,
            ],
            scratch_shapes=[
                pltpu.VMEM((width, width), BF),
                pltpu.VMEM((4, clips, tokens, width), BF),
                pltpu.VMEM((4, rows, width), BF),
                pltpu.VMEM((rows, width), F32),
                pltpu.SemaphoreType.DMA((4 * (4 * groups + 1) + 2,)),
            ],
        ),
        out_shape=[
            jax.ShapeDtypeStruct((rows, width), F32),
            jax.ShapeDtypeStruct((rows, width), BF),
            jax.ShapeDtypeStruct((4 * rows, width), BF),
            jax.ShapeDtypeStruct((width, width), BF),
        ],
        compiler_params=params(),
        cost_estimate=cost(13),
        name="project_out",
    )(where, *(p for group in pieces for p in group), *x_blocks, *own, *other, bias, gain, shift)


def gelu_pair(values):
    cumulative = 0.5 * (1.0 + lax.erf(values * np.float32(0.5**0.5)))
    density = jnp.exp(-0.5 * values * values) * np.float32((2.0 * np.pi) ** -0.5)
    return values * cumulative, cumulative + values * density


def up_kernel(where, normed, near, beside, bias, *refs):
    grads, refs = refs[:4], refs[4:]
    activated, slope, near_out, beside_out, rows_held, columns, held, low, sems = refs
    levels = near.shape[0]
    block = activated.shape[1]
    share = block // 2
    step = pl.program_id(0)
    tokens = grads[0].shape[0]
    here = [pl.ds(i * tokens, tokens) for i in range(4)]
    weight_copies = loads(sems, 0, by_rows(where[0], near, beside, columns))
    count = len(weight_copies)
    row_copies = loads(sems, count, [(normed.at[h], rows_held.at[h]) for h in here])
    grad_copies = loads(sems, count + 4, [(g, held.at[h]) for g, h in zip(grads, here)])

    @pl.when(step == 0)
    def _():
        start(weight_copies)
        start(row_copies)
        start(grad_copies)
        wait(weight_copies)
        wait(row_copies)

    column = pl.ds(pl.multiple_of(step * block, block), block)
    for i in range(4):
        hidden = dot(rows_held[here[i], :], columns[:, column], NN) + bias[0]
        act, d_act = gelu_pair(hidden)
        activated[here[i], :] = act.astype(BF)
        slope[here[i], :] = d_act.astype(BF)

    @pl.when(step == 0)
    def _():
        wait(grad_copies)

    low[...] = dot(activated[...], held[...], TN).astype(BF)
    for far_x, out in enumerate((near_out, beside_out)):
        first = (where[0] ^ far_x) * share
        out[0] = low[pl.ds(pl.multiple_of(first, share), share), :]


def feed_up(where, normed, grads, pieces, bias):
    levels, rows, hidden = pieces[1].shape
    tokens, width = normed.shape
    block = hidden // levels
    line = pl.BlockSpec((tokens, block), lambda t, w: (0, t))
    out = pl.BlockSpec((1, block // 2, width), lambda t, w: (t, 0, 0))
    return pl.pallas_call(
        up_kernel,
        grid_spec=pltpu.PrefetchScalarGridSpec(
            num_scalar_prefetch=1,
            grid=(levels,),
            in_specs=[ANYWHERE] * 3
            + [pl.BlockSpec((1, 1, block), lambda t, w: (t, 0, 0))]
            + [ANYWHERE] * 4,
            out_specs=[line, line, out, out],
            scratch_shapes=[
                pltpu.VMEM((tokens, width), BF),
                pltpu.VMEM((width, hidden), BF),
                pltpu.VMEM((tokens, width), BF),
                pltpu.VMEM((block, width), BF),
                pltpu.SemaphoreType.DMA((2 * levels + 8,)),
            ],
        ),
        out_shape=[jax.ShapeDtypeStruct((tokens, hidden), BF)] * 2
        + [jax.ShapeDtypeStruct((levels, block // 2, width), BF)] * 2,
        compiler_params=params(),
        cost_estimate=cost(17),
        name="feed_up",
    )(where, normed, *pieces, bias, *grads)


def far_kernel(
    where, first_grad, last_grad, near, beside, up_near, up_beside, slope,
    first_back, last_back, d_hidden, grads, down, up, slopes, hidden, sems,
):
    step = pl.program_id(0)
    steps = pl.num_programs(0) - 1
    tokens = first_grad.shape[0]
    block = d_hidden.shape[1]
    pairs = [(first_grad, grads.at[pl.ds(0, tokens)]), (last_grad, grads.at[pl.ds(tokens, tokens)])]
    pairs += by_rows(where[0], near, beside, down)
    first_copies = loads(sems, 0, pairs)
    count = len(first_copies)
    columns = [pl.ds(k * block, block) for k in range(steps)]
    rows = pl.ds(2 * tokens, 2 * tokens)
    slope_copies = loads(sems, count, [(slope.at[rows, k], slopes.at[:, k]) for k in columns])
    up_copies = loads(sems, count + steps, by_rows(where[0], up_near, up_beside, up))

    @pl.when(step == 0)
    def _():
        start(first_copies)
        start(slope_copies)
        start(up_copies)
        wait(first_copies)

    for k in range(steps):

        @pl.when(step == k)
        def _(k=k):
            slope_copies[k].wait()

    @pl.when(step < steps)
    def _():
        place = pl.ds(pl.multiple_of(step * block, block), block)
        for i in range(2):
            here = slice(i * tokens, (i + 1) * tokens)
            d_act = dot(grads[here, :], down[place, :], NT)
            low = (d_act * slopes[here, place].astype(F32)).astype(BF)
            hidden[here, place] = low
            d_hidden[here, :] = low

    @pl.when(step == steps)
    def _():
        wait(up_copies)
        first_back[...] = dot(hidden[:tokens, :], up[...], NT).astype(BF)
        last_back[...] = dot(hidden[tokens:, :], up[...], NT).astype(BF)


def feed_down_far(where, grads, pieces, up_pieces, slope):
    levels, share, width = pieces[0].shape
    tokens = grads[0].shape[0]
    hidden = slope.shape[1]
    steps = 2
    block = hidden // steps
    return pl.pallas_call(
        far_kernel,
        grid_spec=pltpu.PrefetchScalarGridSpec(
            num_scalar_prefetch=1,
            grid=(steps + 1,),
            in_specs=[ANYWHERE] * 7,
            out_specs=[whole((tokens, width))] * 2
            + [pl.BlockSpec((2 * tokens, block), lambda t, w: (0, jnp.minimum(t, steps - 1)))],
            scratch_shapes=[
                pltpu.VMEM((2 * tokens, width), BF),
                pltpu.VMEM((hidden, width), BF),
                pltpu.VMEM((width, hidden), BF),
                pltpu.VMEM((2 * tokens, hidden), BF),
                pltpu.VMEM((2 * tokens, hidden), BF),
                pltpu.SemaphoreType.DMA((2 + 4 * levels + steps,)),
            ],
        ),
        out_shape=[
            jax.ShapeDtypeStruct((tokens, width), BF),
            jax.ShapeDtypeStruct((tokens, width), BF),
            jax.ShapeDtypeStruct((2 * tokens, hidden), BF),
        ],
        compiler_params=params(),
        cost_estimate=cost(8),
        name="feed_down_far",
    )(where, *grads, *pieces, *up_pieces, slope)


def near_kernel(
    where, normed, first_grad, last_grad, near, beside, up_near, up_beside, slope, far_hidden,
    activated, first_back, last_back, own_part, part1, part2, part3, sums, near_out, beside_out,
    grads, down, up, slopes, far, acts, rows_held, flipped, hidden, product, own_held, held, sems,
):
    step = pl.program_id(0)
    steps = 2
    levels, rows, block = near_out.shape
    tokens = first_grad.shape[0]
    pairs = [(first_grad, grads.at[pl.ds(0, tokens)]), (last_grad, grads.at[pl.ds(tokens, tokens)])]
    pairs += by_rows(where[0], near, beside, down)
    first_copies = loads(sems, 0, pairs)
    count = len(first_copies)
    columns = [pl.ds(k * block, block) for k in range(steps)]
    mine = pl.ds(0, 2 * tokens)
    pairs = [(slope.at[mine, k], slopes.at[:, k]) for k in columns]
    slope_copies = loads(sems, count, pairs)
    far_copies = loads(sems, count + 2, [(far_hidden.at[:, k], far.at[:, k]) for k in columns])
    rest = [(normed, rows_held), (activated, acts)]
    rest = loads(sems, count + 4, rest + by_rows(where[0], up_near, up_beside, up))
    count += 4 + len(rest)
    out_pairs = [(held.at[0], first_back), (held.at[1], last_back), (own_held, own_part)]
    out_pairs += [(held.at[2 + i], part) for i, part in enumerate((part1, part2, part3))]
    saves = loads(sems, count, out_pairs)

    @pl.when(step == 0)
    def _():
        start(first_copies)
        start(slope_copies[:1])
        start(rest[:1])
        start(far_copies[:1])
        start(slope_copies[1:])
        start(far_copies[1:])
        start(rest[2:])
        start(rest[1:2])
        wait(first_copies)

    for k in range(steps):

        @pl.when(step == k)
        def _(k=k):
            slope_copies[k].wait()

    @pl.when(step < steps)
    def _():
        place = pl.ds(pl.multiple_of(step * block, block), block)
        parts = []
        for i in range(2):
            here = slice(i * tokens, (i + 1) * tokens)
            d_act = dot(grads[here, :], down[place, :], NT)
            low = (d_act * slopes[here, place].astype(F32)).astype(BF)
            hidden[here, place] = low
            parts.append(low)

        @pl.when(step == 0)
        def _():
            rest[0].wait()
            for i in range(4):
                here = slice(i * tokens, (i + 1) * tokens)
                flipped[:, here] = rows_held[here, :].T
            far_copies[0].wait()

        @pl.when(step == 1)
        def _():
            far_copies[1].wait()

        parts.append(far[:, place])
        every = jnp.concatenate(parts, axis=0)
        sums[0] = jnp.sum(every.astype(F32), axis=0, keepdims=True)
        product[...] = dot(flipped[...], every, NN).astype(BF)
        for far_x, out in enumerate((near_out, beside_out)):
            for z in range(levels):
                first = (z * 2 + (where[0] ^ far_x)) * rows
                out[z] = product[pl.ds(pl.multiple_of(first, rows), rows), :]

    @pl.when(step == steps)
    def _():
        wait(rest[2:])
        for i in range(2):
            here = slice(i * tokens, (i + 1) * tokens)
            held[i] = dot(hidden[here, :], up[...], NT).astype(BF)
            saves[i].start()
        rest[1].wait()

    @pl.when(step == steps + 1)
    def _():
        own_held[...] = dot(acts[:tokens, :], down[...], NN).astype(BF)
        saves[2].start()
        held[2] = dot(acts[tokens : 2 * tokens, :], down[...], NN).astype(BF)
        saves[3].start()

    @pl.when(step == steps + 2)
    def _():
        for i in (1, 2):
            here = slice((1 + i) * tokens, (2 + i) * tokens)
            held[2 + i] = dot(acts[here, :], down[...], NN).astype(BF)
            saves[3 + i].start()
        wait(saves)


def feed_down_near(where, normed, grads, pieces, up_pieces, slope, far_hidden, activated):
    tokens, width = grads[0].shape
    levels, share, _ = pieces[0].shape
    hidden = slope.shape[1]
    steps = 2
    block = hidden // steps
    rows = width // (2 * levels)
    at = lambda t: jnp.minimum(t, steps - 1)
    out = pl.BlockSpec((levels, rows, block), lambda t, w: (0, 0, at(t)))
    return pl.pallas_call(
        near_kernel,
        grid_spec=pltpu.PrefetchScalarGridSpec(
            num_scalar_prefetch=1,
            grid=(steps + 3,),
            in_specs=[ANYWHERE] * 10,
            out_specs=[ANYWHERE] * 6
            + [pl.BlockSpec((1, 1, block), lambda t, w: (at(t), 0, 0)), out, out],
            scratch_shapes=[
                pltpu.VMEM((2 * tokens, width), BF),
                pltpu.VMEM((hidden, width), BF),
                pltpu.VMEM((width, hidden), BF),
                pltpu.VMEM((2 * tokens, hidden), BF),
                pltpu.VMEM((2 * tokens, hidden), BF),
                pltpu.VMEM((4 * tokens, hidden), BF),
                pltpu.VMEM((4 * tokens, width), BF),
                pltpu.VMEM((width, 4 * tokens), BF),
                pltpu.VMEM((2 * tokens, hidden), BF),
                pltpu.VMEM((width, block), BF),
                pltpu.VMEM((tokens, width), BF),
                pltpu.VMEM((5, tokens, width), BF),
                pltpu.SemaphoreType.DMA((2 + 4 * levels + 4 + 2 + 6,)),
            ],
        ),
        out_shape=[jax.ShapeDtypeStruct((tokens, width), BF)] * 2
        + [jax.ShapeDtypeStruct((tokens, width), kind) for kind in (BF, BF, BF, BF)]
        + [jax.ShapeDtypeStruct((steps, 1, block), F32)]
        + [jax.ShapeDtypeStruct((levels, rows, hidden), BF)] * 2,
        compiler_params=params(),
        cost_estimate=cost(12),
        name="feed_down_near",
    )(where, normed, *grads, *pieces, *up_pieces, slope, far_hidden, activated)


def norm_back_kernel(
    where, own, arrived, far, resid, grad, gain, weights, d_resid, d_low, *rest
):
    outs, sums = rest[:-1], rest[-1]
    d_normed = own[...].astype(F32) + arrived[...].astype(F32) + far[...].astype(F32)
    unit, inverse = normalise(resid[...])
    wide = grad[...].astype(F32)
    out = wide + norm_back(unit, inverse, d_normed * gain[...])
    low = out.astype(BF)
    d_resid[...] = out
    d_low[...] = low
    parts = [d_normed * unit, d_normed, low.astype(F32), wide]
    parts = [jnp.sum(p, axis=0, keepdims=True) for p in parts]
    parts = jnp.concatenate(parts + [jnp.zeros_like(parts[0])] * 4, axis=0)

    @pl.when(pl.program_id(0) == 0)
    def _():
        sums[...] = parts

    @pl.when(pl.program_id(0) > 0)
    def _():
        sums[...] += parts

    d_attended = dot(low, weights[...], NT).astype(BF)
    for m, out in enumerate(outs):
        for h in range(out.shape[0]):
            lanes = out.shape[2]
            first = (m * out.shape[0] + h) * lanes
            out[h] = d_attended[:, first : first + lanes]


def second_norm_back(where, own, arrived, far, resid, grad, gain, weights, seq, groups):
    rows, width = resid.shape
    step = rows // 2
    lanes = width // (seq * groups)
    line = pl.BlockSpec((step, width), lambda i, w: (i, 0))
    return pl.pallas_call(
        norm_back_kernel,
        grid_spec=pltpu.PrefetchScalarGridSpec(
            num_scalar_prefetch=1,
            grid=(rows // step,),
            in_specs=[line] * 5 + [whole((1, width)), whole((width, width))],
            out_specs=[line, line]
            + [pl.BlockSpec((groups, step, lanes), lambda i, w: (0, i, 0))] * seq
            + [whole((8, width))],
        ),
        out_shape=[
            jax.ShapeDtypeStruct((rows, width), F32),
            jax.ShapeDtypeStruct((rows, width), BF),
        ]
        + [jax.ShapeDtypeStruct((groups, rows, lanes), BF)] * seq
        + [jax.ShapeDtypeStruct((8, width), F32)],
        compiler_params=params(),
        cost_estimate=cost(8),
        name="second_norm_back",
    )(where, own, arrived, far, resid, grad, gain, weights)


def out_grad_kernel(where, attended, grad, near, beside, product):
    product[...] = dot(attended[...], grad[...], TN).astype(BF)
    levels, _, _, lanes = near.shape[1:]
    rows = near.shape[3] * lanes // product.shape[1]
    for m in range(4):
        out = (near, beside)[m % 2]
        for far_x in range(2):
            for z in range(levels):
                first = out_row(z, where[0] ^ far_x, where, 4 * rows) + (where[3] ^ m) * rows
                here = pl.ds(pl.multiple_of(first, rows), rows)
                for k in range(product.shape[1] // lanes):
                    out[m // 2, z, far_x, k * rows : (k + 1) * rows, :] = product[
                        here, k * lanes : (k + 1) * lanes
                    ]


def out_grad(where, attended, grad, levels, lanes):
    width = grad.shape[1]
    shape = (2, levels, 2, width // (8 * levels) * (width // lanes), lanes)
    return pl.pallas_call(
        out_grad_kernel,
        grid_spec=pltpu.PrefetchScalarGridSpec(
            num_scalar_prefetch=1,
            grid=(1,),
            in_specs=[whole(attended.shape), whole(grad.shape)],
            out_specs=[whole(shape)] * 2,
            scratch_shapes=[pltpu.VMEM((width, width), BF)],
        ),
        out_shape=[jax.ShapeDtypeStruct(shape, BF)] * 2,
        compiler_params=params(),
        cost_estimate=cost(4),
        name="out_grad",
    )(where, attended, grad)


def heads_back_kernel(
    head_size, blocks, last, where, *refs
):
    pieces, refs = refs[:blocks], refs[blocks:]
    (query, keys, values, tops, inverses, table, *refs) = refs
    spots, (first_rows, last_rows, *rest) = refs[:blocks], refs[blocks:]
    *rest, rows_held, sems = rest
    if last:
        *rest, unit_held = rest
        near0, near1, beside0, beside1, earlier, first_unit, last_unit, *rest = rest
        norm_sums2, up_line, tops_row, earlier_sum, *rest = rest
        sent_back, sent_beside, near_grad, beside_grad, *rest = rest
        weights, joined, vectors, norm_sums, bias_sum, total, d_keys, d_values, grads = rest
    else:
        sent_back, near_grad, bias_sum, *rest = rest
        total, d_keys, d_values, grads = rest
    levels, rows = near_grad.shape[0], near_grad.shape[-1]
    length, lanes = query.shape[1:]
    three = 3 * lanes
    tokens = length // blocks
    clip = pl.program_id(0)

    half = length // 2
    pairs = []
    for i, part in enumerate((first_rows, last_rows)):
        pairs.append((part.at[clip], rows_held.at[pl.ds(i * half, half)]))
    if last:
        for i, part in enumerate((first_unit, last_unit)):
            pairs.append((part.at[clip], unit_held.at[pl.ds(i * half, half)]))
        pairs.append((earlier.at[clip], joined.at[:, pl.ds(0, three)]))
    copies = [pltpu.make_async_copy(a, b, sems.at[i]) for i, (a, b) in enumerate(pairs)]
    for one in copies:
        one.start()
    weight_copies = []
    if last:
        for z in range(levels):
            for far_x, parts in enumerate(((near0, near1), (beside0, beside1))):
                first = (z * 2 + (where[0] ^ far_x)) * rows
                here = pl.ds(pl.multiple_of(first, rows), rows)
                for h, part in enumerate(parts):
                    weight_copies.append(
                        pltpu.make_async_copy(
                            part.at[z, :, pl.ds(0, three)],
                            weights.at[here, pl.ds(h * three, three)],
                            sems.at[len(pairs) + len(weight_copies)],
                        )
                    )

        @pl.when(clip == 0)
        def _():
            for one in weight_copies:
                one.start()

    for b in range(blocks):
        grads[b * tokens : (b + 1) * tokens, :] = pieces[b][0]
    spots = spots_of(clip, pl.num_programs(0), spots, tokens)
    cosine, sine = rotary_of(spots, table)
    scale = jnp.asarray(head_size**-0.5, BF)
    chunk = length // 2
    parts = []
    for i in range(2):
        here = pl.ds(i * chunk, chunk)
        query_rows, grad_rows = query[0, here, :], grads[here, :]
        query_total = None
        for h in range(lanes // head_size):
            own_keys = keep_head(keys[0], h, head_size) * scale
            own_values = keep_head(values[0], h, head_size)
            scores = dot(own_keys, query_rows, NT)
            probs = jnp.exp(scores - tops[0, h : h + 1, here]) * inverses[0, h : h + 1, here]
            d_probs = dot(own_values, grad_rows, NT)
            delta = jnp.sum(probs * d_probs, axis=0, keepdims=True)
            d_scores = (probs * (d_probs - delta)).astype(BF)
            value_part = dot(probs.astype(BF), keep_head(grad_rows, h, head_size), NN)
            key_part = dot(d_scores, keep_head(query_rows, h, head_size) * scale, NN)
            query_part = dot(d_scores, own_keys, TN)
            if h == 0 and i == 0:
                d_values[...] = value_part
                d_keys[...] = key_part
            else:
                d_values[...] += value_part
                d_keys[...] += key_part
            query_total = query_part if query_total is None else query_total + query_part
        parts.append(query_total)
    d_query = jnp.concatenate(parts, axis=0)

    def back(part):
        return (part * cosine - swap_halves(part, head_size) * sine).astype(BF)

    d_mixed = jnp.concatenate(
        [back(d_query), back(d_keys[...]), d_values[...].astype(BF)], axis=1
    )
    sums = jnp.sum(d_mixed.astype(F32), axis=0, keepdims=True)
    for one in copies:
        one.wait()
    part = dot(d_mixed, rows_held[...], TN)

    @pl.when(clip == 0)
    def _():
        bias_sum[...] = sums
        total[...] = part

    @pl.when(clip > 0)
    def _():
        bias_sum[...] += sums
        total[...] += part

    def put_grads(bit, out):
        for z in range(levels):
            first = (z * 2 + (where[0] ^ bit)) * rows
            out[z, :three, :] = total[:, pl.ds(pl.multiple_of(first, rows), rows)].astype(BF)

    if not last:
        sent_back[0] = d_mixed

        @pl.when(clip == pl.num_programs(0) - 1)
        def _():
            put_grads(0, near_grad.at[:, 0])
            put_grads(1, near_grad.at[:, 1])

        return
    joined[:, three:] = d_mixed

    @pl.when(clip == 0)
    def _():
        for one in weight_copies:
            one.wait()

    both = 0.0
    for i in range(2):
        d_normed = dot(joined[i * half : (i + 1) * half, :], weights[...], NT)
        two = [
            jnp.sum(
                d_normed * unit_held[i * half : (i + 1) * half, :].astype(F32), axis=0, keepdims=True
            ),
            jnp.sum(d_normed, axis=0, keepdims=True),
        ]
        both = both + jnp.concatenate(two + [jnp.zeros_like(two[0])] * 6, axis=0)
        low = d_normed.astype(BF)
        for b in range(blocks // 2):
            out = (sent_back, sent_beside)[b % 2]
            out[i * (blocks // 4) + b // 2, 0] = low[b * tokens : (b + 1) * tokens]

    @pl.when(clip == 0)
    def _():
        norm_sums[...] = both

    @pl.when(clip > 0)
    def _():
        norm_sums[...] += both

    @pl.when(clip == pl.num_programs(0) - 1)
    def _():
        vectors[...] = jnp.zeros_like(vectors)
        for f in range(2 * levels):
            here = slice(f * rows, (f + 1) * rows)
            for row, (source, at) in enumerate(
                ((norm_sums, 0), (norm_sums2, 0), (norm_sums, 1), (norm_sums2, 1),
                 (norm_sums2, 2), (norm_sums2, 3))
            ):
                vectors[f, row : row + 1, :] = source[at : at + 1, here]
            vectors[f, pl.ds(9 + where[1], 1), :] = up_line[:, f * rows : (f + 1) * rows]
            vectors[f, VECTOR_ROWS - 1 : VECTOR_ROWS, :] = tops_row[...]
        for h, source in enumerate((earlier_sum, bias_sum)):
            for part in range(3):
                place = (part * blocks + where[1]) * 2 + h
                at = 6 + lax.rem(place, 3)
                vectors[place // 3, pl.ds(at, 1), :] = source[:, part * lanes : (part + 1) * lanes]
        put_grads(0, near_grad)
        put_grads(1, beside_grad)
        for z in range(levels):
            for bit, out in ((0, near_grad), (1, beside_grad)):
                out[z, three:, :] = vectors[z * 2 + (where[0] ^ bit)].astype(BF)


def heads_back(
    where, group, grads_in, saved, table, x_blocks, normed, levels, blocks, head_size,
    weights=(), earlier=None, unit=None, vectors=(),
):
    clips, half, width = normed[0].shape
    length, lanes = 2 * half, grads_in[0].shape[2]
    three, rows = 3 * lanes, width // (2 * levels)
    last = earlier is not None
    clip = lambda *rest: pl.BlockSpec((1,) + rest, lambda i, w: (i,) + (0,) * len(rest))
    by_block = lambda m, n: pl.BlockSpec(
        (m, 1, length // blocks, n), lambda i, w: (0, i, 0, 0)
    )
    stats = clip(lanes // head_size, length)
    query, keys, values, tops, inverses = saved
    grads = [(levels, three + VECTOR_ROWS + 2, rows)] * 2 if last else [(levels, 2, three, rows)]
    outs = [jax.ShapeDtypeStruct(shape, BF) for shape in grads]
    out_specs = [whole(shape) for shape in grads]
    piece = pl.BlockSpec((1, length // blocks, lanes), lambda i, w: (group, i, 0))
    anywhere = pl.BlockSpec(memory_space=pl.ANY)
    in_specs = [piece] * blocks + [clip(length, lanes)] * 3 + [stats] * 2
    in_specs += [whole(table.shape)] + [spot_block(x) for x in x_blocks]
    in_specs += [anywhere] * 2
    scratch = [
        pltpu.VMEM((three, width), F32),
        pltpu.VMEM((length, lanes), F32),
        pltpu.VMEM((length, lanes), F32),
        pltpu.VMEM((length, lanes), BF),
    ]
    if last:
        outs = [jax.ShapeDtypeStruct((blocks // 2, clips, length // blocks, width), BF)] * 2 + outs
        out_specs = [by_block(blocks // 2, width)] * 2 + out_specs
        in_specs += [anywhere] * (len(weights) + 3)
        in_specs += [whole(v.shape) for v in vectors]
        scratch = [
            pltpu.VMEM((width, 2 * three), BF),
            pltpu.VMEM((length, 2 * three), BF),
            pltpu.VMEM((2 * levels, VECTOR_ROWS + 2, lanes), F32),
            pltpu.VMEM((8, width), F32),
            pltpu.VMEM((1, three), F32),
        ] + scratch
        scratch += [pltpu.VMEM((length, width), BF)]
    else:
        outs = [jax.ShapeDtypeStruct((clips, length, three), BF)] + outs
        outs += [jax.ShapeDtypeStruct((1, three), F32)]
        out_specs = [clip(length, three)] + out_specs + [whole((1, three))]
    scratch += [pltpu.VMEM((length, width), BF), pltpu.SemaphoreType.DMA((5 + 4 * levels,))]
    return pl.pallas_call(
        functools.partial(heads_back_kernel, head_size, blocks, last),
        grid_spec=pltpu.PrefetchScalarGridSpec(
            num_scalar_prefetch=1,
            grid=(clips,),
            in_specs=in_specs,
            out_specs=out_specs,
            scratch_shapes=scratch,
        ),
        out_shape=outs,
        compiler_params=params(),
        cost_estimate=cost(22),
        name="heads_back",
    )(
        where, *grads_in, query, keys, values, tops, inverses, table, *x_blocks, *normed,
        *weights, *([earlier, *unit, *vectors] if last else []),
    )


def finish_out_kernel(resid, near, beside, far, bias, out):
    total = resid[...] + near[...].astype(F32) + beside[...].astype(F32) + far[...].astype(F32) + bias[...]
    out[...] = total.astype(BF)


def finish_out(resid, near, beside, far, bias):
    rows, width = resid.shape
    step = rows // 4
    line = pl.BlockSpec((step, width), lambda i: (i, 0))
    return pl.pallas_call(
        finish_out_kernel,
        grid=(rows // step,),
        in_specs=[line] * 4 + [whole((1, width))],
        out_specs=line,
        out_shape=jax.ShapeDtypeStruct((rows, width), BF),
        compiler_params=params(),
        cost_estimate=cost(4),
        name="finish_out",
    )(resid, near, beside, far, bias)


def first_norm_back_kernel(own, beside, far, x, d_resid, gain, out):
    d_normed = own[0, 0].astype(F32) + beside[0, 0].astype(F32) + far[...].astype(F32)
    unit, inverse = normalise(x[...].astype(F32))
    out[...] = d_resid[...] + norm_back(unit, inverse, d_normed * gain[...])


def first_norm_back(own, beside, far, x, d_resid, gain):
    rows, width = x.shape
    _, clips, tokens, _ = own.shape
    line = pl.BlockSpec((tokens, width), lambda i: (i, 0))
    first = pl.BlockSpec((1, 1, tokens, width), lambda i: (0, i, 0, 0))
    return pl.pallas_call(
        first_norm_back_kernel,
        grid=(clips,),
        in_specs=[first, first, line, line, line] + [whole((1, width))],
        out_specs=line,
        out_shape=jax.ShapeDtypeStruct((rows, width), F32),
        compiler_params=params(),
        cost_estimate=cost(4),
        name="first_norm_back",
    )(own, beside, far, x, d_resid, gain)


def pack_kernel(three, first, last, up, out, out_grads):
    lanes = first.shape[2]
    seq, rows = out.shape[0], up.shape[0] // out.shape[0]
    for h, part in enumerate((first, last)):
        total = part[0].astype(F32)
        for z in range(1, part.shape[0]):
            total = total + part[z].astype(F32)
        if h == 0:
            for k in range(out_grads.shape[1] // lanes):
                block = total[three + k * rows : three + (k + 1) * rows]
                out_grads[:, k * lanes : (k + 1) * lanes] = block
        turned = total[:three].T.astype(BF)
        for t in range(seq):
            out[t, :rows, h * three : (h + 1) * three] = turned[t * rows : (t + 1) * rows]
    for t in range(seq):
        out[t, rows:, :lanes] = total[three:].astype(BF)
        out[t, :rows, 2 * three :] = up[t * rows : (t + 1) * rows]


def pack(first, last, up, seq, three):
    extra, rows = last.shape[1] - three, up.shape[0] // seq
    shape = (seq, rows + extra, 2 * three + up.shape[1])
    width = (first.shape[1] - three) * first.shape[2] // rows
    return pl.pallas_call(
        functools.partial(pack_kernel, three),
        out_shape=[jax.ShapeDtypeStruct(shape, BF), jax.ShapeDtypeStruct((rows, width), F32)],
        compiler_params=params(),
        cost_estimate=cost(4),
        name="pack",
    )(first, last, up)


def unpack_kernel(
    rows, count, where, packed, weights, bias, threshold, qkv, up, gains, shifts, biases, qkv_line,
    up_line, maxima, clipped, clipped_bias
):
    seq, lanes = packed.shape[0], maxima.shape[1]
    width = qkv.shape[1] // 3
    group = width // seq
    own_heads = HEADS // seq
    sums = None
    column = lax.broadcasted_iota(jnp.int32, (1, width), 1) // (width // HEADS)
    lane = lax.broadcasted_iota(jnp.int32, (1, lanes), 1)
    limit = threshold[...]
    best = jnp.full((1, lanes), -jnp.inf, F32)
    scales = jnp.ones((1, width), F32)
    for t in range(seq):
        for h in range(group // lanes):
            for part in range(3):
                at = (h * 3 + part) * lanes
                to = part * width + t * group + h * lanes
                qkv[:, to : to + lanes] = packed[t, :rows, at : at + lanes].astype(F32)
        for k in range(up.shape[1] // (seq * lanes)):
            at = (3 * group // lanes + k) * lanes
            to = (k * seq + t) * lanes
            up[:, to : to + lanes] = packed[t, :rows, at : at + lanes].astype(F32)
        extra = packed[t, rows:, :lanes].astype(F32)
        sums = extra if sums is None else sums + extra
        tops = extra[VECTOR_ROWS - 1 : VECTOR_ROWS]
        tops = tops + pltpu.roll(tops, lanes - own_heads, 1) + pltpu.roll(tops, lanes - 2 * own_heads, 1)
        for h in range(own_heads):
            here = (lane % (3 * own_heads) == h) & (lane < count * 3 * own_heads)
            top = jnp.max(jnp.where(here, tops, -jnp.inf), axis=1, keepdims=True)
            head = t * own_heads + h
            best = jnp.where(lane == head, top, best)
            gamma = jnp.sqrt(limit / jnp.maximum(top, limit))
            scales = jnp.where(column == head, gamma, scales)
    lines = pltpu.roll(sums[:8], lanes - where[3] * rows, 1)
    for i, out in enumerate((gains, shifts, biases)):
        out[...] = lines[2 * i : 2 * i + 2, :rows]
    line = jnp.concatenate([sums[i : i + 1] for i in (6, 7, 8)], axis=1)
    line = pltpu.roll(jnp.broadcast_to(line, (8, 3 * lanes)), 3 * lanes - where[3] * 3 * rows, 1)
    qkv_line[...] = line[:1, : 3 * rows]
    line = sums[9:10]
    for t in range(1, seq):
        line = jnp.where(where[3] == t, sums[9 + t : 10 + t], line)
    up_line[...] = line
    maxima[...] = best
    for part in range(2):
        here = slice(part * width, (part + 1) * width)
        clipped[:, here] = weights[:, here].astype(F32) * scales
        clipped_bias[:, here] = bias[:, here] * scales


def unpack(where, packed, weights, bias, threshold, rows, count, hidden, lanes):
    width = weights.shape[1] // 3
    two = (weights.shape[0], 2 * width)
    shapes = [
        (rows, 3 * width), (rows, hidden), (2, rows), (2, rows), (2, rows), (1, 3 * rows), (1, lanes),
        (1, lanes), two, (1, 2 * width),
    ]
    return pl.pallas_call(
        functools.partial(unpack_kernel, rows, count),
        grid_spec=pltpu.PrefetchScalarGridSpec(
            num_scalar_prefetch=1,
            grid=(1,),
            in_specs=[whole(packed.shape), whole(two), whole(bias.shape), whole(threshold.shape)],
            out_specs=[whole(shape) for shape in shapes],
        ),
        out_shape=[jax.ShapeDtypeStruct(shape, F32) for shape in shapes],
        compiler_params=params(),
        cost_estimate=cost(4),
        name="unpack",
    )(where, packed, weights, bias, threshold)


VECTOR_ROWS = 14


def square_device(
    block_input,
    out_cotangent,
    positions,
    w_qkv,
    w_out,
    w_up,
    w_down,
    norm_gains,
    norm_shifts,
    qkv_bias,
    proj_bias,
    up_bias,
    clip_threshold,
):
    clips, tokens, width = block_input.shape
    fsdp, seq = axis_size(FSDP), axis_size(SEQ)
    levels, outer = fsdp // 2, seq // 2
    head_size = width // HEADS
    group = width // seq
    lanes = 128
    groups = group // lanes
    hidden = up_bias.shape[0]
    share = hidden // (fsdp * seq)
    length = tokens * seq
    rows = width // fsdp
    levels_index = lax.axis_index("z")
    x, y, c = lax.axis_index("x"), lax.axis_index("y"), lax.axis_index("core")
    s = y * 2 + c
    heads_where = jnp.stack([x, s]).astype(jnp.int32)
    where = jnp.stack([x, y, c, s]).astype(jnp.int32)
    x_own = block_input.reshape(clips * tokens, width)
    g_own = out_cotangent.reshape(clips * tokens, width)

    def copies(piece):
        return jnp.broadcast_to(piece[None], (levels,) + piece.shape)

    def over_z(piece):
        return lax.all_to_all(piece, "z", 0, 0, tiled=True)

    spots = positions.astype(BF).reshape(-1)
    spots = jnp.pad(spots, (0, 8 * width - spots.shape[0])).reshape(8, width)
    near0, near1, x_ext = prepare(where, w_qkv, w_out, x_own, spots, levels, lanes)
    x_beside = flip_one(x_ext, "y")
    near0 = over_z(near0)
    x_core = flip_one(x_ext, "core")

    near1 = lax.all_gather(near1, "z", axis=0)
    up = own_columns(where, w_up, fsdp, share)
    down = lax.dynamic_slice_in_dim(w_down, s * share, share, 0)

    halves = [first_norm(x_ext, x_core, norm_gains[:1], norm_shifts[:1], clips)]
    beside0 = flip_one(near0, "x")
    bias = up_bias.reshape(levels, 2, seq, share)
    bias = lax.dynamic_index_in_dim(bias, s, 2, keepdims=False).reshape(levels, 1, 2 * share)
    x_far = flip_one(after(x_beside, near0, halves[0][0], up, bias), "core")
    up = lax.all_gather(after(up, x_beside), "z", axis=0)
    down = lax.all_gather(after(down, x_beside), "z", axis=0)
    halves.append(first_norm(x_beside, x_far, norm_gains[:1], norm_shifts[:1], clips))
    normed1, unit1 = zip(*halves, strict=True)
    x_blocks = (x_ext, x_core, x_beside, x_far)
    table = jnp.asarray(rotary_parts(head_size, lanes))
    near1 = after(near1, normed1[1])
    beside1 = flip_one(near1[..., : 3 * lanes], "x")

    own_bias = lax.dynamic_index_in_dim(
        qkv_bias.reshape(3, seq, groups, lanes), s, 1, keepdims=False
    )

    def forward(h, near, beside, *extra):
        return heads_forward(
            heads_where, normed1, near, beside, own_bias[:, h].reshape(1, -1),
            table, x_blocks, seq, head_size, *extra,
        )

    *saved0, out0, tops0, inverses0, own_out = forward(0, near0, beside0, near1)
    saved0 += [tops0, inverses0]
    out0 = after(out0, beside1)
    out0_beside = flip_one(out0, "y")
    out0_core = flip_one(out0, "core")
    own_out = (own_out, flip_one(own_out, "x"))

    *saved1, out1, tops1, inverses1 = forward(1, near1, beside1)
    saved1 += [tops1, inverses1]
    out1 = after(out1, out0_beside, out0_core, own_out[1])
    up = (up, flip_one(after(up, tops1), "x"))
    out1_beside = flip_one(out1, "y")
    out1_core = flip_one(out1, "core")
    out0_far = flip_one(after(out0_beside, tops1), "core")
    other_out = [flip_one(after(part, tops1), "core") for part in own_out]
    out1_far = flip_one(out1_beside, "core")
    g_beside = flip_one(after(g_own, out1_beside), "y")
    g_core = flip_one(after(g_own, out1_beside), "core")
    pieces0 = (out0, out0_core, out0_beside, out0_far)
    pieces1 = (out1, out1_core, out1_beside, out1_far)
    shift_bias = after(proj_bias[:1], down)
    down = (down, flip_one(after(down, out1_beside), "x"))
    tops_own = jnp.concatenate([jnp.max(t, axis=(0, 2)) for t in (tops0, tops1)])

    resid1, attended_own, normed2, full_out = project(
        where, (pieces0, pieces1), x_blocks, own_out, other_out,
        shift_bias, norm_gains[1:], norm_shifts[1:],
    )

    g_far = flip_one(after(g_beside, normed2), "core")
    grads = (g_own, g_core, g_beside, g_far)
    activated, slope, down_near, down_beside = feed_up(where, normed2, grads, up, bias)
    down_beside = flip_one(down_beside, "x")
    far_back, far_other, far_hidden = feed_down_far(
        where, grads[2:], down, up, slope
    )
    far_back = add_low(far_back, flip_one(far_other, "core"))
    far_hidden = after(far_hidden, far_back)
    far_back = flip_one(far_back, "y")
    (own_back, other_back, part_near, part_beside, far_near, far_beside,
     up_sums, up_near, up_beside) = feed_down_near(
        where, normed2, grads[:2], down, up, slope, far_hidden, activated
    )
    up_beside = flip_one(up_beside, "x")
    part_beside = flip_one(part_beside, "core")
    far_beside = flip_one(far_beside, "core")
    down_sum = add_low(down_near, after(down_beside, up_sums))
    other_back = flip_one(after(other_back, far_back, down_sum), "core")
    d_resid1, d_resid1_low, *rest = second_norm_back(
        where, own_back, after(other_back, part_near), far_back, resid1, g_own,
        norm_gains[1:], full_out, seq, groups,
    )
    d_attended, sums2 = rest[:-1], rest[-1]
    d_heads = [d_attended[0]] + [flip(d_attended[m], SEQ, m) for m in range(1, seq)]
    grad_down = lax.psum_scatter(down_sum, "z", scatter_dimension=0, tiled=True)
    grad_down = grad_down.reshape(share, width).astype(F32)
    up_sum = add_low(up_near, after(up_beside, d_resid1_low))
    out_near, out_beside = out_grad(where, attended_own, d_resid1_low, levels, lanes)
    part_far = add_low(far_near, far_beside)
    out_beside = flip_one(after(out_beside, part_far, *d_heads[1:]), "core")

    tops_row, rest = [], tops_own
    for _ in range(3):
        tops_row.append(lax.reduce_precision(rest, 8, 7))
        rest = rest - tops_row[-1]
    tops_row = lax.dynamic_update_slice_in_dim(
        jnp.zeros((lanes,), F32), jnp.concatenate(tops_row), (levels_index * 2 + x) * 12, 0
    )[None]

    out_sum = add_low(out_near, out_beside)
    d_heads = after_all(d_heads, down_sum, up_sum, out_sum)
    up_sum = lax.psum_scatter(after(up_sum, d_heads[2]), "z", scatter_dimension=0, tiled=True)
    up_sum = up_sum.reshape(rows, fsdp * share)
    mixed0, qkv_sum0, bias_sum0 = heads_back(
        heads_where, 0, d_heads, saved0, table, x_blocks, normed1, levels, seq, head_size
    )
    out_far = flip_one(out_sum[1], "y")
    part_far = flip_one(after(part_far, out_far), "y")
    out_sum = add_low(out_sum[0], after(out_far, bias_sum0))
    qkv_sum0 = jnp.concatenate([qkv_sum0, out_sum], axis=2)
    qkv_sum0 = lax.psum_scatter(qkv_sum0, "z", scatter_dimension=0, tiled=True)[0]
    last, last_beside, near_grad1, beside_grad1 = heads_back(
        heads_where, 1, after_all(d_heads, grad_down), saved1, table, x_blocks, normed1,
        levels, seq, head_size, (near0, near1, beside0, beside1), mixed0, unit1,
        (sums2, up_sums.reshape(1, -1), tops_row, bias_sum0),
    )
    last_beside = flip_one(after(last_beside, qkv_sum0, up_sum, part_far), "core")
    beside_grad1 = flip_one(after(beside_grad1, qkv_sum0, up_sum), "x")
    far_block = add_low(last[1], last_beside[1])
    beside_sum0 = flip_one(qkv_sum0[1], "x")
    sent_block = after(far_block, beside_grad1).reshape(x_own.shape)
    far_block = flip_one(sent_block, "y")
    block_out = finish_out(
        after(resid1, sent_block), part_near, part_beside, part_far, proj_bias[1:]
    )
    qkv_sum1 = over_z(add_low(near_grad1, beside_grad1))
    grad_input = first_norm_back(
        last, last_beside, far_block, x_own, d_resid1, norm_gains[:1],
    ).reshape(block_input.shape)

    one = rows // seq
    first = jnp.stack([after(qkv_sum0[0], block_out), beside_sum0])
    packed, grad_out = pack(first, qkv_sum1, up_sum, seq, 3 * lanes)
    packed = lax.all_to_all(after(packed, far_block, block_out), SEQ, 0, 0, tiled=True)
    (grad_qkv, grad_up, grad_gains, grad_shifts, grad_proj_bias, grad_qkv_bias, grad_up_bias,
     maxima, clipped, clipped_bias) = unpack(
        where, packed, w_qkv, qkv_bias[None], clip_threshold[None], one, fsdp, hidden, lanes
    )
    grad_qkv_bias, grad_up_bias = grad_qkv_bias[0], grad_up_bias[0]
    maxima, clipped_bias = maxima[0, :HEADS], clipped_bias[0]
    return (
        block_out.reshape(block_input.shape),
        grad_input,
        grad_qkv,
        grad_out,
        grad_up,
        grad_down,
        grad_gains,
        grad_shifts,
        grad_qkv_bias,
        grad_proj_bias,
        grad_up_bias,
        maxima,
        clipped,
        clipped_bias,
    )


def on_device(block_input, *rest):
    fsdp, seq = axis_size(FSDP), axis_size(SEQ)
    width, hidden = block_input.shape[2], rest[-2].shape[0]
    square = seq == 4 and fsdp % 4 == 0 and fsdp == 8 and width == 256 * seq and hidden % (128 * fsdp * seq) == 0
    square = square and width % (128 * fsdp) == 0
    return (square_device if square else general_device)(block_input, *rest)


def solution(mesh):
    fsdp, seq = mesh.shape["fsdp"], mesh.shape["seq"]
    fine = Mesh(mesh.devices.reshape(fsdp // 2, 2, seq // 2, 2), FSDP + SEQ)
    in_specs = (
        P(FSDP, SEQ, None),
        P(FSDP, SEQ, None),
        P(None, FSDP, SEQ),
        P(FSDP, None),
        P(FSDP, None),
        P(FSDP, None),
        P(FSDP, None),
        P(),
        P(),
        P(),
        P(),
        P(),
        P(),
    )
    out_specs = (
        P(FSDP, SEQ, None),
        P(FSDP, SEQ, None),
        P(FSDP + SEQ, None),
        P(FSDP + SEQ, None),
        P(FSDP + SEQ, None),
        P(FSDP + SEQ, None),
        P(None, FSDP + SEQ),
        P(None, FSDP + SEQ),
        P(FSDP + SEQ),
        P(None, FSDP + SEQ),
        P(FSDP + SEQ),
        P(),
        P(FSDP, None),
        P(),
    )
    return jax.shard_map(
        on_device, mesh=fine, in_specs=in_specs, out_specs=out_specs, check_vma=False
    )
```
